32 devices in a mesh: row: 2 (over y), col: 16 (over z, x, core).
Axes of the slice: x: 2, y: 2, z: 4, core: 2. Of those that a mesh axis runs over, the one named last changes fastest.
Arguments:
- grad_output: bfloat16 [256, 8192], P('col', 'row'), may hold values from -6 to 6
- inputs: bfloat16 [256, 28672], P('row', 'col'), may hold values from -0.375 to 0.375
- weight: bfloat16 [28672, 8192], P('col', 'row'), may hold values from -0.125 to 0.125
- block_mask: int32 [224, 64], P('col'), may hold values from 0 to 1, as said below
Outputs:
- grad_input: bfloat16 [256, 28672], P('row', 'col')
- grad_weight: bfloat16 [28672, 8192], P('col', 'row')
The draws below stay inside these ranges and needn't reach their ends.
Inputs may be any that keep to these rules, and one draw needn't show every extreme that they name: `block_mask`: 1 where the 128 x 128 block of weight is kept, 0 where it is zero; the share of kept blocks differs widely from block row to block row.
All inputs are finite; a program needn't handle non-finite values.
Results may differ from the reference program's by a relative error of at most 0.001.
Values may be sent and summed in bfloat16 or wider, within the bound.
No kernel may reach another device: no remote copies, remote signals or barrier semaphores. Data moves between devices by JAX's collectives and lax.ppermute only.
A program may use at most 128 MiB of HBM per device.

```python
import jax
import jax.numpy as jnp
from jax import lax

D = 8192
H = 28672
BLOCK = 128
TOKENS = 256
HB = 224
DB = 64


def draw_block_mask(key, part):
    level_key, cell_key = jax.random.split(jax.random.fold_in(key, 7))
    levels = jax.random.randint(level_key, (HB, 1), 0, 4)
    percent = jnp.array([8, 18, 36, 58], jnp.int32)[levels]
    rolls = jax.random.randint(cell_key, (HB, DB), 0, 100)
    return (rolls < percent).astype(jnp.int32)


def block_levels(rng, shape, shards, smallest, top_value):
    def one(dim, shards_of):
        draws = jax.random.uniform(jax.random.fold_in(jax.random.fold_in(rng, 6), dim), (shards_of,), jnp.float32, smallest / len(shards), top_value / len(shards))
        return jnp.repeat(jnp.exp(draws), shape[dim] // shards_of).reshape((-1,) + (1,) * (len(shape) - dim - 1))

    factor_of = one(*shards[0])
    for cut in shards[1:]:
        factor_of = factor_of * one(*cut)
    return factor_of


def centred(key, dims, width, limit, pieces=(), kind=jnp.bfloat16):
    values = width * jax.random.normal(key, dims, jnp.float32)
    if pieces:
        values = values * block_levels(key, dims, pieces, -0.22, 0.18)
    return jnp.clip(values, -limit, limit).astype(kind)


def setup_inputs(seed: int = 0) -> dict:
    splits = jax.random.split(jax.random.key(seed), 5)
    return {
        "grad_output": centred(splits[0], (TOKENS, D), 1.0, 6.0, ((0, 16), (1, 2))),
        "inputs": centred(splits[1], (TOKENS, H), (TOKENS ** -0.5), 0.375, ((0, 2), (1, 16))),
        "weight": centred(splits[2], (H, D), (D * 3 // 10) ** -0.5, 0.125, ((0, 16), (1, 2))),
        "block_mask": draw_block_mask(jax.random.fold_in(splits[4], 71), 0),
    }


def reference(grad_output, inputs, weight, block_mask):
    mask_values = block_mask.astype(jnp.bfloat16)
    kept = (weight.reshape(HB, BLOCK, DB, BLOCK) * mask_values[:, None, :, None]).reshape(H, D)
    grad_input = jnp.dot(grad_output, kept.T, preferred_element_type=jnp.float32).astype(jnp.bfloat16)

    def one_row(row_index):
        columns = lax.dynamic_slice_in_dim(inputs, row_index * BLOCK, BLOCK, 1)
        product = lax.dot_general(columns, grad_output, (((0,), (0,)), ((), ())), preferred_element_type=jnp.float32)
        mask_row = lax.dynamic_index_in_dim(block_mask, row_index, 0, keepdims=False).astype(jnp.float32)
        masked = product.reshape(BLOCK, DB, BLOCK) * mask_row[None, :, None]
        return masked.reshape(BLOCK, D).astype(jnp.bfloat16)

    grad_weight = lax.map(one_row, jnp.arange(HB, dtype=jnp.int32)).reshape(H, D)
    return grad_input, grad_weight
```

```python
import functools

import jax
import jax.numpy as jnp
from jax import lax
from jax.experimental import pallas as pl
from jax.experimental.pallas import tpu as pltpu
from jax.sharding import PartitionSpec as P

BLOCK = 128
CODE = 32700.0
STEPS = 64.0
VMEM_LIMIT = 56 * 1024 * 1024


def pair_of(blocks):
    return 2 if blocks % 2 == 0 else 1


def grid_of(cols):
    half, fast = cols // 2, 1
    while half % (fast * 2) == 0 and fast * 2 * fast * 2 <= half:
        fast *= 2
    return half // fast, fast


def encode(part):
    top = jnp.max(jnp.abs(part), axis=0, keepdims=True)
    code = jnp.ceil(STEPS * jnp.log2(jnp.maximum(top, 1e-30)))
    scaled = part * (jnp.exp2(code * (-1.0 / STEPS)) * CODE)
    whole = jnp.clip(jnp.round(scaled), -32767.0, 32767.0)
    return whole.astype(jnp.int32), code.astype(jnp.int32)


def fill_tokens(src_cols, shards, full):
    rows = shards[0].shape[0]
    for n, shard in enumerate(shards):
        at = pl.multiple_of(src_cols[n] * rows, rows)
        full[pl.ds(at, rows), :] = shard[...]


def remote_kernel(n_shards, n_parts, blocks, pair, idx, *refs):
    shards = refs[:n_shards]
    weight, mask = refs[n_shards : n_shards + 2]
    full = refs[n_shards + 2]
    outs = refs[n_shards + 3 : n_shards + 3 + n_parts]
    codes = refs[n_shards + 3 + n_parts]
    step = pl.program_id(0)
    tokens = full.shape[0] // (n_parts + 1)

    @pl.when(step == 0)
    def _():
        fill_tokens(idx, shards, full)
        codes[...] = jnp.zeros_like(codes)

    kept = []
    for b in range(pair):
        factor = mask[pl.ds(step * pair + b, 1), :].astype(jnp.bfloat16)
        kept.append(weight[b * BLOCK : (b + 1) * BLOCK, :] * factor)
    kept = kept[0] if pair == 1 else jnp.concatenate(kept, axis=0)
    row_of_code = lax.broadcasted_iota(jnp.int32, codes.shape[1:], 0)
    for k in range(n_parts):
        at = pl.multiple_of(idx[n_shards + 1 + k] * tokens, tokens)
        part = lax.dot_general(
            full[pl.ds(at, tokens), :],
            kept,
            (((1,), (1,)), ((), ())),
            preferred_element_type=jnp.float32,
        )
        for b in range(pair):
            block = step * pair + b
            whole, code = encode(part[:, b * BLOCK : (b + 1) * BLOCK])
            rows = pl.ds(pl.multiple_of(block * tokens, tokens), tokens)
            outs[k][rows, :] = whole.astype(jnp.int16)
            codes[k] = jnp.where(row_of_code == block, code, codes[k])

    @pl.when(step == blocks // pair - 1)
    def _():
        for k in range(n_parts):
            outs[k][blocks * tokens :, :] = codes[k].astype(jnp.int16)


def own_kernel(pair, idx, full, weight, mask, out):
    step = pl.program_id(0)
    tokens = out.shape[0]
    kept = []
    for b in range(pair):
        factor = mask[pl.ds(step * pair + b, 1), :].astype(jnp.bfloat16)
        kept.append(weight[b * BLOCK : (b + 1) * BLOCK, :] * factor)
    kept = kept[0] if pair == 1 else jnp.concatenate(kept, axis=0)
    at = pl.multiple_of(idx[0] * tokens, tokens)
    out[...] = lax.dot_general(
        full[pl.ds(at, tokens), :],
        kept,
        (((1,), (1,)), ((), ())),
        preferred_element_type=jnp.float32,
    )


def weight_grad_kernel(n_parts, pair, chunk, idx, *refs):
    acts = refs[:n_parts]
    full, mask, out = refs[n_parts : n_parts + 3]
    held = refs[n_parts + 3]
    step = pl.program_id(0)
    tokens = acts[0].shape[0]
    for k in range(n_parts):
        held[pl.ds(pl.multiple_of(idx[k] * tokens, tokens), tokens), :] = acts[k][...]

    def columns(c, _):
        at = pl.ds(pl.multiple_of(c * chunk, chunk), chunk)
        product = lax.dot_general(
            held[...],
            full[:, at],
            (((0,), (0,)), ((), ())),
            preferred_element_type=jnp.float32,
        )
        for b in range(pair):
            factor = mask[pl.ds(step * pair + b, 1), at]
            rows = slice(b * BLOCK, (b + 1) * BLOCK)
            out[rows, at] = (product[rows, :] * factor).astype(out.dtype)
        return 0

    lax.fori_loop(0, out.shape[1] // chunk, columns, 0, unroll=True)


def finish_kernel(n_parts, blocks, own, *refs):
    parts = refs[:n_parts]
    out = refs[n_parts]
    tokens = own.shape[0]
    scales = []
    for part in parts:
        code = part[blocks * tokens :, :].astype(jnp.int32).astype(jnp.float32)
        scales.append(jnp.exp2(code * (1.0 / STEPS)) * (1.0 / CODE))
    for i in range(blocks):
        cols = slice(i * BLOCK, (i + 1) * BLOCK)
        total = own[:, cols]
        for part, scale in zip(parts, scales, strict=True):
            got = part[i * tokens : (i + 1) * tokens, :].astype(jnp.int32)
            total = total + got.astype(jnp.float32) * scale[i : i + 1, :]
        out[:, cols] = total.astype(out.dtype)


def in_vmem():
    return pl.BlockSpec(memory_space=pltpu.VMEM)


def in_smem():
    return pl.BlockSpec(memory_space=pltpu.SMEM)


def params():
    return pltpu.CompilerParams(vmem_limit_bytes=VMEM_LIMIT)


def per_device(n_rows, n_cols, grad_output, inputs, weight, block_mask):
    slow, fast = grid_of(n_cols)
    row, col = lax.axis_index("row"), lax.axis_index("col")
    my_slow, my_fast, my_core = col // (2 * fast), (col // 2) % fast, col % 2
    hidden, width = weight.shape
    blocks = hidden // BLOCK
    pair = pair_of(blocks)
    n_parts = n_rows - 1
    tokens = inputs.shape[0]

    def col_index(s, f, c):
        return (s * fast + f) * 2 + c

    def send_col(x, by_slow, by_fast, by_core):
        perm = [
            (
                col_index(s, f, c),
                col_index((s + by_slow) % slow, (f + by_fast) % fast, (c + by_core) % 2),
            )
            for s in range(slow)
            for f in range(fast)
            for c in range(2)
        ]
        return lax.ppermute(x, "col", perm)

    def send_row(x, by):
        return lax.ppermute(x, "row", [(r, (r + by) % n_rows) for r in range(n_rows)])

    acts = [inputs] + [send_row(inputs, k) for k in range(1, n_rows)]

    held = {(0, 0): grad_output}
    for s in range(1, slow):
        held[s, 0] = send_col(grad_output, s, 0, 0)
    for f in range(1, fast):
        for s in range(slow):
            held[s, f] = send_col(held[s, 0], 0, f, 0)
    shards, sources = [], []
    for (s, f), shard in held.items():
        for c in range(2):
            shards.append(shard if c == 0 else send_col(shard, 0, 0, 1))
            sources.append(
                col_index(
                    (my_slow + slow - s) % slow,
                    (my_fast + fast - f) % fast,
                    (my_core + c) % 2,
                )
            )

    tile_cols = width // BLOCK
    mask_tile = lax.dynamic_slice_in_dim(block_mask, row * tile_cols, tile_cols, 1)
    wide_mask = jnp.repeat(mask_tile.astype(jnp.float32), BLOCK, axis=1)

    all_tokens = tokens * n_rows
    n_shards = len(shards)
    code_rows = -(-blocks // 16) * 16
    idx = jnp.stack(
        [jnp.asarray(s, jnp.int32) for s in sources]
        + [((row + k) % n_rows).astype(jnp.int32) for k in range(n_rows)]
    )
    sent_shape = jax.ShapeDtypeStruct((blocks * tokens + code_rows, BLOCK), jnp.int16)
    weight_spec = pl.BlockSpec((pair * BLOCK, width), lambda i: (i, 0))
    remote = pl.pallas_call(
        functools.partial(remote_kernel, n_shards, n_parts, blocks, pair),
        grid=(blocks // pair,),
        in_specs=[in_smem()] + [in_vmem()] * n_shards + [weight_spec, in_vmem()],
        out_specs=[in_vmem()] * (n_parts + 1),
        out_shape=[jax.ShapeDtypeStruct((all_tokens, width), jnp.bfloat16)]
        + [sent_shape] * n_parts,
        scratch_shapes=[pltpu.VMEM((n_parts, code_rows, BLOCK), jnp.int32)],
        compiler_params=params(),
        cost_estimate=pl.CostEstimate(
            flops=2 * tokens * n_parts * hidden * width,
            bytes_accessed=2 * hidden * width,
            transcendentals=0,
        ),
        name="remote_terms",
    )(idx, *shards, weight, wide_mask)
    full = remote[0]
    parts = [send_row(remote[k], k) for k in range(1, n_rows)]

    own_idx = row.astype(jnp.int32).reshape(1)
    own = pl.pallas_call(
        functools.partial(own_kernel, pair),
        grid=(blocks // pair,),
        in_specs=[in_smem(), in_vmem(), weight_spec, in_vmem()],
        out_specs=pl.BlockSpec((tokens, pair * BLOCK), lambda i: (0, i)),
        out_shape=jax.ShapeDtypeStruct((tokens, hidden), jnp.float32),
        compiler_params=params(),
        cost_estimate=pl.CostEstimate(
            flops=2 * tokens * hidden * width,
            bytes_accessed=2 * hidden * width,
            transcendentals=0,
        ),
        name="own_terms",
    )(own_idx, full, weight, wide_mask)

    act_idx = jnp.stack([((row + n_rows - k) % n_rows).astype(jnp.int32) for k in range(n_rows)])
    grad_weight = pl.pallas_call(
        functools.partial(weight_grad_kernel, n_rows, pair, min(512, width)),
        grid=(blocks // pair,),
        in_specs=[in_smem()]
        + [pl.BlockSpec((tokens, pair * BLOCK), lambda i: (0, i))] * n_rows
        + [in_vmem(), in_vmem()],
        out_specs=weight_spec,
        out_shape=jax.ShapeDtypeStruct((hidden, width), jnp.bfloat16),
        scratch_shapes=[pltpu.VMEM((all_tokens, pair * BLOCK), jnp.bfloat16)],
        compiler_params=params(),
        cost_estimate=pl.CostEstimate(
            flops=2 * all_tokens * hidden * width,
            bytes_accessed=2 * hidden * width,
            transcendentals=0,
        ),
        name="weight_grad",
    )(act_idx, *acts, full, wide_mask)

    grad_input = pl.pallas_call(
        functools.partial(finish_kernel, n_parts, blocks),
        in_specs=[in_vmem()] * (1 + n_parts),
        out_specs=in_vmem(),
        out_shape=jax.ShapeDtypeStruct((tokens, hidden), jnp.bfloat16),
        compiler_params=params(),
        name="add_terms",
    )(own, *parts)
    return (grad_input, grad_weight)


def solution(mesh):
    return jax.shard_map(
        functools.partial(per_device, mesh.shape["row"], mesh.shape["col"]),
        mesh=mesh,
        in_specs=(P("col", "row"), P("row", "col"), P("col", "row"), P("col", None)),
        out_specs=(P("row", "col"), P("col", "row")),
        check_vma=False,
    )
```

```python
import functools

import jax
import jax.numpy as jnp
from jax import lax
from jax.experimental import pallas as pl
from jax.experimental.pallas import tpu as pltpu
from jax.sharding import PartitionSpec as P

BLOCK = 128
CODE = 32700.0
STEPS = 64.0
VMEM_LIMIT = 32 * 1024 * 1024


def pair_of(blocks):
    return 2 if blocks % 2 == 0 else 1


def chip_ring(cols):
    half, fast = cols // 2, 1
    while half % (fast * 2) == 0 and fast * 2 * fast * 2 <= half:
        fast *= 2
    slow = half // fast
    ring = []
    for s in range(slow):
        along = range(1, fast) if s % 2 == 0 else range(fast - 1, 0, -1)
        ring += [s * fast + f for f in along]
    ring += [s * fast for s in range(slow - 1, -1, -1)]
    return ring


def encode(part):
    top = jnp.max(jnp.abs(part), axis=0, keepdims=True)
    code = jnp.ceil(STEPS * jnp.log2(jnp.maximum(top, 1e-30)))
    scaled = part * (jnp.exp2(code * (-1.0 / STEPS)) * CODE)
    whole = jnp.clip(jnp.round(scaled), -32767.0, 32767.0)
    return whole.astype(jnp.int32), code.astype(jnp.int32)


def wide_mask(mask, first, width):
    cols = mask.shape[1]
    of_column = first + lax.broadcasted_iota(jnp.int32, (cols, width), 1) // BLOCK
    spread = of_column == lax.broadcasted_iota(jnp.int32, (cols, width), 0)
    return jnp.dot(
        mask.astype(jnp.float32).astype(jnp.bfloat16),
        spread.astype(jnp.float32).astype(jnp.bfloat16),
        preferred_element_type=jnp.float32,
    )


def terms_kernel(n_shards, n_parts, pair, chunk, idx, *refs):
    shards = refs[:n_shards]
    weight, mask, full, own = refs[n_shards : n_shards + 4]
    outs = refs[n_shards + 4 : n_shards + 4 + n_parts]
    turned, spread, codes = refs[n_shards + 4 + n_parts :]
    step = pl.program_id(0)
    tokens = own.shape[1]
    hidden = outs[0].shape[0] - codes.shape[1]
    width = full.shape[1]

    @pl.when(step == 0)
    def _():
        rows = shards[0].shape[0]
        for n, shard in enumerate(shards):
            full[pl.ds(pl.multiple_of(idx[n + 1] * rows, rows), rows), :] = shard[...]
        for c in range(0, width, chunk):
            turned[c : c + chunk, :] = full[:, c : c + chunk].T
        spread[...] = wide_mask(mask[...], idx[0] * (width // BLOCK), width)
        codes[...] = jnp.zeros_like(codes)

    kept = []
    for b in range(pair):
        factor = spread[pl.ds(step * pair + b, 1), :].astype(jnp.bfloat16)
        kept.append(weight[b * BLOCK : (b + 1) * BLOCK, :] * factor)
    kept = kept[0] if pair == 1 else jnp.concatenate(kept, axis=0)
    terms = jnp.dot(kept, turned[...], preferred_element_type=jnp.float32)
    own[...] = terms[:, :tokens]
    row_of_code = lax.broadcasted_iota(jnp.int32, codes.shape[1:], 0)
    for k in range(n_parts):
        for b in range(pair):
            block = step * pair + b
            whole, code = encode(
                terms[b * BLOCK : (b + 1) * BLOCK, (k + 1) * tokens : (k + 2) * tokens]
            )
            rows = pl.ds(pl.multiple_of(block * BLOCK, BLOCK), BLOCK)
            outs[k][rows, :] = whole.astype(jnp.int16)
            codes[k] = jnp.where(row_of_code == block, code, codes[k])

    @pl.when(step == pl.num_programs(0) - 1)
    def _():
        for k in range(n_parts):
            outs[k][hidden:, :] = codes[k].astype(jnp.int16)


def weight_grad_kernel(n_parts, idx, *refs):
    acts = refs[:n_parts]
    full, mask, out, turned = refs[n_parts:]
    step = pl.program_id(0)
    tokens, hidden = acts[0].shape
    width = full.shape[1]

    @pl.when(step == 0)
    def _():
        for k in range(n_parts):
            place = (n_parts - k) % n_parts
            for c in range(0, hidden, BLOCK):
                turned[c : c + BLOCK, place * tokens : (place + 1) * tokens] = (
                    acts[k][:, c : c + BLOCK].T
                )

    first = idx[0] * (pl.num_programs(0) * (width // BLOCK)) + step * (width // BLOCK)
    spread = wide_mask(mask[...], first, width)
    product = jnp.dot(turned[...], full[...], preferred_element_type=jnp.float32)
    for b in range(hidden // BLOCK):
        rows = slice(b * BLOCK, (b + 1) * BLOCK)
        out[rows, :] = (product[rows, :] * spread[b : b + 1, :]).astype(out.dtype)


def finish_kernel(n_parts, own, *refs):
    parts = refs[:n_parts]
    out = refs[n_parts]
    hidden = own.shape[0]
    scales = []
    for part in parts:
        code = part[hidden:, :].astype(jnp.int32).astype(jnp.float32)
        scales.append(jnp.exp2(code * (1.0 / STEPS)) * (1.0 / CODE))
    for i in range(hidden // BLOCK):
        rows = slice(i * BLOCK, (i + 1) * BLOCK)
        total = own[rows, :]
        for part, scale in zip(parts, scales, strict=True):
            got = part[rows, :].astype(jnp.int32).astype(jnp.float32)
            total = total + got * scale[i : i + 1, :]
        out[:, rows] = total.T.astype(out.dtype)


def in_vmem():
    return pl.BlockSpec(memory_space=pltpu.VMEM)


def in_smem():
    return pl.BlockSpec(memory_space=pltpu.SMEM)


def params():
    return pltpu.CompilerParams(vmem_limit_bytes=VMEM_LIMIT)


def per_device(n_rows, n_cols, grad_output, inputs, weight, block_mask):
    row, col = lax.axis_index("row"), lax.axis_index("col")
    hidden, width = weight.shape
    blocks = hidden // BLOCK
    pair = pair_of(blocks)
    n_parts = n_rows - 1
    tokens = inputs.shape[0]
    shard_rows = grad_output.shape[0]
    all_tokens = tokens * n_rows

    ring = chip_ring(n_cols)
    n_chips = len(ring)

    def send_ring(x, by):
        perm = []
        for p in range(n_chips):
            for core in range(2):
                q = (p + (by if core == 0 else -by)) % n_chips
                perm.append((ring[p] * 2 + core, ring[q] * 2 + core))
        return lax.ppermute(x, "col", perm)

    def send_core(x):
        return lax.ppermute(x, "col", [(c, c ^ 1) for c in range(n_cols)])

    def send_row(x, by):
        return lax.ppermute(x, "row", [(r, (r + by) % n_rows) for r in range(n_rows)])

    held = {0: grad_output}
    there, back = grad_output, grad_output
    for j in range(1, n_chips // 2 + 1):
        there = send_ring(there, 1)
        held[j] = there
        if 2 * j < n_chips:
            back = send_ring(back, -1)
            held[-j] = back
    acts = [inputs] + [send_row(inputs, k) for k in range(1, n_rows)]
    shards, steps = [], []
    for j, shard in held.items():
        shards += [shard, send_core(shard)]
        steps += [(j, 0), (j, 1)]

    table = []
    for c in range(n_cols):
        p, core = ring.index(c // 2), c % 2
        line = []
        for j, other in steps:
            of_core = core ^ other
            q = (p - j if of_core == 0 else p + j) % n_chips
            line.append(ring[q] * 2 + of_core)
        table.append(line)
    sources = lax.dynamic_index_in_dim(jnp.array(table, jnp.int32), col, 0, keepdims=False)
    places = (sources - row * (tokens // shard_rows)) % n_cols
    idx = jnp.concatenate([row.astype(jnp.int32).reshape(1), places.astype(jnp.int32)])

    n_shards = len(shards)
    code_rows = -(-blocks // 16) * 16
    sent_shape = jax.ShapeDtypeStruct((hidden + code_rows, tokens), jnp.int16)
    full, own, *coded = pl.pallas_call(
        functools.partial(terms_kernel, n_shards, n_parts, pair, min(512, width)),
        grid=(blocks // pair,),
        in_specs=[in_smem()]
        + [in_vmem()] * n_shards
        + [pl.BlockSpec((pair * BLOCK, width), lambda i: (i, 0)), in_vmem()],
        out_specs=[in_vmem(), pl.BlockSpec((pair * BLOCK, tokens), lambda i: (i, 0))]
        + [in_vmem()] * n_parts,
        out_shape=[
            jax.ShapeDtypeStruct((all_tokens, width), jnp.bfloat16),
            jax.ShapeDtypeStruct((hidden, tokens), jnp.float32),
        ]
        + [sent_shape] * n_parts,
        scratch_shapes=[
            pltpu.VMEM((width, all_tokens), jnp.bfloat16),
            pltpu.VMEM((blocks, width), jnp.float32),
            pltpu.VMEM((n_parts, code_rows, tokens), jnp.int32),
        ],
        compiler_params=params(),
        cost_estimate=pl.CostEstimate(
            flops=2 * all_tokens * hidden * width,
            bytes_accessed=2 * hidden * width,
            transcendentals=0,
        ),
        name="terms",
    )(idx, *shards, weight, block_mask)
    parts = [send_row(coded[k], k + 1) for k in range(n_parts)]

    columns = min(512, width)
    grad_weight = pl.pallas_call(
        functools.partial(weight_grad_kernel, n_rows),
        grid=(width // columns,),
        in_specs=[in_smem()]
        + [in_vmem()] * n_rows
        + [pl.BlockSpec((all_tokens, columns), lambda i: (0, i)), in_vmem()],
        out_specs=pl.BlockSpec((hidden, columns), lambda i: (0, i)),
        out_shape=jax.ShapeDtypeStruct((hidden, width), jnp.bfloat16),
        scratch_shapes=[pltpu.VMEM((hidden, all_tokens), jnp.bfloat16)],
        compiler_params=params(),
        cost_estimate=pl.CostEstimate(
            flops=2 * all_tokens * hidden * width,
            bytes_accessed=2 * hidden * width,
            transcendentals=0,
        ),
        name="weight_grad",
    )(idx, *acts, full, block_mask)

    grad_input = pl.pallas_call(
        functools.partial(finish_kernel, n_parts),
        in_specs=[in_vmem()] * (1 + n_parts),
        out_specs=in_vmem(),
        out_shape=jax.ShapeDtypeStruct((tokens, hidden), jnp.bfloat16),
        compiler_params=params(),
        name="add_terms",
    )(own, *parts)
    return (grad_input, grad_weight)


def solution(mesh):
    return jax.shard_map(
        functools.partial(per_device, mesh.shape["row"], mesh.shape["col"]),
        mesh=mesh,
        in_specs=(P("col", "row"), P("row", "col"), P("col", "row"), P("col", None)),
        out_specs=(P("row", "col"), P("col", "row")),
        check_vma=False,
    )
```

```python
import functools

import jax
import jax.numpy as jnp
from jax import lax
from jax.experimental import pallas as pl
from jax.experimental.pallas import tpu as pltpu
from jax.sharding import PartitionSpec as P

BLOCK = 128
CODE = 32700.0
STEPS = 64.0
VMEM_LIMIT = 32 * 1024 * 1024


def chip_ring(cols):
    half, fast = cols // 2, 1
    while half % (fast * 2) == 0 and fast * 2 * fast * 2 <= half:
        fast *= 2
    slow = half // fast
    ring = []
    for s in range(slow):
        along = range(1, fast) if s % 2 == 0 else range(fast - 1, 0, -1)
        ring += [s * fast + f for f in along]
    ring += [s * fast for s in range(slow - 1, -1, -1)]
    return ring


def encode(part):
    top = jnp.max(jnp.abs(part), axis=0, keepdims=True)
    code = jnp.ceil(STEPS * jnp.log2(jnp.maximum(top, 1e-30)))
    scaled = part * (jnp.exp2(code * (-1.0 / STEPS)) * CODE)
    whole = jnp.clip(jnp.round(scaled), -32767.0, 32767.0)
    return whole.astype(jnp.int32), code.astype(jnp.int32)


def wide_mask(mask, first, width):
    cols = mask.shape[1]
    of_column = first + lax.broadcasted_iota(jnp.int32, (cols, width), 1) // BLOCK
    spread = of_column == lax.broadcasted_iota(jnp.int32, (cols, width), 0)
    return jnp.dot(
        mask.astype(jnp.float32).astype(jnp.bfloat16),
        spread.astype(jnp.float32).astype(jnp.bfloat16),
        preferred_element_type=jnp.float32,
    )


def keep_kernel(idx, shard, weight, mask, kept, shard_copy, sems):
    rows, width = kept.shape
    blocks = rows // BLOCK
    copies = []
    for b in range(blocks):
        at = pl.ds(b * BLOCK, BLOCK)
        copies.append(pltpu.make_async_copy(weight.at[at, :], kept.at[at, :], sems.at[b]))
        copies[-1].start()
    shard_copy[...] = shard[...]
    spread = wide_mask(mask[...], idx[0] * (width // BLOCK), width).astype(jnp.bfloat16)
    for b in range(blocks):
        copies[b].wait()
        at = slice(b * BLOCK, (b + 1) * BLOCK)
        kept[at, :] = kept[at, :] * spread[b : b + 1, :]


def turn_kernel(n_rows, *refs):
    acts, out = refs[:n_rows], refs[n_rows]
    tokens, hidden = acts[0].shape
    for k in range(n_rows):
        place = (n_rows - k) % n_rows
        for c in range(0, hidden, BLOCK):
            out[c : c + BLOCK, place * tokens : (place + 1) * tokens] = acts[k][:, c : c + BLOCK].T


def store_terms(total, own, outs):
    rows, tokens = own.shape
    own[...] = total[:, :tokens]
    for k, out in enumerate(outs):
        of_code = lax.broadcasted_iota(jnp.int32, (out.shape[0] - rows, tokens), 0)
        codes = jnp.zeros(of_code.shape, jnp.int32)
        for b in range(rows // BLOCK):
            at = slice(b * BLOCK, (b + 1) * BLOCK)
            whole, code = encode(total[at, (k + 1) * tokens : (k + 2) * tokens])
            out[at, :] = whole.astype(jnp.int16)
            codes = jnp.where(of_code == b, code, codes)
        out[rows:, :] = codes.astype(jnp.int16)


def first_terms_kernel(n_shards, n_parts, chunk, idx, *refs):
    shards = refs[:n_shards]
    kept, _, full, turned, own = refs[n_shards : n_shards + 5]
    outs = refs[n_shards + 5 : n_shards + 5 + n_parts]
    total = refs[n_shards + 5 + n_parts]
    rows = shards[0].shape[0]
    for n, shard in enumerate(shards):
        full[pl.ds(pl.multiple_of(idx[n + 1] * rows, rows), rows), :] = shard[...]
    for c in range(0, full.shape[1], chunk):
        turned[c : c + chunk, :] = full[:, c : c + chunk].T
        terms = jnp.dot(
            kept[:, c : c + chunk], turned[c : c + chunk, :], preferred_element_type=jnp.float32
        )
        total[...] = terms if c == 0 else total[...] + terms
    store_terms(total, own, outs)


def more_terms_kernel(n_parts, first_block, idx, turned, weight, mask, own, *refs):
    outs, total = refs[:n_parts], refs[n_parts]
    step = pl.program_id(0)
    rows, chunk = weight.shape
    per_row = pl.num_programs(0) * (chunk // BLOCK)
    first = idx[0] * per_row + step * (chunk // BLOCK)
    spread = wide_mask(mask[...], first, chunk).astype(jnp.bfloat16)
    kept = []
    for b in range(rows // BLOCK):
        at = first_block + b
        kept.append(weight[b * BLOCK : (b + 1) * BLOCK, :] * spread[at : at + 1, :])
    terms = jnp.dot(
        jnp.concatenate(kept, axis=0), turned[...], preferred_element_type=jnp.float32
    )

    @pl.when(step == 0)
    def _():
        total[...] = terms

    @pl.when(step > 0)
    def _():
        total[...] += terms

    @pl.when(step == pl.num_programs(0) - 1)
    def _():
        store_terms(total, own, outs)


def weight_grad_kernel(idx, acts, full, mask, out):
    hidden, width = out.shape
    step = pl.program_id(0)
    first = idx[0] * (pl.num_programs(0) * (width // BLOCK)) + step * (width // BLOCK)
    spread = wide_mask(mask[...], first, width)
    product = jnp.dot(acts[...], full[...], preferred_element_type=jnp.float32)
    for b in range(hidden // BLOCK):
        rows = slice(b * BLOCK, (b + 1) * BLOCK)
        out[rows, :] = (product[rows, :] * spread[b : b + 1, :]).astype(out.dtype)


def finish_kernel(n_pieces, n_parts, *refs):
    owns, parts, out = refs[:n_pieces], refs[n_pieces:-1], refs[-1]
    rows = owns[0].shape[0]
    for p, own in enumerate(owns):
        mine = parts[p * n_parts : (p + 1) * n_parts]
        scales = []
        for part in mine:
            code = part[rows:, :].astype(jnp.int32).astype(jnp.float32)
            scales.append(jnp.exp2(code * (1.0 / STEPS)) * (1.0 / CODE))
        for b in range(rows // BLOCK):
            at = slice(b * BLOCK, (b + 1) * BLOCK)
            total = own[at, :]
            for part, scale in zip(mine, scales, strict=True):
                got = part[at, :].astype(jnp.int32).astype(jnp.float32)
                total = total + got * scale[b : b + 1, :]
            to = p * rows + b * BLOCK
            out[:, to : to + BLOCK] = total.T.astype(out.dtype)


def in_vmem():
    return pl.BlockSpec(memory_space=pltpu.VMEM)


def in_smem():
    return pl.BlockSpec(memory_space=pltpu.SMEM)


def in_hbm():
    return pl.BlockSpec(memory_space=pl.ANY)


def params():
    return pltpu.CompilerParams(vmem_limit_bytes=VMEM_LIMIT)


def cost(flops, nbytes):
    return pl.CostEstimate(flops=flops, bytes_accessed=nbytes, transcendentals=0)


def per_device(n_rows, n_cols, grad_output, inputs, weight, block_mask):
    row, col = lax.axis_index("row"), lax.axis_index("col")
    hidden, width = weight.shape
    blocks = hidden // BLOCK
    n_pieces = 2 if blocks % 2 == 0 else 1
    piece = hidden // n_pieces
    n_parts = n_rows - 1
    tokens = inputs.shape[0]
    shard_rows = grad_output.shape[0]
    all_tokens = tokens * n_rows
    chunk = min(512, width)
    bf16 = jnp.bfloat16

    ring = chip_ring(n_cols)
    n_chips = len(ring)

    def send_ring(x, by):
        perm = []
        for p in range(n_chips):
            for core in range(2):
                q = (p + (by if core == 0 else -by)) % n_chips
                perm.append((ring[p] * 2 + core, ring[q] * 2 + core))
        return lax.ppermute(x, "col", perm)

    def send_core(x):
        return lax.ppermute(x, "col", [(c, c ^ 1) for c in range(n_cols)])

    def send_row(x, by):
        return lax.ppermute(x, "row", [(r, (r + by) % n_rows) for r in range(n_rows)])

    reach = [0]
    for j in range(1, n_chips // 2 + 1):
        reach += [j] if 2 * j == n_chips else [j, -j]
    steps = [(j, other) for j in reach for other in range(2)]
    table = []
    for c in range(n_cols):
        p, core = ring.index(c // 2), c % 2
        line = []
        for j, other in steps:
            of_core = core ^ other
            q = (p - j if of_core == 0 else p + j) % n_chips
            line.append(ring[q] * 2 + of_core)
        table.append(line)
    sources = lax.dynamic_index_in_dim(jnp.array(table, jnp.int32), col, 0, keepdims=False)
    places = (sources - row * (tokens // shard_rows)) % n_cols
    idx = jnp.concatenate([row.astype(jnp.int32).reshape(1), places.astype(jnp.int32)])

    weight = pltpu.with_memory_space_constraint(weight, pltpu.HBM)
    kept, shard_copy = pl.pallas_call(
        keep_kernel,
        in_specs=[in_smem(), in_vmem(), in_hbm(), in_vmem()],
        out_specs=[in_vmem(), in_vmem()],
        out_shape=[
            pltpu.VMEM((piece, width), bf16),
            jax.ShapeDtypeStruct(grad_output.shape, bf16),
        ],
        scratch_shapes=[pltpu.SemaphoreType.DMA((piece // BLOCK,))],
        compiler_params=params(),
        cost_estimate=cost(piece * width, 2 * piece * width),
        name="keep",
    )(idx, grad_output, weight, block_mask)

    held = {0: grad_output}
    there, back = grad_output, shard_copy
    for j in range(1, n_chips // 2 + 1):
        there = send_ring(there, 1)
        held[j] = there
        if 2 * j < n_chips:
            back = send_ring(back, -1)
            held[-j] = back
    shards = []
    for j in reach:
        shards += [held[j], send_core(held[j])]

    acts = [inputs] + [send_row(inputs, k) for k in range(1, n_rows)]
    acts_turned = pl.pallas_call(
        functools.partial(turn_kernel, n_rows),
        in_specs=[in_vmem()] * n_rows,
        out_specs=in_vmem(),
        out_shape=jax.ShapeDtypeStruct((hidden, all_tokens), bf16),
        compiler_params=params(),
        cost_estimate=cost(all_tokens * hidden, 4 * all_tokens * hidden),
        name="turn",
    )(*acts)

    n_shards = len(shards)
    code_rows = -(-(piece // BLOCK) // 16) * 16
    sent_shape = jax.ShapeDtypeStruct((piece + code_rows, tokens), jnp.int16)
    own_shape = jax.ShapeDtypeStruct((piece, tokens), jnp.float32)
    piece_cost = cost(2 * all_tokens * piece * width, 2 * piece * width)
    full, turned, own, *coded = pl.pallas_call(
        functools.partial(first_terms_kernel, n_shards, n_parts, chunk),
        in_specs=[in_smem()] + [in_vmem()] * n_shards + [in_vmem(), in_hbm()],
        out_specs=[in_vmem()] * (3 + n_parts),
        out_shape=[
            jax.ShapeDtypeStruct((all_tokens, width), bf16),
            jax.ShapeDtypeStruct((width, all_tokens), bf16),
            own_shape,
        ]
        + [sent_shape] * n_parts,
        scratch_shapes=[pltpu.VMEM((piece, all_tokens), jnp.float32)],
        compiler_params=params(),
        cost_estimate=piece_cost,
        name="first_terms",
    )(idx, *shards, kept, acts_turned)
    owns = [own]
    parts = [send_row(coded[k], k + 1) for k in range(n_parts)]

    for p in range(1, n_pieces):
        own, *coded = pl.pallas_call(
            functools.partial(more_terms_kernel, n_parts, p * (piece // BLOCK)),
            grid=(width // chunk,),
            in_specs=[
                in_smem(),
                pl.BlockSpec((chunk, all_tokens), lambda i: (i, 0)),
                pl.BlockSpec((piece, chunk), lambda i, p=p: (p, i)),
                in_vmem(),
            ],
            out_specs=[in_vmem()] * (1 + n_parts),
            out_shape=[own_shape] + [sent_shape] * n_parts,
            scratch_shapes=[pltpu.VMEM((piece, all_tokens), jnp.float32)],
            compiler_params=params(),
            cost_estimate=piece_cost,
            name="more_terms",
        )(idx, turned, weight, block_mask)
        owns.append(own)
        parts += [send_row(coded[k], k + 1) for k in range(n_parts)]

    grad_weight = pl.pallas_call(
        weight_grad_kernel,
        grid=(width // chunk,),
        in_specs=[
            in_smem(),
            in_vmem(),
            pl.BlockSpec((all_tokens, chunk), lambda i: (0, i)),
            in_vmem(),
        ],
        out_specs=pl.BlockSpec((hidden, chunk), lambda i: (0, i)),
        out_shape=jax.ShapeDtypeStruct((hidden, width), bf16),
        compiler_params=params(),
        cost_estimate=cost(2 * all_tokens * hidden * width, 2 * hidden * width),
        name="weight_grad",
    )(idx, acts_turned, full, block_mask)

    grad_input = pl.pallas_call(
        functools.partial(finish_kernel, n_pieces, n_parts),
        in_specs=[in_vmem()] * (n_pieces * (1 + n_parts)),
        out_specs=in_vmem(),
        out_shape=jax.ShapeDtypeStruct((tokens, hidden), bf16),
        compiler_params=params(),
        name="add_terms",
    )(*owns, *parts)
    return (grad_input, grad_weight)


def solution(mesh):
    return jax.shard_map(
        functools.partial(per_device, mesh.shape["row"], mesh.shape["col"]),
        mesh=mesh,
        in_specs=(P("col", "row"), P("row", "col"), P("col", "row"), P("col", None)),
        out_specs=(P("row", "col"), P("col", "row")),
        check_vma=False,
    )
```

```python
import functools

import jax
import jax.numpy as jnp
from jax import lax
from jax.experimental import pallas as pl
from jax.experimental.pallas import tpu as pltpu
from jax.sharding import PartitionSpec as P

BLOCK = 128
CODE = 32700.0
STEPS = 64.0
VMEM_LIMIT = 24 * 1024 * 1024


def chip_ring(cols):
    half, fast = cols // 2, 1
    while half % (fast * 2) == 0 and fast * 2 * fast * 2 <= half:
        fast *= 2
    slow = half // fast
    ring = []
    for s in range(slow):
        along = range(1, fast) if s % 2 == 0 else range(fast - 1, 0, -1)
        ring += [s * fast + f for f in along]
    ring += [s * fast for s in range(slow - 1, -1, -1)]
    return ring


def encode(part):
    top = jnp.max(jnp.abs(part), axis=0, keepdims=True)
    code = jnp.ceil(STEPS * jnp.log2(jnp.maximum(top, 1e-30)))
    scaled = part * (jnp.exp2(code * (-1.0 / STEPS)) * CODE)
    whole = jnp.clip(jnp.round(scaled), -32767.0, 32767.0)
    return whole.astype(jnp.int32), code.astype(jnp.int32)


def wide_mask(mask, first, width):
    cols = mask.shape[1]
    of_column = first + lax.broadcasted_iota(jnp.int32, (cols, width), 1) // BLOCK
    spread = of_column == lax.broadcasted_iota(jnp.int32, (cols, width), 0)
    return jnp.dot(
        mask.astype(jnp.float32).astype(jnp.bfloat16),
        spread.astype(jnp.float32).astype(jnp.bfloat16),
        preferred_element_type=jnp.float32,
    )


def keep_kernel(idx, weight, mask, kept, sems):
    rows, width = kept.shape
    blocks = rows // BLOCK
    copies = []
    for b in range(blocks):
        at = pl.ds(b * BLOCK, BLOCK)
        copies.append(pltpu.make_async_copy(weight.at[at, :], kept.at[at, :], sems.at[b]))
        copies[-1].start()
    spread = wide_mask(mask[...], idx[0] * (width // BLOCK), width).astype(jnp.bfloat16)
    for b in range(blocks):
        copies[b].wait()
        at = slice(b * BLOCK, (b + 1) * BLOCK)
        kept[at, :] = kept[at, :] * spread[b : b + 1, :]


def turn_kernel(n_rows, *refs):
    acts, out = refs[:n_rows], refs[n_rows]
    tokens, hidden = acts[0].shape
    for k in range(n_rows):
        place = (n_rows - k) % n_rows
        for c in range(0, hidden, BLOCK):
            out[c : c + BLOCK, place * tokens : (place + 1) * tokens] = acts[k][:, c : c + BLOCK].T


def store_terms(total, own, outs):
    rows, tokens = own.shape
    own[...] = total[:, :tokens]
    for k, out in enumerate(outs):
        of_code = lax.broadcasted_iota(jnp.int32, (out.shape[0] - rows, tokens), 0)
        codes = jnp.zeros(of_code.shape, jnp.int32)
        for b in range(rows // BLOCK):
            at = slice(b * BLOCK, (b + 1) * BLOCK)
            whole, code = encode(total[at, (k + 1) * tokens : (k + 2) * tokens])
            out[at, :] = whole.astype(jnp.int16)
            codes = jnp.where(of_code == b, code, codes)
        out[rows:, :] = codes.astype(jnp.int16)


def first_terms_kernel(n_shards, n_parts, chunk, idx, *refs):
    shards = refs[:n_shards]
    kept, _, full, turned, own = refs[n_shards : n_shards + 5]
    outs = refs[n_shards + 5 : n_shards + 5 + n_parts]
    total = refs[n_shards + 5 + n_parts]
    rows = shards[0].shape[0]
    for n, shard in enumerate(shards):
        full[pl.ds(pl.multiple_of(idx[n + 1] * rows, rows), rows), :] = shard[...]
    for c in range(0, full.shape[1], chunk):
        turned[c : c + chunk, :] = full[:, c : c + chunk].T
        terms = jnp.dot(
            kept[: own.shape[0], c : c + chunk],
            turned[c : c + chunk, :],
            preferred_element_type=jnp.float32,
        )
        total[...] = terms if c == 0 else total[...] + terms
    store_terms(total, own, outs)


def more_terms_kernel(n_parts, first_row, chunk, turned, kept, own, *refs):
    outs, total = refs[:n_parts], refs[n_parts]
    rows = slice(first_row, first_row + own.shape[0])
    for c in range(0, kept.shape[1], chunk):
        terms = jnp.dot(
            kept[rows, c : c + chunk], turned[c : c + chunk, :], preferred_element_type=jnp.float32
        )
        total[...] = terms if c == 0 else total[...] + terms
    store_terms(total, own, outs)


def weight_grad_kernel(idx, acts, full, mask, out):
    hidden, width = out.shape
    step = pl.program_id(0)
    first = idx[0] * (pl.num_programs(0) * (width // BLOCK)) + step * (width // BLOCK)
    spread = wide_mask(mask[...], first, width)
    height = 2 * BLOCK if hidden % (2 * BLOCK) == 0 else BLOCK
    for r in range(0, hidden, height):
        product = jnp.dot(acts[r : r + height, :], full[...], preferred_element_type=jnp.float32)
        for b in range(0, height, BLOCK):
            factor = spread[(r + b) // BLOCK : (r + b) // BLOCK + 1, :]
            out[r + b : r + b + BLOCK, :] = (product[b : b + BLOCK, :] * factor).astype(out.dtype)


def finish_kernel(n_parts, own, *refs):
    parts, out = refs[:n_parts], refs[-1]
    rows = own.shape[0]
    scales = []
    for part in parts:
        code = part[rows:, :].astype(jnp.int32).astype(jnp.float32)
        scales.append(jnp.exp2(code * (1.0 / STEPS)) * (1.0 / CODE))
    for b in range(rows // BLOCK):
        at = slice(b * BLOCK, (b + 1) * BLOCK)
        total = own[at, :]
        for part, scale in zip(parts, scales, strict=True):
            got = part[at, :].astype(jnp.int32).astype(jnp.float32)
            total = total + got * scale[b : b + 1, :]
        out[:, at] = total.T.astype(out.dtype)


def in_vmem():
    return pl.BlockSpec(memory_space=pltpu.VMEM)


def in_smem():
    return pl.BlockSpec(memory_space=pltpu.SMEM)


def in_hbm():
    return pl.BlockSpec(memory_space=pl.ANY)


def params():
    return pltpu.CompilerParams(vmem_limit_bytes=VMEM_LIMIT)


def cost(flops, nbytes):
    return pl.CostEstimate(flops=flops, bytes_accessed=nbytes, transcendentals=0)


def per_device(n_rows, n_cols, grad_output, inputs, weight, block_mask):
    row, col = lax.axis_index("row"), lax.axis_index("col")
    hidden, width = weight.shape
    blocks = hidden // BLOCK
    n_pieces = 2 if blocks % 2 == 0 else 1
    piece = hidden // n_pieces
    n_parts = n_rows - 1
    tokens = inputs.shape[0]
    shard_rows = grad_output.shape[0]
    all_tokens = tokens * n_rows
    chunk = min(512, width)
    bf16 = jnp.bfloat16

    ring = chip_ring(n_cols)
    n_chips = len(ring)

    def send_ring(x, by):
        perm = []
        for p in range(n_chips):
            for core in range(2):
                q = (p + (by if core == 0 else -by)) % n_chips
                perm.append((ring[p] * 2 + core, ring[q] * 2 + core))
        return lax.ppermute(x, "col", perm)

    def send_core(x):
        return lax.ppermute(x, "col", [(c, c ^ 1) for c in range(n_cols)])

    def send_row(x, by):
        return lax.ppermute(x, "row", [(r, (r + by) % n_rows) for r in range(n_rows)])

    reach = [0]
    for j in range(1, n_chips // 2 + 1):
        reach += [j] if 2 * j == n_chips else [j, -j]
    steps = [(j, other) for j in reach for other in range(2)]
    table = []
    for c in range(n_cols):
        p, core = ring.index(c // 2), c % 2
        line = []
        for j, other in steps:
            of_core = core ^ other
            q = (p - j if of_core == 0 else p + j) % n_chips
            line.append(ring[q] * 2 + of_core)
        table.append(line)
    sources = lax.dynamic_index_in_dim(jnp.array(table, jnp.int32), col, 0, keepdims=False)
    places = (sources - row * (tokens // shard_rows)) % n_cols
    idx = jnp.concatenate([row.astype(jnp.int32).reshape(1), places.astype(jnp.int32)])

    weight = pltpu.with_memory_space_constraint(weight, pltpu.HBM)
    kept = pl.pallas_call(
        keep_kernel,
        in_specs=[in_smem(), in_hbm(), in_vmem()],
        out_specs=in_vmem(),
        out_shape=pltpu.VMEM((hidden, width), bf16),
        scratch_shapes=[pltpu.SemaphoreType.DMA((blocks,))],
        compiler_params=params(),
        cost_estimate=cost(hidden * width, 2 * hidden * width),
        name="keep",
    )(idx, weight, block_mask)

    held = {0: grad_output}
    for j in (1, -1, 2, -2):
        if abs(j) < n_chips // 2 or j == n_chips // 2:
            held[j] = send_ring(grad_output, j)
    waits = [j for j in held if j]
    kept, *ready = lax.optimization_barrier((kept, *(held[j] for j in waits)))
    held.update(zip(waits, ready, strict=True))
    for j in range(3, n_chips // 2 + 1):
        by = 1 if j % 2 else 2
        held[j] = send_ring(held[j - by], by)
        if 2 * j < n_chips:
            held[-j] = send_ring(held[by - j], -by)
    shards = []
    for j in reach:
        shards += [held[j], send_core(held[j])]

    acts = [inputs] + [send_row(inputs, k) for k in range(1, n_rows)]
    acts_turned = pl.pallas_call(
        functools.partial(turn_kernel, n_rows),
        in_specs=[in_vmem()] * n_rows,
        out_specs=in_vmem(),
        out_shape=jax.ShapeDtypeStruct((hidden, all_tokens), bf16),
        compiler_params=params(),
        cost_estimate=cost(all_tokens * hidden, 4 * all_tokens * hidden),
        name="turn",
    )(*acts)

    n_shards = len(shards)
    code_rows = -(-(piece // BLOCK) // 16) * 16
    sent_shape = jax.ShapeDtypeStruct((piece + code_rows, tokens), jnp.int16)
    own_shape = jax.ShapeDtypeStruct((piece, tokens), jnp.float32)
    piece_cost = cost(piece * width, piece * width // 8)
    full, turned, own, *coded = pl.pallas_call(
        functools.partial(first_terms_kernel, n_shards, n_parts, chunk),
        in_specs=[in_smem()] + [in_vmem()] * n_shards + [in_vmem(), in_hbm()],
        out_specs=[in_vmem()] * (3 + n_parts),
        out_shape=[
            jax.ShapeDtypeStruct((all_tokens, width), bf16),
            jax.ShapeDtypeStruct((width, all_tokens), bf16),
            own_shape,
        ]
        + [sent_shape] * n_parts,
        scratch_shapes=[pltpu.VMEM((piece, all_tokens), jnp.float32)],
        compiler_params=params(),
        cost_estimate=piece_cost,
        name="first_terms",
    )(idx, *shards, kept, acts_turned)
    owns = [own]
    parts = [send_row(coded[k], k + 1) for k in range(n_parts)]

    for p in range(1, n_pieces):
        own, *coded = pl.pallas_call(
            functools.partial(more_terms_kernel, n_parts, p * piece, chunk),
            in_specs=[in_vmem()] * 2,
            out_specs=[in_vmem()] * (1 + n_parts),
            out_shape=[own_shape] + [sent_shape] * n_parts,
            scratch_shapes=[pltpu.VMEM((piece, all_tokens), jnp.float32)],
            compiler_params=params(),
            cost_estimate=piece_cost,
            name="more_terms",
        )(turned, kept)
        owns.append(own)
        parts += [send_row(coded[k], k + 1) for k in range(n_parts)]

    grad_weight = pl.pallas_call(
        weight_grad_kernel,
        grid=(width // chunk,),
        in_specs=[
            in_smem(),
            in_vmem(),
            pl.BlockSpec((all_tokens, chunk), lambda i: (0, i)),
            in_vmem(),
        ],
        out_specs=pl.BlockSpec((hidden, chunk), lambda i: (0, i)),
        out_shape=jax.ShapeDtypeStruct((hidden, width), bf16),
        compiler_params=params(),
        cost_estimate=cost(hidden * width, hidden * width // 8),
        name="weight_grad",
    )(idx, acts_turned, full, block_mask)

    grad_input = None
    for p in range(n_pieces):
        operands = [owns[p], *parts[p * n_parts : (p + 1) * n_parts]]
        specs = [in_vmem()] * len(operands)
        if p:
            operands.append(grad_input)
            specs.append(in_hbm())
        grad_input = pl.pallas_call(
            functools.partial(finish_kernel, n_parts),
            grid=(1,),
            in_specs=specs,
            out_specs=pl.BlockSpec((tokens, piece), lambda i, p=p: (0, p)),
            out_shape=jax.ShapeDtypeStruct((tokens, hidden), bf16),
            input_output_aliases={len(operands) - 1: 0} if p else {},
            compiler_params=params(),
            name="add_terms",
        )(*operands)
    return (grad_input, grad_weight)


def solution(mesh):
    return jax.shard_map(
        functools.partial(per_device, mesh.shape["row"], mesh.shape["col"]),
        mesh=mesh,
        in_specs=(P("col", "row"), P("row", "col"), P("col", "row"), P("col", None)),
        out_specs=(P("row", "col"), P("col", "row")),
        check_vma=False,
    )
```

```python
import functools

import jax
import jax.numpy as jnp
from jax import lax
from jax.experimental import pallas as pl
from jax.experimental.pallas import tpu as pltpu
from jax.sharding import PartitionSpec as P

BLOCK = 128
CODE = 32700.0
STEPS = 64.0
VMEM_LIMIT = 24 * 1024 * 1024


def chip_ring(cols):
    half, fast = cols // 2, 1
    while half % (fast * 2) == 0 and fast * 2 * fast * 2 <= half:
        fast *= 2
    slow = half // fast
    ring = []
    for s in range(slow):
        along = range(1, fast) if s % 2 == 0 else range(fast - 1, 0, -1)
        ring += [s * fast + f for f in along]
    ring += [s * fast for s in range(slow - 1, -1, -1)]
    return ring


def encode(part):
    top = jnp.max(jnp.abs(part), axis=0, keepdims=True)
    code = jnp.ceil(STEPS * jnp.log2(jnp.maximum(top, 1e-30)))
    scaled = part * (jnp.exp2(code * (-1.0 / STEPS)) * CODE)
    whole = jnp.clip(jnp.round(scaled), -32767.0, 32767.0)
    return whole.astype(jnp.int32), code.astype(jnp.int32)


def wide_mask(mask, first, width):
    cols = mask.shape[1]
    of_column = first + lax.broadcasted_iota(jnp.int32, (cols, width), 1) // BLOCK
    spread = of_column == lax.broadcasted_iota(jnp.int32, (cols, width), 0)
    return jnp.dot(
        mask.astype(jnp.float32).astype(jnp.bfloat16),
        spread.astype(jnp.float32).astype(jnp.bfloat16),
        preferred_element_type=jnp.float32,
    )


def keep_kernel(place, weight, mask, kept, spread, mask_here, mask_sem, sems):
    rows, width = kept.shape
    mask_copy = pltpu.make_async_copy(mask, mask_here, mask_sem)
    mask_copy.start()
    copies = []
    for b in range(rows // BLOCK):
        at = pl.ds(b * BLOCK, BLOCK)
        copies.append(pltpu.make_async_copy(weight.at[at, :], kept.at[at, :], sems.at[b]))
        copies[-1].start()
    mask_copy.wait()
    spread[...] = wide_mask(mask_here[...], place[0] * (width // BLOCK), width)
    factors = spread[...].astype(jnp.bfloat16)
    for b, copy in enumerate(copies):
        copy.wait()
        at = slice(b * BLOCK, (b + 1) * BLOCK)
        kept[at, :] = kept[at, :] * factors[b : b + 1, :]


def turn_kernel(n_rows, *refs):
    acts, out = refs[:n_rows], refs[n_rows]
    tokens, hidden = acts[0].shape
    for k in range(n_rows):
        place = (n_rows - k) % n_rows
        for c in range(0, hidden, BLOCK):
            out[c : c + BLOCK, place * tokens : (place + 1) * tokens] = acts[k][:, c : c + BLOCK].T


def store_terms(total, own, outs):
    rows, tokens = own.shape
    own[...] = total[:, :tokens]
    for k, out in enumerate(outs):
        of_code = lax.broadcasted_iota(jnp.int32, (out.shape[0] - rows, tokens), 0)
        codes = jnp.zeros(of_code.shape, jnp.int32)
        for b in range(rows // BLOCK):
            at = slice(b * BLOCK, (b + 1) * BLOCK)
            whole, code = encode(total[at, (k + 1) * tokens : (k + 2) * tokens])
            out[at, :] = whole.astype(jnp.int16)
            codes = jnp.where(of_code == b, code, codes)
        out[rows:, :] = codes.astype(jnp.int16)


def first_terms_kernel(n_shards, n_parts, shift, chunk, place, table, *refs):
    shards = refs[:n_shards]
    kept, weight, _, full, turned, own = refs[n_shards : n_shards + 6]
    outs = refs[n_shards + 6 : n_shards + 6 + n_parts]
    *rest, total, sems = refs[n_shards + 6 + n_parts :]
    piece = own.shape[0]
    copies = []
    for p, later in enumerate(rest):
        at = pl.ds((p + 1) * piece, piece)
        copies.append(pltpu.make_async_copy(weight.at[at, :], later, sems.at[p]))
        copies[-1].start()
    rows = shards[0].shape[0]
    n_cols = table.shape[0]
    for n, shard in enumerate(shards):
        to = lax.rem(table[place[1], n] + n_cols - place[0] * shift, n_cols)
        full[pl.ds(pl.multiple_of(to * rows, rows), rows), :] = shard[...]
    for c in range(0, full.shape[1], chunk):
        turned[c : c + chunk, :] = full[:, c : c + chunk].T
        terms = jnp.dot(
            kept[:, c : c + chunk], turned[c : c + chunk, :], preferred_element_type=jnp.float32
        )
        total[...] = terms if c == 0 else total[...] + terms
    store_terms(total, own, outs)
    for copy in copies:
        copy.wait()


def more_terms_kernel(n_parts, first_block, chunk, turned, weight, spread, own, *refs):
    outs, total = refs[:n_parts], refs[n_parts]
    blocks = own.shape[0] // BLOCK
    for c in range(0, weight.shape[1], chunk):
        cols = slice(c, c + chunk)
        factors = spread[first_block : first_block + blocks, cols].astype(jnp.bfloat16)
        kept = jnp.concatenate(
            [weight[b * BLOCK : (b + 1) * BLOCK, cols] * factors[b : b + 1, :] for b in range(blocks)],
            axis=0,
        )
        terms = jnp.dot(kept, turned[cols, :], preferred_element_type=jnp.float32)
        total[...] = terms if c == 0 else total[...] + terms
    store_terms(total, own, outs)


def weight_grad_kernel(chunk, acts, full, spread, out, held, sems):
    hidden, width = out.shape
    blocks = hidden // BLOCK
    pair = 2 if blocks % 2 == 0 else 1

    def leave(block):
        at = pl.ds(pl.multiple_of(block * BLOCK, BLOCK), BLOCK)
        return pltpu.make_async_copy(held.at[at, :], out.at[at, :], sems.at[block])

    def rows(step, _):
        first = step * pair
        left = acts[pl.ds(pl.multiple_of(first * BLOCK, pair * BLOCK), pair * BLOCK), :]
        for c in range(0, width, chunk):
            cols = slice(c, c + chunk)
            product = jnp.dot(left, full[:, cols], preferred_element_type=jnp.float32)
            for b in range(pair):
                at = pl.ds(pl.multiple_of((first + b) * BLOCK, BLOCK), BLOCK)
                part = product[b * BLOCK : (b + 1) * BLOCK, :] * spread[pl.ds(first + b, 1), cols]
                held[at, cols] = part.astype(out.dtype)
        for b in range(pair):
            leave(first + b).start()
        return 0

    lax.fori_loop(0, blocks // pair, rows, 0)
    lax.fori_loop(0, blocks, lambda block, _: (leave(block).wait(), 0)[1], 0)


def finish_kernel(n_parts, own, *refs):
    parts, out = refs[:n_parts], refs[-1]
    rows = own.shape[0]
    scales = []
    for part in parts:
        code = part[rows:, :].astype(jnp.int32).astype(jnp.float32)
        scales.append(jnp.exp2(code * (1.0 / STEPS)) * (1.0 / CODE))
    for b in range(rows // BLOCK):
        at = slice(b * BLOCK, (b + 1) * BLOCK)
        total = own[at, :]
        for part, scale in zip(parts, scales, strict=True):
            got = part[at, :].astype(jnp.int32).astype(jnp.float32)
            total = total + got * scale[b : b + 1, :]
        out[:, at] = total.T.astype(out.dtype)


def in_vmem():
    return pl.BlockSpec(memory_space=pltpu.VMEM)


def in_smem():
    return pl.BlockSpec(memory_space=pltpu.SMEM)


def in_hbm():
    return pl.BlockSpec(memory_space=pl.ANY)


def params():
    return pltpu.CompilerParams(vmem_limit_bytes=VMEM_LIMIT)


def cost(flops, nbytes):
    return pl.CostEstimate(flops=flops, bytes_accessed=nbytes, transcendentals=0)


def per_device(n_rows, n_cols, grad_output, inputs, weight, block_mask):
    row, col = lax.axis_index("row"), lax.axis_index("col")
    hidden, width = weight.shape
    blocks = hidden // BLOCK
    n_pieces = 2 if blocks % 2 == 0 else 1
    piece = hidden // n_pieces
    n_parts = n_rows - 1
    tokens = inputs.shape[0]
    shard_rows = grad_output.shape[0]
    all_tokens = tokens * n_rows
    chunk = min(512, width)
    bf16 = jnp.bfloat16

    ring = chip_ring(n_cols)
    n_chips = len(ring)

    def send_ring(x, by):
        perm = []
        for p in range(n_chips):
            for core in range(2):
                q = (p + (by if core == 0 else -by)) % n_chips
                perm.append((ring[p] * 2 + core, ring[q] * 2 + core))
        return lax.ppermute(x, "col", perm)

    def send_core(x):
        return lax.ppermute(x, "col", [(c, c ^ 1) for c in range(n_cols)])

    def send_row(x, by):
        return lax.ppermute(x, "row", [(r, (r + by) % n_rows) for r in range(n_rows)])

    reach = [0]
    for j in range(1, n_chips // 2 + 1):
        reach += [j] if 2 * j == n_chips else [j, -j]
    steps = [(j, other) for j in reach for other in range(2)]
    table = []
    for c in range(n_cols):
        p, core = ring.index(c // 2), c % 2
        line = []
        for j, other in steps:
            of_core = core ^ other
            q = (p - j if of_core == 0 else p + j) % n_chips
            line.append(ring[q] * 2 + of_core)
        table.append(line)
    place = jnp.stack([row, col]).astype(jnp.int32)

    weight = pltpu.with_memory_space_constraint(weight, pltpu.HBM)
    kept, spread = pl.pallas_call(
        keep_kernel,
        in_specs=[in_smem(), in_hbm(), in_hbm()],
        out_specs=[in_vmem()] * 2,
        out_shape=[
            pltpu.VMEM((piece, width), bf16),
            pltpu.VMEM((blocks, width), jnp.float32),
        ],
        scratch_shapes=[
            pltpu.VMEM(block_mask.shape, jnp.int32),
            pltpu.SemaphoreType.DMA,
            pltpu.SemaphoreType.DMA((piece // BLOCK,)),
        ],
        compiler_params=params(),
        cost_estimate=cost(piece * width, 2 * piece * width),
        name="keep",
    )(place, weight, block_mask)

    held = {0: grad_output}
    for j in (2, -2, 1, -1):
        if abs(j) < n_chips // 2 or j == n_chips // 2:
            held[j] = send_ring(grad_output, j)
    near = [j for j in held if j]
    kept, *ready = lax.optimization_barrier((kept, *(held[j] for j in near)))
    held.update(zip(near, ready, strict=True))
    for j in range(3, n_chips // 2 + 1):
        by = 1 if j % 2 else 2
        held[j] = send_ring(held[j - by], by)
        if 2 * j < n_chips:
            held[-j] = send_ring(held[by - j], -by)
    shards = []
    for j in reach:
        shards += [held[j], send_core(held[j])]

    acts = [inputs] + [send_row(inputs, k) for k in range(1, n_rows)]
    acts_turned = pl.pallas_call(
        functools.partial(turn_kernel, n_rows),
        in_specs=[in_vmem()] * n_rows,
        out_specs=in_vmem(),
        out_shape=jax.ShapeDtypeStruct((hidden, all_tokens), bf16),
        compiler_params=params(),
        cost_estimate=cost(all_tokens * hidden, 4 * all_tokens * hidden),
        name="turn",
    )(*acts)

    n_shards = len(shards)
    code_rows = -(-(piece // BLOCK) // 16) * 16
    sent_shape = jax.ShapeDtypeStruct((piece + code_rows, tokens), jnp.int16)
    own_shape = jax.ShapeDtypeStruct((piece, tokens), jnp.float32)
    small_cost = cost(piece * width, piece * width // 8)
    later = n_pieces - 1
    full, turned, own, *coded = pl.pallas_call(
        functools.partial(first_terms_kernel, n_shards, n_parts, tokens // shard_rows, chunk),
        in_specs=[in_smem()] * 2 + [in_vmem()] * n_shards + [in_vmem(), in_hbm(), in_hbm()],
        out_specs=[in_vmem()] * (3 + n_parts + later),
        out_shape=[
            jax.ShapeDtypeStruct((all_tokens, width), bf16),
            jax.ShapeDtypeStruct((width, all_tokens), bf16),
            own_shape,
        ]
        + [sent_shape] * n_parts
        + [pltpu.VMEM((piece, width), bf16)] * later,
        scratch_shapes=[
            pltpu.VMEM((piece, all_tokens), jnp.float32),
            pltpu.SemaphoreType.DMA((max(later, 1),)),
        ],
        compiler_params=params(),
        cost_estimate=small_cost,
        name="first_terms",
    )(place, jnp.array(table, jnp.int32), *shards, kept, weight, acts_turned)
    owns = [own]
    coded, rest = coded[:n_parts], coded[n_parts:]
    parts = [send_row(coded[k], k + 1) for k in range(n_parts)]

    for p in range(1, n_pieces):
        own, *coded = pl.pallas_call(
            functools.partial(more_terms_kernel, n_parts, p * (piece // BLOCK), chunk),
            in_specs=[in_vmem()] * 3,
            out_specs=[in_vmem()] * (1 + n_parts),
            out_shape=[own_shape] + [sent_shape] * n_parts,
            scratch_shapes=[pltpu.VMEM((piece, all_tokens), jnp.float32)],
            compiler_params=params(),
            cost_estimate=small_cost,
            name="more_terms",
        )(turned, rest[p - 1], spread)
        owns.append(own)
        parts += [send_row(coded[k], k + 1) for k in range(n_parts)]

    grad_weight = pl.pallas_call(
        functools.partial(weight_grad_kernel, chunk),
        in_specs=[in_vmem()] * 3,
        out_specs=in_hbm(),
        out_shape=jax.ShapeDtypeStruct((hidden, width), bf16),
        scratch_shapes=[
            pltpu.VMEM((hidden, width), bf16),
            pltpu.SemaphoreType.DMA((blocks,)),
        ],
        compiler_params=params(),
        cost_estimate=small_cost,
        name="weight_grad",
    )(acts_turned, full, spread)

    grad_input = None
    for p in range(n_pieces):
        operands = [owns[p], *parts[p * n_parts : (p + 1) * n_parts]]
        specs = [in_vmem()] * len(operands)
        if p:
            operands.append(grad_input)
            specs.append(in_hbm())
        grad_input = pl.pallas_call(
            functools.partial(finish_kernel, n_parts),
            grid=(1,),
            in_specs=specs,
            out_specs=pl.BlockSpec((tokens, piece), lambda i, p=p: (0, p)),
            out_shape=jax.ShapeDtypeStruct((tokens, hidden), bf16),
            input_output_aliases={len(operands) - 1: 0} if p else {},
            compiler_params=params(),
            name="add_terms",
        )(*operands)
    return (grad_input, grad_weight)


def solution(mesh):
    return jax.shard_map(
        functools.partial(per_device, mesh.shape["row"], mesh.shape["col"]),
        mesh=mesh,
        in_specs=(P("col", "row"), P("row", "col"), P("col", "row"), P("col", None)),
        out_specs=(P("row", "col"), P("col", "row")),
        check_vma=False,
    )
```

```python
import functools

import jax
import jax.numpy as jnp
from jax import lax
from jax.experimental import pallas as pl
from jax.experimental.pallas import tpu as pltpu
from jax.sharding import PartitionSpec as P

BLOCK = 128
CODE = 32700.0
STEPS = 64.0
VMEM_LIMIT = 24 * 1024 * 1024


def chip_ring(cols):
    half, fast = cols // 2, 1
    while half % (fast * 2) == 0 and fast * 2 * fast * 2 <= half:
        fast *= 2
    slow = half // fast
    ring = []
    for s in range(slow):
        along = range(1, fast) if s % 2 == 0 else range(fast - 1, 0, -1)
        ring += [s * fast + f for f in along]
    ring += [s * fast for s in range(slow - 1, -1, -1)]
    return ring


def encode(part):
    top = jnp.max(jnp.abs(part), axis=0, keepdims=True)
    code = jnp.ceil(STEPS * jnp.log2(jnp.maximum(top, 1e-30)))
    scaled = part * (jnp.exp2(code * (-1.0 / STEPS)) * CODE)
    whole = jnp.clip(jnp.round(scaled), -32767.0, 32767.0)
    return whole.astype(jnp.int32), code.astype(jnp.int32)


def wide_mask(mask, first, width):
    cols = mask.shape[1]
    of_column = first + lax.broadcasted_iota(jnp.int32, (cols, width), 1) // BLOCK
    spread = of_column == lax.broadcasted_iota(jnp.int32, (cols, width), 0)
    return jnp.dot(
        mask.astype(jnp.float32).astype(jnp.bfloat16),
        spread.astype(jnp.float32).astype(jnp.bfloat16),
        preferred_element_type=jnp.float32,
    )


def spread_and_keep_kernel(place, weight, mask, kept, spread, mask_here, mask_sem, sems):
    rows, width = kept.shape
    mask_copy = pltpu.make_async_copy(mask, mask_here, mask_sem)
    mask_copy.start()
    copies = fetch(weight, 0, kept, sems)
    mask_copy.wait()
    spread[...] = wide_mask(mask_here[...], place[0] * (width // BLOCK), width)
    drop_blocks(copies, kept, spread[: rows // BLOCK, :])


def keep_kernel(first, spread, weight, kept, sems):
    copies = fetch(weight, first, kept, sems)
    drop_blocks(copies, kept, spread[first : first + kept.shape[0] // BLOCK, :])


def fetch(weight, first, kept, sems):
    copies = []
    for b in range(kept.shape[0] // BLOCK):
        copies.append(
            pltpu.make_async_copy(
                weight.at[pl.ds((first + b) * BLOCK, BLOCK), :],
                kept.at[pl.ds(b * BLOCK, BLOCK), :],
                sems.at[b],
            )
        )
        copies[-1].start()
    return copies


def drop_blocks(copies, kept, spread):
    factors = spread.astype(jnp.bfloat16)
    for b, copy in enumerate(copies):
        copy.wait()
        at = slice(b * BLOCK, (b + 1) * BLOCK)
        kept[at, :] = kept[at, :] * factors[b : b + 1, :]


def turn_kernel(n_rows, *refs):
    acts, out = refs[:n_rows], refs[n_rows]
    tokens, hidden = acts[0].shape
    for k in range(n_rows):
        place = (n_rows - k) % n_rows
        for c in range(0, hidden, BLOCK):
            out[c : c + BLOCK, place * tokens : (place + 1) * tokens] = acts[k][:, c : c + BLOCK].T


def store_terms(total, own, outs):
    rows, tokens = own.shape
    own[...] = total[:, :tokens]
    for k, out in enumerate(outs):
        of_code = lax.broadcasted_iota(jnp.int32, (out.shape[0] - rows, tokens), 0)
        codes = jnp.zeros(of_code.shape, jnp.int32)
        for b in range(rows // BLOCK):
            at = slice(b * BLOCK, (b + 1) * BLOCK)
            whole, code = encode(total[at, (k + 1) * tokens : (k + 2) * tokens])
            out[at, :] = whole.astype(jnp.int16)
            codes = jnp.where(of_code == b, code, codes)
        out[rows:, :] = codes.astype(jnp.int16)


def first_terms_kernel(n_shards, n_kept, n_parts, shift, chunk, place, table, *refs):
    shards, kepts = refs[:n_shards], refs[n_shards : n_shards + n_kept]
    _, full, turned, own, *outs, total = refs[n_shards + n_kept :]
    rows = shards[0].shape[0]
    n_cols = table.shape[0]
    for n, shard in enumerate(shards):
        to = lax.rem(table[place[1], n] + n_cols - place[0] * shift, n_cols)
        full[pl.ds(pl.multiple_of(to * rows, rows), rows), :] = shard[...]
    for c in range(0, full.shape[1], chunk):
        cols = slice(c, c + chunk)
        turned[cols, :] = full[:, cols].T
        at = 0
        for kept in kepts:
            to = slice(at, at + kept.shape[0])
            terms = jnp.dot(kept[:, cols], turned[cols, :], preferred_element_type=jnp.float32)
            total[to, :] = terms if c == 0 else total[to, :] + terms
            at += kept.shape[0]
    store_terms(total, own, outs)


def more_terms_kernel(n_parts, first, chunk, turned, weight, spread, own, *refs):
    outs, (here, total, sems) = refs[:n_parts], refs[n_parts:]
    rows = own.shape[0]
    blocks = rows // BLOCK
    copies = []
    for c in range(0, weight.shape[1], chunk):
        cols = pl.ds(c, chunk)
        copies.append(
            pltpu.make_async_copy(
                weight.at[pl.ds(first * BLOCK, rows), cols], here.at[:, cols], sems.at[c // chunk]
            )
        )
        copies[-1].start()
    for c, copy in zip(range(0, weight.shape[1], chunk), copies, strict=True):
        cols = slice(c, c + chunk)
        factors = spread[first : first + blocks, cols].astype(jnp.bfloat16)
        copy.wait()
        kept = jnp.concatenate(
            [here[b * BLOCK : (b + 1) * BLOCK, cols] * factors[b : b + 1, :] for b in range(blocks)],
            axis=0,
        )
        terms = jnp.dot(kept, turned[cols, :], preferred_element_type=jnp.float32)
        total[...] = terms if c == 0 else total[...] + terms
    store_terms(total, own, outs)


def weight_grad_kernel(chunk, acts, full, spread, out, held, sems):
    hidden, width = out.shape
    blocks = hidden // BLOCK
    pair = 2 if blocks % 2 == 0 else 1

    def leave(block):
        at = pl.ds(pl.multiple_of(block * BLOCK, BLOCK), BLOCK)
        return pltpu.make_async_copy(held.at[at, :], out.at[at, :], sems.at[block])

    def rows(step, _):
        first = step * pair
        left = acts[pl.ds(pl.multiple_of(first * BLOCK, pair * BLOCK), pair * BLOCK), :]
        for c in range(0, width, chunk):
            cols = slice(c, c + chunk)
            product = jnp.dot(left, full[:, cols], preferred_element_type=jnp.float32)
            for b in range(pair):
                at = pl.ds(pl.multiple_of((first + b) * BLOCK, BLOCK), BLOCK)
                part = product[b * BLOCK : (b + 1) * BLOCK, :] * spread[pl.ds(first + b, 1), cols]
                held[at, cols] = part.astype(out.dtype)
        for b in range(pair):
            leave(first + b).start()
        return 0

    lax.fori_loop(0, blocks // pair, rows, 0)
    lax.fori_loop(0, blocks, lambda block, _: (leave(block).wait(), 0)[1], 0)


def finish_kernel(n_parts, own, *refs):
    parts, out = refs[:n_parts], refs[-1]
    rows = own.shape[0]
    scales = []
    for part in parts:
        code = part[rows:, :].astype(jnp.int32).astype(jnp.float32)
        scales.append(jnp.exp2(code * (1.0 / STEPS)) * (1.0 / CODE))
    for b in range(rows // BLOCK):
        at = slice(b * BLOCK, (b + 1) * BLOCK)
        total = own[at, :]
        for part, scale in zip(parts, scales, strict=True):
            got = part[at, :].astype(jnp.int32).astype(jnp.float32)
            total = total + got * scale[b : b + 1, :]
        out[:, at] = total.T.astype(out.dtype)


def in_vmem():
    return pl.BlockSpec(memory_space=pltpu.VMEM)


def in_smem():
    return pl.BlockSpec(memory_space=pltpu.SMEM)


def in_hbm():
    return pl.BlockSpec(memory_space=pl.ANY)


def params():
    return pltpu.CompilerParams(vmem_limit_bytes=VMEM_LIMIT)


def cost(flops, nbytes):
    return pl.CostEstimate(flops=flops, bytes_accessed=nbytes, transcendentals=0)


def per_device(n_rows, n_cols, grad_output, inputs, weight, block_mask):
    row, col = lax.axis_index("row"), lax.axis_index("col")
    hidden, width = weight.shape
    blocks = hidden // BLOCK
    n_pieces = 2 if blocks % 2 == 0 else 1
    piece = hidden // n_pieces
    n_parts = n_rows - 1
    tokens = inputs.shape[0]
    shard_rows = grad_output.shape[0]
    all_tokens = tokens * n_rows
    chunk = min(512, width)
    bf16 = jnp.bfloat16

    ring = chip_ring(n_cols)
    n_chips = len(ring)

    def send_ring(x, by):
        perm = []
        for p in range(n_chips):
            for core in range(2):
                q = (p + (by if core == 0 else -by)) % n_chips
                perm.append((ring[p] * 2 + core, ring[q] * 2 + core))
        return lax.ppermute(x, "col", perm)

    def send_core(x):
        return lax.ppermute(x, "col", [(c, c ^ 1) for c in range(n_cols)])

    def send_row(x, by):
        return lax.ppermute(x, "row", [(r, (r + by) % n_rows) for r in range(n_rows)])

    reach = [0]
    for j in range(1, n_chips // 2 + 1):
        reach += [j] if 2 * j == n_chips else [j, -j]
    steps = [(j, other) for j in reach for other in range(2)]
    table = []
    for c in range(n_cols):
        p, core = ring.index(c // 2), c % 2
        line = []
        for j, other in steps:
            of_core = core ^ other
            q = (p - j if of_core == 0 else p + j) % n_chips
            line.append(ring[q] * 2 + of_core)
        table.append(line)
    place = jnp.stack([row, col]).astype(jnp.int32)

    weight = pltpu.with_memory_space_constraint(weight, pltpu.HBM)
    block_mask = pltpu.with_memory_space_constraint(block_mask, pltpu.HBM)
    piece_blocks = piece // BLOCK
    early = max(1, piece_blocks * 3 // 7)
    kept_early, spread = pl.pallas_call(
        spread_and_keep_kernel,
        in_specs=[in_smem(), in_hbm(), in_hbm()],
        out_specs=[in_vmem()] * 2,
        out_shape=[
            pltpu.VMEM((early * BLOCK, width), bf16),
            pltpu.VMEM((blocks, width), jnp.float32),
        ],
        scratch_shapes=[
            pltpu.VMEM(block_mask.shape, jnp.int32),
            pltpu.SemaphoreType.DMA,
            pltpu.SemaphoreType.DMA((early,)),
        ],
        compiler_params=params(),
        cost_estimate=cost(early * BLOCK * width, 2 * early * BLOCK * width),
        name="spread_and_keep",
    )(place, weight, block_mask)

    held = {0: grad_output}
    for j in (2, -2):
        if abs(j) < n_chips // 2 or j == n_chips // 2:
            held[j] = send_ring(grad_output, j)
    far = [j for j in held if j]
    spread, again = lax.optimization_barrier((spread, grad_output))
    held[1], held[-1] = send_ring(again, 1), send_ring(again, -1)
    acts = [inputs] + [send_row(inputs, k) for k in range(1, n_rows)]
    spread, *ready = lax.optimization_barrier((spread, *(held[j] for j in far)))
    held.update(zip(far, ready, strict=True))
    last = range(3, n_chips // 2 + 1)
    for j in last:
        by = 1 if j % 2 else 2
        held[j] = send_ring(held[j - by], by)
        if 2 * j < n_chips:
            held[-j] = send_ring(held[by - j], -by)

    kepts = [kept_early]
    if early < piece_blocks:
        late = piece_blocks - early
        spread, held[1], held[-1] = lax.optimization_barrier((spread, held[1], held[-1]))
        kept_late = pl.pallas_call(
            functools.partial(keep_kernel, early),
            in_specs=[in_vmem(), in_hbm()],
            out_specs=in_vmem(),
            out_shape=pltpu.VMEM((late * BLOCK, width), bf16),
            scratch_shapes=[pltpu.SemaphoreType.DMA((late,))],
            compiler_params=params(),
            cost_estimate=cost(late * BLOCK * width, 2 * late * BLOCK * width),
            name="keep",
        )(spread, weight)
        kept_late, *ready = lax.optimization_barrier(
            (kept_late, *(held[j] for j in reach if abs(j) > 2))
        )
        held.update(zip([j for j in reach if abs(j) > 2], ready, strict=True))
        kepts.append(kept_late)
    shards = []
    for j in reach:
        shards += [held[j], send_core(held[j])]

    acts_turned = pl.pallas_call(
        functools.partial(turn_kernel, n_rows),
        in_specs=[in_vmem()] * n_rows,
        out_specs=in_vmem(),
        out_shape=jax.ShapeDtypeStruct((hidden, all_tokens), bf16),
        compiler_params=params(),
        cost_estimate=cost(all_tokens * hidden, 4 * all_tokens * hidden),
        name="turn",
    )(*acts)

    n_shards = len(shards)
    code_rows = -(-(piece // BLOCK) // 16) * 16
    sent_shape = jax.ShapeDtypeStruct((piece + code_rows, tokens), jnp.int16)
    own_shape = jax.ShapeDtypeStruct((piece, tokens), jnp.float32)
    small_cost = cost(piece * width, piece * width // 8)
    full, turned, own, *coded = pl.pallas_call(
        functools.partial(
            first_terms_kernel, n_shards, len(kepts), n_parts, tokens // shard_rows, chunk
        ),
        in_specs=[in_smem()] * 2 + [in_vmem()] * (n_shards + len(kepts)) + [in_hbm()],
        out_specs=[in_vmem()] * (3 + n_parts),
        out_shape=[
            jax.ShapeDtypeStruct((all_tokens, width), bf16),
            jax.ShapeDtypeStruct((width, all_tokens), bf16),
            own_shape,
        ]
        + [sent_shape] * n_parts,
        scratch_shapes=[pltpu.VMEM((piece, all_tokens), jnp.float32)],
        compiler_params=params(),
        cost_estimate=small_cost,
        name="first_terms",
    )(place, jnp.array(table, jnp.int32), *shards, *kepts, acts_turned)
    owns = [own]
    parts = [send_row(coded[k], k + 1) for k in range(n_parts)]

    for p in range(1, n_pieces):
        own, *coded = pl.pallas_call(
            functools.partial(more_terms_kernel, n_parts, p * piece_blocks, chunk),
            in_specs=[in_vmem(), in_hbm(), in_vmem()],
            out_specs=[in_vmem()] * (1 + n_parts),
            out_shape=[own_shape] + [sent_shape] * n_parts,
            scratch_shapes=[
                pltpu.VMEM((piece, width), bf16),
                pltpu.VMEM((piece, all_tokens), jnp.float32),
                pltpu.SemaphoreType.DMA((width // chunk,)),
            ],
            compiler_params=params(),
            cost_estimate=small_cost,
            name="more_terms",
        )(turned, weight, spread)
        owns.append(own)
        parts += [send_row(coded[k], k + 1) for k in range(n_parts)]

    grad_weight = pl.pallas_call(
        functools.partial(weight_grad_kernel, chunk),
        in_specs=[in_vmem()] * 3,
        out_specs=in_hbm(),
        out_shape=jax.ShapeDtypeStruct((hidden, width), bf16),
        scratch_shapes=[
            pltpu.VMEM((hidden, width), bf16),
            pltpu.SemaphoreType.DMA((blocks,)),
        ],
        compiler_params=params(),
        cost_estimate=small_cost,
        name="weight_grad",
    )(acts_turned, full, spread)

    grad_input = None
    for p in range(n_pieces):
        operands = [owns[p], *parts[p * n_parts : (p + 1) * n_parts]]
        specs = [in_vmem()] * len(operands)
        if p:
            operands.append(grad_input)
            specs.append(in_hbm())
        grad_input = pl.pallas_call(
            functools.partial(finish_kernel, n_parts),
            grid=(1,),
            in_specs=specs,
            out_specs=pl.BlockSpec((tokens, piece), lambda i, p=p: (0, p)),
            out_shape=jax.ShapeDtypeStruct((tokens, hidden), bf16),
            input_output_aliases={len(operands) - 1: 0} if p else {},
            compiler_params=params(),
            name="add_terms",
        )(*operands)
    return (grad_input, grad_weight)


def solution(mesh):
    return jax.shard_map(
        functools.partial(per_device, mesh.shape["row"], mesh.shape["col"]),
        mesh=mesh,
        in_specs=(P("col", "row"), P("row", "col"), P("col", "row"), P("col", None)),
        out_specs=(P("row", "col"), P("col", "row")),
        check_vma=False,
    )
```

```python
import functools

import jax
import jax.numpy as jnp
from jax import lax
from jax.experimental import pallas as pl
from jax.experimental.pallas import tpu as pltpu
from jax.sharding import PartitionSpec as P

BLOCK = 128
CODE = 32700.0
STEPS = 64.0
VMEM_LIMIT = 24 * 1024 * 1024


def chip_ring(cols):
    half, fast = cols // 2, 1
    while half % (fast * 2) == 0 and fast * 2 * fast * 2 <= half:
        fast *= 2
    slow = half // fast
    ring = []
    for s in range(slow):
        along = range(1, fast) if s % 2 == 0 else range(fast - 1, 0, -1)
        ring += [s * fast + f for f in along]
    ring += [s * fast for s in range(slow - 1, -1, -1)]
    return ring


def encode(part):
    top = jnp.max(jnp.abs(part), axis=0, keepdims=True)
    code = jnp.ceil(STEPS * jnp.log2(jnp.maximum(top, 1e-30)))
    scaled = part * (jnp.exp2(code * (-1.0 / STEPS)) * CODE)
    whole = jnp.clip(jnp.round(scaled), -32767.0, 32767.0)
    return whole.astype(jnp.int32), code.astype(jnp.int32)


def wide_mask(mask, first, width):
    cols = mask.shape[1]
    of_column = first + lax.broadcasted_iota(jnp.int32, (cols, width), 1) // BLOCK
    spread = of_column == lax.broadcasted_iota(jnp.int32, (cols, width), 0)
    return jnp.dot(
        mask.astype(jnp.float32).astype(jnp.bfloat16),
        spread.astype(jnp.float32).astype(jnp.bfloat16),
        preferred_element_type=jnp.float32,
    )


def spread_and_keep_kernel(place, weight, mask, kept, spread, mask_here, mask_sem, sems):
    rows, width = kept.shape
    mask_copy = pltpu.make_async_copy(mask, mask_here, mask_sem)
    mask_copy.start()
    copies = fetch(weight, 0, kept, sems)
    mask_copy.wait()
    spread[...] = wide_mask(mask_here[...], place[0] * (width // BLOCK), width)
    drop_blocks(copies, kept, spread[: rows // BLOCK, :])


def keep_kernel(first, spread, weight, kept, sems):
    copies = fetch(weight, first, kept, sems)
    drop_blocks(copies, kept, spread[first : first + kept.shape[0] // BLOCK, :])


def fetch(weight, first, kept, sems):
    copies = []
    for b in range(kept.shape[0] // BLOCK):
        copies.append(
            pltpu.make_async_copy(
                weight.at[pl.ds((first + b) * BLOCK, BLOCK), :],
                kept.at[pl.ds(b * BLOCK, BLOCK), :],
                sems.at[b],
            )
        )
        copies[-1].start()
    return copies


def drop_blocks(copies, kept, spread):
    factors = spread.astype(jnp.bfloat16)
    for b, copy in enumerate(copies):
        copy.wait()
        at = slice(b * BLOCK, (b + 1) * BLOCK)
        kept[at, :] = kept[at, :] * factors[b : b + 1, :]


def turn_kernel(n_rows, *refs):
    acts, out = refs[:n_rows], refs[n_rows]
    tokens, hidden = acts[0].shape
    for k in range(n_rows):
        place = (n_rows - k) % n_rows
        for c in range(0, hidden, BLOCK):
            out[c : c + BLOCK, place * tokens : (place + 1) * tokens] = acts[k][:, c : c + BLOCK].T


def store_terms(total, own, outs):
    rows, tokens = own.shape
    own[...] = total[:, :tokens]
    for k, out in enumerate(outs):
        of_code = lax.broadcasted_iota(jnp.int32, (out.shape[0] - rows, tokens), 0)
        codes = jnp.zeros(of_code.shape, jnp.int32)
        for b in range(rows // BLOCK):
            at = slice(b * BLOCK, (b + 1) * BLOCK)
            whole, code = encode(total[at, (k + 1) * tokens : (k + 2) * tokens])
            out[at, :] = whole.astype(jnp.int16)
            codes = jnp.where(of_code == b, code, codes)
        out[rows:, :] = codes.astype(jnp.int16)


def add_products(total, at, weight, turned, chunk, factors=None):
    rows = weight.shape[0]
    for c in range(0, weight.shape[1], chunk):
        cols = slice(c, c + chunk)
        kept = weight[:, cols]
        if factors is not None:
            of_blocks = factors[:, cols].astype(jnp.bfloat16)
            kept = jnp.concatenate(
                [
                    kept[b * BLOCK : (b + 1) * BLOCK, :] * of_blocks[b : b + 1, :]
                    for b in range(rows // BLOCK)
                ],
                axis=0,
            )
        terms = jnp.dot(kept, turned[cols, :], preferred_element_type=jnp.float32)
        to = slice(at, at + rows)
        total[to, :] = terms if c == 0 else total[to, :] + terms


def first_terms_kernel(n_shards, n_kept, n_parts, shift, chunk, first, place, table, *refs):
    shards, kepts = refs[:n_shards], refs[n_shards : n_shards + n_kept]
    weight, _, full, turned, own, ahead, *outs, total, sems = refs[n_shards + n_kept :]
    copies = fetch(weight, first, ahead, sems)
    rows = shards[0].shape[0]
    n_cols = table.shape[0]
    for n, shard in enumerate(shards):
        to = lax.rem(table[place[1], n] + n_cols - place[0] * shift, n_cols)
        full[pl.ds(pl.multiple_of(to * rows, rows), rows), :] = shard[...]
    for c in range(0, full.shape[1], chunk):
        cols = slice(c, c + chunk)
        turned[cols, :] = full[:, cols].T
        at = 0
        for kept in kepts:
            to = slice(at, at + kept.shape[0])
            terms = jnp.dot(kept[:, cols], turned[cols, :], preferred_element_type=jnp.float32)
            total[to, :] = terms if c == 0 else total[to, :] + terms
            at += kept.shape[0]
    store_terms(total, own, outs)
    for copy in copies:
        copy.wait()


def more_terms_kernel(n_parts, first, chunk, turned, ahead, weight, spread, own, *refs):
    outs, (here, total, sems) = refs[:n_parts], refs[n_parts:]
    there = ahead.shape[0] // BLOCK
    copies = fetch(weight, first + there, here, sems)
    add_products(total, 0, ahead, turned, chunk, spread[first : first + there, :])
    for copy in copies:
        copy.wait()
    last = first + there + here.shape[0] // BLOCK
    add_products(total, ahead.shape[0], here, turned, chunk, spread[first + there : last, :])
    store_terms(total, own, outs)


def weight_grad_kernel(chunk, acts, full, spread, out, held, sems):
    hidden, width = out.shape
    blocks = hidden // BLOCK
    pair = 2 if blocks % 2 == 0 else 1

    def leave(block):
        at = pl.ds(pl.multiple_of(block * BLOCK, BLOCK), BLOCK)
        return pltpu.make_async_copy(held.at[at, :], out.at[at, :], sems.at[block])

    def rows(step, _):
        first = step * pair
        left = acts[pl.ds(pl.multiple_of(first * BLOCK, pair * BLOCK), pair * BLOCK), :]
        for c in range(0, width, chunk):
            cols = slice(c, c + chunk)
            product = jnp.dot(left, full[:, cols], preferred_element_type=jnp.float32)
            for b in range(pair):
                at = pl.ds(pl.multiple_of((first + b) * BLOCK, BLOCK), BLOCK)
                part = product[b * BLOCK : (b + 1) * BLOCK, :] * spread[pl.ds(first + b, 1), cols]
                held[at, cols] = part.astype(out.dtype)
        for b in range(pair):
            leave(first + b).start()
        return 0

    lax.fori_loop(0, blocks // pair, rows, 0)
    lax.fori_loop(0, blocks, lambda block, _: (leave(block).wait(), 0)[1], 0)


def finish_kernel(n_parts, own, *refs):
    parts, out = refs[:n_parts], refs[-1]
    rows = own.shape[0]
    scales = []
    for part in parts:
        code = part[rows:, :].astype(jnp.int32).astype(jnp.float32)
        scales.append(jnp.exp2(code * (1.0 / STEPS)) * (1.0 / CODE))
    for b in range(rows // BLOCK):
        at = slice(b * BLOCK, (b + 1) * BLOCK)
        total = own[at, :]
        for part, scale in zip(parts, scales, strict=True):
            got = part[at, :].astype(jnp.int32).astype(jnp.float32)
            total = total + got * scale[b : b + 1, :]
        out[:, at] = total.T.astype(out.dtype)


def in_vmem():
    return pl.BlockSpec(memory_space=pltpu.VMEM)


def in_smem():
    return pl.BlockSpec(memory_space=pltpu.SMEM)


def in_hbm():
    return pl.BlockSpec(memory_space=pl.ANY)


def params():
    return pltpu.CompilerParams(vmem_limit_bytes=VMEM_LIMIT)


def cost(flops, nbytes):
    return pl.CostEstimate(flops=flops, bytes_accessed=nbytes, transcendentals=0)


def per_device(n_rows, n_cols, grad_output, inputs, weight, block_mask):
    row, col = lax.axis_index("row"), lax.axis_index("col")
    hidden, width = weight.shape
    blocks = hidden // BLOCK
    n_pieces = 2 if blocks % 2 == 0 else 1
    piece = hidden // n_pieces
    n_parts = n_rows - 1
    tokens = inputs.shape[0]
    shard_rows = grad_output.shape[0]
    all_tokens = tokens * n_rows
    chunk = min(512, width)
    bf16 = jnp.bfloat16

    ring = chip_ring(n_cols)
    n_chips = len(ring)

    def send_ring(x, by):
        perm = []
        for p in range(n_chips):
            for core in range(2):
                q = (p + (by if core == 0 else -by)) % n_chips
                perm.append((ring[p] * 2 + core, ring[q] * 2 + core))
        return lax.ppermute(x, "col", perm)

    def send_core(x):
        return lax.ppermute(x, "col", [(c, c ^ 1) for c in range(n_cols)])

    def send_row(x, by):
        return lax.ppermute(x, "row", [(r, (r + by) % n_rows) for r in range(n_rows)])

    reach = [0]
    for j in range(1, n_chips // 2 + 1):
        reach += [j] if 2 * j == n_chips else [j, -j]
    steps = [(j, other) for j in reach for other in range(2)]
    table = []
    for c in range(n_cols):
        p, core = ring.index(c // 2), c % 2
        line = []
        for j, other in steps:
            of_core = core ^ other
            q = (p - j if of_core == 0 else p + j) % n_chips
            line.append(ring[q] * 2 + of_core)
        table.append(line)
    place = jnp.stack([row, col]).astype(jnp.int32)

    weight = pltpu.with_memory_space_constraint(weight, pltpu.HBM)
    block_mask = pltpu.with_memory_space_constraint(block_mask, pltpu.HBM)
    piece_blocks = piece // BLOCK
    early = max(1, piece_blocks * 3 // 7)
    kept_early, spread = pl.pallas_call(
        spread_and_keep_kernel,
        in_specs=[in_smem(), in_hbm(), in_hbm()],
        out_specs=[in_vmem()] * 2,
        out_shape=[
            pltpu.VMEM((early * BLOCK, width), bf16),
            pltpu.VMEM((blocks, width), jnp.float32),
        ],
        scratch_shapes=[
            pltpu.VMEM(block_mask.shape, jnp.int32),
            pltpu.SemaphoreType.DMA,
            pltpu.SemaphoreType.DMA((early,)),
        ],
        compiler_params=params(),
        cost_estimate=cost(early * BLOCK * width, 2 * early * BLOCK * width),
        name="spread_and_keep",
    )(place, weight, block_mask)

    held = {0: grad_output}
    for j in (2, -2):
        if abs(j) < n_chips // 2 or j == n_chips // 2:
            held[j] = send_ring(grad_output, j)
    far = [j for j in held if j]
    spread, again = lax.optimization_barrier((spread, grad_output))
    held[1], held[-1] = send_ring(again, 1), send_ring(again, -1)
    acts = [inputs] + [send_row(inputs, k) for k in range(1, n_rows)]

    kepts = [kept_early]
    if early < piece_blocks:
        late = piece_blocks - early
        kept_late = pl.pallas_call(
            functools.partial(keep_kernel, early),
            in_specs=[in_vmem(), in_hbm()],
            out_specs=in_vmem(),
            out_shape=pltpu.VMEM((late * BLOCK, width), bf16),
            scratch_shapes=[pltpu.SemaphoreType.DMA((late,))],
            compiler_params=params(),
            cost_estimate=cost(late * BLOCK * width, 2 * late * BLOCK * width),
            name="keep",
        )(spread, weight)
        kepts.append(kept_late)
    kepts[-1], *ready = lax.optimization_barrier((kepts[-1], *(held[j] for j in far)))
    held.update(zip(far, ready, strict=True))
    for j in range(3, n_chips // 2 + 1):
        by = 1 if j % 2 else 2
        held[j] = send_ring(held[j - by], by)
        if 2 * j < n_chips:
            held[-j] = send_ring(held[by - j], -by)

    *acts, held[1], held[-1] = lax.optimization_barrier((*acts, held[1], held[-1]))
    acts_turned = pl.pallas_call(
        functools.partial(turn_kernel, n_rows),
        in_specs=[in_vmem()] * n_rows,
        out_specs=in_vmem(),
        out_shape=jax.ShapeDtypeStruct((hidden, all_tokens), bf16),
        compiler_params=params(),
        cost_estimate=cost(all_tokens * hidden, 4 * all_tokens * hidden),
        name="turn",
    )(*acts)
    last = [j for j in reach if abs(j) > 2]
    acts_turned, *ready = lax.optimization_barrier((acts_turned, *(held[j] for j in last)))
    held.update(zip(last, ready, strict=True))
    shards = []
    for j in reach:
        shards += [held[j], send_core(held[j])]

    n_shards = len(shards)
    code_rows = -(-(piece // BLOCK) // 16) * 16
    sent_shape = jax.ShapeDtypeStruct((piece + code_rows, tokens), jnp.int16)
    own_shape = jax.ShapeDtypeStruct((piece, tokens), jnp.float32)
    small_cost = cost(piece * width, piece * width // 8)
    n_ahead = piece_blocks - early if n_pieces > 1 else 1
    full, turned, own, ahead, *coded = pl.pallas_call(
        functools.partial(
            first_terms_kernel,
            n_shards,
            len(kepts),
            n_parts,
            tokens // shard_rows,
            chunk,
            (n_pieces - 1) * piece_blocks,
        ),
        in_specs=[in_smem()] * 2 + [in_vmem()] * (n_shards + len(kepts)) + [in_hbm()] * 2,
        out_specs=[in_vmem()] * (4 + n_parts),
        out_shape=[
            jax.ShapeDtypeStruct((all_tokens, width), bf16),
            jax.ShapeDtypeStruct((width, all_tokens), bf16),
            own_shape,
            pltpu.VMEM((n_ahead * BLOCK, width), bf16),
        ]
        + [sent_shape] * n_parts,
        scratch_shapes=[
            pltpu.VMEM((piece, all_tokens), jnp.float32),
            pltpu.SemaphoreType.DMA((n_ahead,)),
        ],
        compiler_params=params(),
        cost_estimate=small_cost,
        name="first_terms",
    )(place, jnp.array(table, jnp.int32), *shards, *kepts, weight, acts_turned)
    owns = [own]
    parts = [send_row(coded[k], k + 1) for k in range(n_parts)]

    if n_pieces > 1:
        own, *coded = pl.pallas_call(
            functools.partial(more_terms_kernel, n_parts, piece_blocks, chunk),
            in_specs=[in_vmem(), in_vmem(), in_hbm(), in_vmem()],
            out_specs=[in_vmem()] * (1 + n_parts),
            out_shape=[own_shape] + [sent_shape] * n_parts,
            scratch_shapes=[
                pltpu.VMEM((early * BLOCK, width), bf16),
                pltpu.VMEM((piece, all_tokens), jnp.float32),
                pltpu.SemaphoreType.DMA((early,)),
            ],
            compiler_params=params(),
            cost_estimate=small_cost,
            name="more_terms",
        )(turned, ahead, weight, spread)
        owns.append(own)
        parts += [send_row(coded[k], k + 1) for k in range(n_parts)]

    grad_weight = pl.pallas_call(
        functools.partial(weight_grad_kernel, chunk),
        in_specs=[in_vmem()] * 3,
        out_specs=in_hbm(),
        out_shape=jax.ShapeDtypeStruct((hidden, width), bf16),
        scratch_shapes=[
            pltpu.VMEM((hidden, width), bf16),
            pltpu.SemaphoreType.DMA((blocks,)),
        ],
        compiler_params=params(),
        cost_estimate=small_cost,
        name="weight_grad",
    )(acts_turned, full, spread)

    grad_input = None
    for p in range(n_pieces):
        operands = [owns[p], *parts[p * n_parts : (p + 1) * n_parts]]
        specs = [in_vmem()] * len(operands)
        if p:
            operands.append(grad_input)
            specs.append(in_hbm())
        grad_input = pl.pallas_call(
            functools.partial(finish_kernel, n_parts),
            grid=(1,),
            in_specs=specs,
            out_specs=pl.BlockSpec((tokens, piece), lambda i, p=p: (0, p)),
            out_shape=jax.ShapeDtypeStruct((tokens, hidden), bf16),
            input_output_aliases={len(operands) - 1: 0} if p else {},
            compiler_params=params(),
            name="add_terms",
        )(*operands)
    return (grad_input, grad_weight)


def solution(mesh):
    return jax.shard_map(
        functools.partial(per_device, mesh.shape["row"], mesh.shape["col"]),
        mesh=mesh,
        in_specs=(P("col", "row"), P("row", "col"), P("col", "row"), P("col", None)),
        out_specs=(P("row", "col"), P("col", "row")),
        check_vma=False,
    )
```

```python
import functools

import jax
import jax.numpy as jnp
from jax import lax
from jax.experimental import pallas as pl
from jax.experimental.pallas import tpu as pltpu
from jax.sharding import PartitionSpec as P

BLOCK = 128
CODE = 32700.0
STEPS = 64.0
VMEM_LIMIT = 24 * 1024 * 1024


def chip_ring(cols):
    half, fast = cols // 2, 1
    while half % (fast * 2) == 0 and fast * 2 * fast * 2 <= half:
        fast *= 2
    slow = half // fast
    ring = []
    for s in range(slow):
        along = range(1, fast) if s % 2 == 0 else range(fast - 1, 0, -1)
        ring += [s * fast + f for f in along]
    ring += [s * fast for s in range(slow - 1, -1, -1)]
    return ring


def encode(part):
    top = jnp.max(jnp.abs(part), axis=0, keepdims=True)
    code = jnp.ceil(STEPS * jnp.log2(jnp.maximum(top, 1e-30)))
    scaled = part * (jnp.exp2(code * (-1.0 / STEPS)) * CODE)
    whole = jnp.clip(jnp.round(scaled), -32767.0, 32767.0)
    return whole.astype(jnp.int32), code.astype(jnp.int32)


def wide_mask(mask, first, width):
    cols = mask.shape[1]
    of_column = first + lax.broadcasted_iota(jnp.int32, (cols, width), 1) // BLOCK
    spread = of_column == lax.broadcasted_iota(jnp.int32, (cols, width), 0)
    return jnp.dot(
        mask.astype(jnp.float32).astype(jnp.bfloat16),
        spread.astype(jnp.float32).astype(jnp.bfloat16),
        preferred_element_type=jnp.float32,
    )


def spread_and_keep_kernel(place, weight, mask, kept, spread, mask_here, mask_sem, sems):
    rows, width = kept.shape
    mask_copy = pltpu.make_async_copy(mask, mask_here, mask_sem)
    mask_copy.start()
    fetch(weight, 0, kept, sems)
    mask_copy.wait()
    spread[...] = wide_mask(mask_here[...], place[0] * (width // BLOCK), width)
    drop_blocks(weight, 0, kept, spread, sems)


def keep_kernel(first, spread, weight, kept, sems):
    fetch(weight, first, kept, sems)
    drop_blocks(weight, first, kept, spread, sems)


def row_copy(weight, first, here, sems, block):
    to = pl.multiple_of(block * BLOCK, BLOCK)
    at = pl.multiple_of((first + block) * BLOCK, BLOCK)
    return pltpu.make_async_copy(
        weight.at[pl.ds(at, BLOCK), :], here.at[pl.ds(to, BLOCK), :], sems.at[block]
    )


def fetch(weight, first, here, sems):
    blocks = here.shape[0] // BLOCK
    lax.fori_loop(0, blocks, lambda b, _: (row_copy(weight, first, here, sems, b).start(), 0)[1], 0)


def fetched(weight, first, here, sems):
    blocks = here.shape[0] // BLOCK
    lax.fori_loop(0, blocks, lambda b, _: (row_copy(weight, first, here, sems, b).wait(), 0)[1], 0)


def drop_blocks(weight, first, kept, spread, sems):
    def one(b, _):
        row_copy(weight, first, kept, sems, b).wait()
        at = pl.ds(pl.multiple_of(b * BLOCK, BLOCK), BLOCK)
        kept[at, :] = kept[at, :] * spread[pl.ds(first + b, 1), :].astype(kept.dtype)
        return 0

    lax.fori_loop(0, kept.shape[0] // BLOCK, one, 0)


def turn_kernel(n_rows, *refs):
    acts, out = refs[:n_rows], refs[n_rows]
    tokens, hidden = acts[0].shape
    for k in range(n_rows):
        place = (n_rows - k) % n_rows
        for c in range(0, hidden, BLOCK):
            out[c : c + BLOCK, place * tokens : (place + 1) * tokens] = acts[k][:, c : c + BLOCK].T


def store_terms(total, own, outs):
    rows, tokens = own.shape
    own[...] = total[:, :tokens]
    for k, out in enumerate(outs):
        of_code = lax.broadcasted_iota(jnp.int32, (out.shape[0] - rows, tokens), 0)

        def one(b, codes, k=k, out=out, of_code=of_code):
            at = pl.ds(pl.multiple_of(b * BLOCK, BLOCK), BLOCK)
            whole, code = encode(total[at, (k + 1) * tokens : (k + 2) * tokens])
            out[at, :] = whole.astype(jnp.int16)
            return jnp.where(of_code == b, code, codes)

        codes = lax.fori_loop(0, rows // BLOCK, one, jnp.zeros(of_code.shape, jnp.int32))
        out[rows:, :] = codes.astype(jnp.int16)


def first_terms_kernel(n_shards, n_kept, n_parts, shift, chunk, first, place, table, *refs):
    shards, kepts = refs[:n_shards], refs[n_shards : n_shards + n_kept]
    weight, _, full, turned, own, ahead, *outs, total, sems = refs[n_shards + n_kept :]
    fetch(weight, first, ahead, sems)
    rows = shards[0].shape[0]
    n_cols = table.shape[0]
    for n, shard in enumerate(shards):
        to = lax.rem(table[place[1], n] + n_cols - place[0] * shift, n_cols)
        full[pl.ds(pl.multiple_of(to * rows, rows), rows), :] = shard[...]
    n_chunks = full.shape[1] // chunk

    def columns(c):
        return pl.ds(pl.multiple_of(c * chunk, chunk), chunk)

    turned[:chunk, :] = full[:, :chunk].T
    total[...] = jnp.zeros_like(total)

    def one(c, _):
        cols, after = columns(c), columns(lax.rem(c + 1, n_chunks))
        at = 0
        for kept in kepts:
            to = slice(at, at + kept.shape[0])
            total[to, :] += jnp.dot(
                kept[:, cols], turned[cols, :], preferred_element_type=jnp.float32
            )
            at += kept.shape[0]
        turned[after, :] = full[:, after].T
        return 0

    lax.fori_loop(0, n_chunks, one, 0)
    store_terms(total, own, outs)
    fetched(weight, first, ahead, sems)


def more_terms_kernel(n_parts, first, chunk, turned, ahead, spread, own, *refs):
    outs, (total,) = refs[:n_parts], refs[n_parts:]
    blocks = own.shape[0] // BLOCK
    total[...] = jnp.zeros_like(total)

    def one(c, _):
        cols = pl.ds(pl.multiple_of(c * chunk, chunk), chunk)
        factors = spread[first : first + blocks, cols].astype(jnp.bfloat16)
        kept = jnp.concatenate(
            [
                ahead[b * BLOCK : (b + 1) * BLOCK, cols] * factors[b : b + 1, :]
                for b in range(blocks)
            ],
            axis=0,
        )
        total[...] += jnp.dot(kept, turned[cols, :], preferred_element_type=jnp.float32)
        return 0

    lax.fori_loop(0, turned.shape[0] // chunk, one, 0)
    store_terms(total, own, outs)


def weight_grad_kernel(chunk, acts, full, spread, out, held, sems):
    hidden, width = out.shape
    blocks = hidden // BLOCK
    pair = 2 if blocks % 2 == 0 else 1

    def leave(block):
        at = pl.ds(pl.multiple_of(block * BLOCK, BLOCK), BLOCK)
        return pltpu.make_async_copy(held.at[at, :], out.at[at, :], sems.at[block])

    def rows(step, _):
        first = step * pair
        left = acts[pl.ds(pl.multiple_of(first * BLOCK, pair * BLOCK), pair * BLOCK), :]
        for c in range(0, width, chunk):
            cols = slice(c, c + chunk)
            product = jnp.dot(left, full[:, cols], preferred_element_type=jnp.float32)
            for b in range(pair):
                at = pl.ds(pl.multiple_of((first + b) * BLOCK, BLOCK), BLOCK)
                part = product[b * BLOCK : (b + 1) * BLOCK, :] * spread[pl.ds(first + b, 1), cols]
                held[at, cols] = part.astype(out.dtype)
        for b in range(pair):
            leave(first + b).start()
        return 0

    lax.fori_loop(0, blocks // pair, rows, 0)
    lax.fori_loop(0, blocks, lambda block, _: (leave(block).wait(), 0)[1], 0)


def finish_kernel(n_parts, own, *refs):
    parts, out = refs[:n_parts], refs[-1]
    rows = own.shape[0]
    scales = []
    for part in parts:
        code = part[rows:, :].astype(jnp.int32).astype(jnp.float32)
        scales.append(jnp.exp2(code * (1.0 / STEPS)) * (1.0 / CODE))

    of_code = lax.broadcasted_iota(jnp.int32, scales[0].shape, 0)

    def one(b, _):
        at = pl.ds(pl.multiple_of(b * BLOCK, BLOCK), BLOCK)
        total = own[at, :]
        for part, scale in zip(parts, scales, strict=True):
            got = part[at, :].astype(jnp.int32).astype(jnp.float32)
            total = total + got * jnp.sum(
                jnp.where(of_code == b, scale, 0.0), axis=0, keepdims=True
            )
        out[:, at] = total.T.astype(out.dtype)
        return 0

    lax.fori_loop(0, rows // BLOCK, one, 0)


def in_vmem():
    return pl.BlockSpec(memory_space=pltpu.VMEM)


def in_smem():
    return pl.BlockSpec(memory_space=pltpu.SMEM)


def in_hbm():
    return pl.BlockSpec(memory_space=pl.ANY)


def params():
    return pltpu.CompilerParams(vmem_limit_bytes=VMEM_LIMIT)


def cost(flops, nbytes):
    return pl.CostEstimate(flops=flops, bytes_accessed=nbytes, transcendentals=0)


def per_device(n_rows, n_cols, grad_output, inputs, weight, block_mask):
    row, col = lax.axis_index("row"), lax.axis_index("col")
    hidden, width = weight.shape
    blocks = hidden // BLOCK
    n_pieces = 2 if blocks % 2 == 0 else 1
    piece = hidden // n_pieces
    n_parts = n_rows - 1
    tokens = inputs.shape[0]
    shard_rows = grad_output.shape[0]
    all_tokens = tokens * n_rows
    chunk = min(512, width)
    bf16 = jnp.bfloat16

    ring = chip_ring(n_cols)
    n_chips = len(ring)

    def send_ring(x, by):
        perm = []
        for p in range(n_chips):
            for core in range(2):
                q = (p + (by if core == 0 else -by)) % n_chips
                perm.append((ring[p] * 2 + core, ring[q] * 2 + core))
        return lax.ppermute(x, "col", perm)

    def send_core(x):
        return lax.ppermute(x, "col", [(c, c ^ 1) for c in range(n_cols)])

    def send_row(x, by):
        return lax.ppermute(x, "row", [(r, (r + by) % n_rows) for r in range(n_rows)])

    reach = [0]
    for j in range(1, n_chips // 2 + 1):
        reach += [j] if 2 * j == n_chips else [j, -j]
    steps = [(j, other) for j in reach for other in range(2)]
    table = []
    for c in range(n_cols):
        p, core = ring.index(c // 2), c % 2
        line = []
        for j, other in steps:
            of_core = core ^ other
            q = (p - j if of_core == 0 else p + j) % n_chips
            line.append(ring[q] * 2 + of_core)
        table.append(line)
    place = jnp.stack([row, col]).astype(jnp.int32)

    weight = pltpu.with_memory_space_constraint(weight, pltpu.HBM)
    block_mask = pltpu.with_memory_space_constraint(block_mask, pltpu.HBM)
    piece_blocks = piece // BLOCK
    early = max(1, piece_blocks * 3 // 7)
    kept_early, spread = pl.pallas_call(
        spread_and_keep_kernel,
        in_specs=[in_smem(), in_hbm(), in_hbm()],
        out_specs=[in_vmem()] * 2,
        out_shape=[
            pltpu.VMEM((early * BLOCK, width), bf16),
            pltpu.VMEM((blocks, width), jnp.float32),
        ],
        scratch_shapes=[
            pltpu.VMEM(block_mask.shape, jnp.int32),
            pltpu.SemaphoreType.DMA,
            pltpu.SemaphoreType.DMA((early,)),
        ],
        compiler_params=params(),
        cost_estimate=cost(early * BLOCK * width, 2 * early * BLOCK * width),
        name="spread_and_keep",
    )(place, weight, block_mask)

    held = {0: grad_output}
    for j in (2, -2):
        if abs(j) < n_chips // 2 or j == n_chips // 2:
            held[j] = send_ring(grad_output, j)
    far = [j for j in held if j]
    spread, again = lax.optimization_barrier((spread, grad_output))
    held[1], held[-1] = send_ring(again, 1), send_ring(again, -1)
    acts = [inputs] + [send_row(inputs, k) for k in range(1, n_rows)]

    kepts = [kept_early]
    if early < piece_blocks:
        late = piece_blocks - early
        kept_late = pl.pallas_call(
            functools.partial(keep_kernel, early),
            in_specs=[in_vmem(), in_hbm()],
            out_specs=in_vmem(),
            out_shape=pltpu.VMEM((late * BLOCK, width), bf16),
            scratch_shapes=[pltpu.SemaphoreType.DMA((late,))],
            compiler_params=params(),
            cost_estimate=cost(late * BLOCK * width, 2 * late * BLOCK * width),
            name="keep",
        )(spread, weight)
        kepts.append(kept_late)
    kepts[-1], *ready = lax.optimization_barrier((kepts[-1], *(held[j] for j in far)))
    held.update(zip(far, ready, strict=True))
    for j in range(3, n_chips // 2 + 1):
        by = 1 if j % 2 else 2
        held[j] = send_ring(held[j - by], by)
        if 2 * j < n_chips:
            held[-j] = send_ring(held[by - j], -by)

    *acts, held[1], held[-1] = lax.optimization_barrier((*acts, held[1], held[-1]))
    acts_turned = pl.pallas_call(
        functools.partial(turn_kernel, n_rows),
        in_specs=[in_vmem()] * n_rows,
        out_specs=in_vmem(),
        out_shape=jax.ShapeDtypeStruct((hidden, all_tokens), bf16),
        compiler_params=params(),
        cost_estimate=cost(all_tokens * hidden, 4 * all_tokens * hidden),
        name="turn",
    )(*acts)
    first = [j for j in reach if abs(j) == 1]
    last = [j for j in reach if abs(j) > 2]
    acts_turned, *ready = lax.optimization_barrier(
        (acts_turned, *(send_core(held[j]) for j in first), *(held[j] for j in last))
    )
    across = dict(zip(first, ready[: len(first)], strict=True))
    ready = ready[len(first) :]
    held.update(zip(last, ready, strict=True))
    shards = []
    for j in reach:
        shards += [held[j], across[j] if j in across else send_core(held[j])]

    n_shards = len(shards)
    code_rows = -(-(piece // BLOCK) // 16) * 16
    sent_shape = jax.ShapeDtypeStruct((piece + code_rows, tokens), jnp.int16)
    own_shape = jax.ShapeDtypeStruct((piece, tokens), jnp.float32)
    small_cost = cost(piece * width, piece * width // 8)
    n_ahead = piece_blocks if n_pieces > 1 else 1
    full, turned, own, ahead, *coded = pl.pallas_call(
        functools.partial(
            first_terms_kernel,
            n_shards,
            len(kepts),
            n_parts,
            tokens // shard_rows,
            chunk,
            (n_pieces - 1) * piece_blocks,
        ),
        in_specs=[in_smem()] * 2 + [in_vmem()] * (n_shards + len(kepts)) + [in_hbm()] * 2,
        out_specs=[in_vmem()] * (4 + n_parts),
        out_shape=[
            jax.ShapeDtypeStruct((all_tokens, width), bf16),
            jax.ShapeDtypeStruct((width, all_tokens), bf16),
            own_shape,
            pltpu.VMEM((n_ahead * BLOCK, width), bf16),
        ]
        + [sent_shape] * n_parts,
        scratch_shapes=[
            pltpu.VMEM((piece, all_tokens), jnp.float32),
            pltpu.SemaphoreType.DMA((n_ahead,)),
        ],
        compiler_params=params(),
        cost_estimate=small_cost,
        name="first_terms",
    )(place, jnp.array(table, jnp.int32), *shards, *kepts, weight, acts_turned)
    owns = [own]
    parts = [send_row(coded[k], k + 1) for k in range(n_parts)]

    if n_pieces > 1:
        own, *coded = pl.pallas_call(
            functools.partial(more_terms_kernel, n_parts, piece_blocks, chunk),
            in_specs=[in_vmem()] * 3,
            out_specs=[in_vmem()] * (1 + n_parts),
            out_shape=[own_shape] + [sent_shape] * n_parts,
            scratch_shapes=[pltpu.VMEM((piece, all_tokens), jnp.float32)],
            compiler_params=params(),
            cost_estimate=small_cost,
            name="more_terms",
        )(turned, ahead, spread)
        owns.append(own)
        parts += [send_row(coded[k], k + 1) for k in range(n_parts)]

    grad_weight = pl.pallas_call(
        functools.partial(weight_grad_kernel, chunk),
        in_specs=[in_vmem()] * 3,
        out_specs=in_hbm(),
        out_shape=jax.ShapeDtypeStruct((hidden, width), bf16),
        scratch_shapes=[
            pltpu.VMEM((hidden, width), bf16),
            pltpu.SemaphoreType.DMA((blocks,)),
        ],
        compiler_params=params(),
        cost_estimate=small_cost,
        name="weight_grad",
    )(acts_turned, full, spread)

    grad_input = None
    for p in range(n_pieces):
        operands = [owns[p], *parts[p * n_parts : (p + 1) * n_parts]]
        specs = [in_vmem()] * len(operands)
        if p:
            operands.append(grad_input)
            specs.append(in_hbm())
        grad_input = pl.pallas_call(
            functools.partial(finish_kernel, n_parts),
            grid=(1,),
            in_specs=specs,
            out_specs=pl.BlockSpec((tokens, piece), lambda i, p=p: (0, p)),
            out_shape=jax.ShapeDtypeStruct((tokens, hidden), bf16),
            input_output_aliases={len(operands) - 1: 0} if p else {},
            compiler_params=params(),
            name="add_terms",
        )(*operands)
    return (grad_input, grad_weight)


def solution(mesh):
    return jax.shard_map(
        functools.partial(per_device, mesh.shape["row"], mesh.shape["col"]),
        mesh=mesh,
        in_specs=(P("col", "row"), P("row", "col"), P("col", "row"), P("col", None)),
        out_specs=(P("row", "col"), P("col", "row")),
        check_vma=False,
    )
```

```python
import functools

import jax
import jax.numpy as jnp
from jax import lax
from jax.experimental import pallas as pl
from jax.experimental.pallas import tpu as pltpu
from jax.sharding import PartitionSpec as P

BLOCK = 128
CODE = 32700.0
STEPS = 64.0
VMEM_LIMIT = 24 * 1024 * 1024


def chip_ring(cols):
    half, fast = cols // 2, 1
    while half % (fast * 2) == 0 and fast * 2 * fast * 2 <= half:
        fast *= 2
    slow = half // fast
    ring = []
    for s in range(slow):
        along = range(1, fast) if s % 2 == 0 else range(fast - 1, 0, -1)
        ring += [s * fast + f for f in along]
    ring += [s * fast for s in range(slow - 1, -1, -1)]
    return ring


def encode(part):
    top = jnp.max(jnp.abs(part), axis=0, keepdims=True)
    code = jnp.ceil(STEPS * jnp.log2(jnp.maximum(top, 1e-30)))
    scaled = part * (jnp.exp2(code * (-1.0 / STEPS)) * CODE)
    whole = jnp.clip(jnp.round(scaled), -32767.0, 32767.0)
    return whole.astype(jnp.int32), code.astype(jnp.int32)


def wide_mask(mask, first, width):
    cols = mask.shape[1]
    of_column = first + lax.broadcasted_iota(jnp.int32, (cols, width), 1) // BLOCK
    spread = of_column == lax.broadcasted_iota(jnp.int32, (cols, width), 0)
    return jnp.dot(
        mask.astype(jnp.float32).astype(jnp.bfloat16),
        spread.astype(jnp.float32).astype(jnp.bfloat16),
        preferred_element_type=jnp.float32,
    )


def spread_and_keep_kernel(place, weight, mask, kept, spread, mask_here, mask_sem, sems):
    rows, width = kept.shape
    mask_copy = pltpu.make_async_copy(mask, mask_here, mask_sem)
    mask_copy.start()
    fetch(weight, 0, kept, sems)
    mask_copy.wait()
    spread[...] = wide_mask(mask_here[...], place[0] * (width // BLOCK), width)
    drop_blocks(weight, 0, kept, spread, sems)


def keep_kernel(first, spread, weight, kept, sems):
    fetch(weight, first, kept, sems)
    drop_blocks(weight, first, kept, spread, sems)


def row_copy(weight, first, here, sems, block):
    to = pl.multiple_of(block * BLOCK, BLOCK)
    at = pl.multiple_of((first + block) * BLOCK, BLOCK)
    return pltpu.make_async_copy(
        weight.at[pl.ds(at, BLOCK), :], here.at[pl.ds(to, BLOCK), :], sems.at[block]
    )


def fetch(weight, first, here, sems):
    blocks = here.shape[0] // BLOCK
    lax.fori_loop(0, blocks, lambda b, _: (row_copy(weight, first, here, sems, b).start(), 0)[1], 0)


def fetched(weight, first, here, sems):
    blocks = here.shape[0] // BLOCK
    lax.fori_loop(0, blocks, lambda b, _: (row_copy(weight, first, here, sems, b).wait(), 0)[1], 0)


def drop_blocks(weight, first, kept, spread, sems):
    def one(b, _):
        row_copy(weight, first, kept, sems, b).wait()
        at = pl.ds(pl.multiple_of(b * BLOCK, BLOCK), BLOCK)
        kept[at, :] = kept[at, :] * spread[pl.ds(first + b, 1), :].astype(kept.dtype)
        return 0

    lax.fori_loop(0, kept.shape[0] // BLOCK, one, 0)


def turn_kernel(n_rows, first, *refs):
    acts, (weight, out, *rest) = refs[:n_rows], refs[n_rows:]
    if rest:
        fetch(weight, first, *rest)
    tokens, hidden = acts[0].shape
    for k in range(n_rows):
        place = (n_rows - k) % n_rows
        for c in range(0, hidden, BLOCK):
            out[c : c + BLOCK, place * tokens : (place + 1) * tokens] = acts[k][:, c : c + BLOCK].T
    if rest:
        fetched(weight, first, *rest)


def store_terms(total, own, outs):
    rows, tokens = own.shape
    own[...] = total[:, :tokens]
    for k, out in enumerate(outs):
        of_code = lax.broadcasted_iota(jnp.int32, (out.shape[0] - rows, tokens), 0)
        codes = jnp.zeros(of_code.shape, jnp.int32)
        for b in range(rows // BLOCK):
            at = slice(b * BLOCK, (b + 1) * BLOCK)
            whole, code = encode(total[at, (k + 1) * tokens : (k + 2) * tokens])
            out[at, :] = whole.astype(jnp.int16)
            codes = jnp.where(of_code == b, code, codes)
        out[rows:, :] = codes.astype(jnp.int16)


def first_terms_kernel(n_shards, n_kept, n_parts, shift, chunk, place, table, *refs):
    shards, kepts = refs[:n_shards], refs[n_shards : n_shards + n_kept]
    full, turned, own, *outs, total = refs[n_shards + n_kept :]
    rows = shards[0].shape[0]
    n_cols = table.shape[0]
    for n, shard in enumerate(shards):
        to = lax.rem(table[place[1], n] + n_cols - place[0] * shift, n_cols)
        full[pl.ds(pl.multiple_of(to * rows, rows), rows), :] = shard[...]
    for c in range(0, full.shape[1], chunk):
        cols = slice(c, c + chunk)
        turned[cols, :] = full[:, cols].T
        at = 0
        for kept in kepts:
            to = slice(at, at + kept.shape[0])
            terms = jnp.dot(kept[:, cols], turned[cols, :], preferred_element_type=jnp.float32)
            total[to, :] = terms if c == 0 else total[to, :] + terms
            at += kept.shape[0]
    store_terms(total, own, outs)


def more_terms_kernel(n_parts, first, chunk, turned, weight, spread, own, *refs):
    outs, (total,) = refs[:n_parts], refs[n_parts:]
    blocks = own.shape[0] // BLOCK
    for c in range(0, weight.shape[1], chunk):
        cols = slice(c, c + chunk)
        factors = spread[first : first + blocks, cols].astype(jnp.bfloat16)
        kept = jnp.concatenate(
            [weight[b * BLOCK : (b + 1) * BLOCK, cols] * factors[b : b + 1, :] for b in range(blocks)],
            axis=0,
        )
        terms = jnp.dot(kept, turned[cols, :], preferred_element_type=jnp.float32)
        total[...] = terms if c == 0 else total[...] + terms
    store_terms(total, own, outs)


def weight_grad_kernel(chunk, acts, full, spread, out, held, sems):
    hidden, width = out.shape
    blocks = hidden // BLOCK
    pair = 2 if blocks % 2 == 0 else 1
    copies = []
    for first in range(0, blocks, pair):
        left = acts[first * BLOCK : (first + pair) * BLOCK, :]
        for c in range(0, width, chunk):
            cols = slice(c, c + chunk)
            product = jnp.dot(left, full[:, cols], preferred_element_type=jnp.float32)
            for b in range(pair):
                part = product[b * BLOCK : (b + 1) * BLOCK, :].astype(out.dtype)
                factor = spread[first + b : first + b + 1, cols].astype(out.dtype)
                held[(first + b) * BLOCK : (first + b + 1) * BLOCK, cols] = part * factor
        for b in range(first, first + pair):
            at = pl.ds(b * BLOCK, BLOCK)
            copies.append(pltpu.make_async_copy(held.at[at, :], out.at[at, :], sems.at[b]))
            copies[-1].start()
    for copy in copies:
        copy.wait()


def finish_kernel(n_parts, own, *refs):
    parts, out = refs[:n_parts], refs[-1]
    rows = own.shape[0]
    scales = []
    for part in parts:
        code = part[rows:, :].astype(jnp.int32).astype(jnp.float32)
        scales.append(jnp.exp2(code * (1.0 / STEPS)) * (1.0 / CODE))
    for b in range(rows // BLOCK):
        at = slice(b * BLOCK, (b + 1) * BLOCK)
        total = own[at, :]
        for part, scale in zip(parts, scales, strict=True):
            got = part[at, :].astype(jnp.int32).astype(jnp.float32)
            total = total + got * scale[b : b + 1, :]
        out[:, at] = total.T.astype(out.dtype)


def in_vmem():
    return pl.BlockSpec(memory_space=pltpu.VMEM)


def in_smem():
    return pl.BlockSpec(memory_space=pltpu.SMEM)


def in_hbm():
    return pl.BlockSpec(memory_space=pl.ANY)


def params():
    return pltpu.CompilerParams(vmem_limit_bytes=VMEM_LIMIT)


def cost(flops, nbytes):
    return pl.CostEstimate(flops=flops, bytes_accessed=nbytes, transcendentals=0)


def per_device(n_rows, n_cols, grad_output, inputs, weight, block_mask):
    row, col = lax.axis_index("row"), lax.axis_index("col")
    hidden, width = weight.shape
    blocks = hidden // BLOCK
    n_pieces = 2 if blocks % 2 == 0 else 1
    piece = hidden // n_pieces
    n_parts = n_rows - 1
    tokens = inputs.shape[0]
    shard_rows = grad_output.shape[0]
    all_tokens = tokens * n_rows
    chunk = min(512, width)
    bf16 = jnp.bfloat16

    ring = chip_ring(n_cols)
    n_chips = len(ring)

    def send_ring(x, by):
        perm = []
        for p in range(n_chips):
            for core in range(2):
                q = (p + (by if core == 0 else -by)) % n_chips
                perm.append((ring[p] * 2 + core, ring[q] * 2 + core))
        return lax.ppermute(x, "col", perm)

    def send_core(x):
        return lax.ppermute(x, "col", [(c, c ^ 1) for c in range(n_cols)])

    def send_row(x, by):
        return lax.ppermute(x, "row", [(r, (r + by) % n_rows) for r in range(n_rows)])

    reach = [0]
    for j in range(1, n_chips // 2 + 1):
        reach += [j] if 2 * j == n_chips else [j, -j]
    steps = [(j, other) for j in reach for other in range(2)]
    table = []
    for c in range(n_cols):
        p, core = ring.index(c // 2), c % 2
        line = []
        for j, other in steps:
            of_core = core ^ other
            q = (p - j if of_core == 0 else p + j) % n_chips
            line.append(ring[q] * 2 + of_core)
        table.append(line)
    place = jnp.stack([row, col]).astype(jnp.int32)

    weight = pltpu.with_memory_space_constraint(weight, pltpu.HBM)
    block_mask = pltpu.with_memory_space_constraint(block_mask, pltpu.HBM)
    piece_blocks = piece // BLOCK
    early = max(1, piece_blocks * 3 // 7)
    kept_early, spread = pl.pallas_call(
        spread_and_keep_kernel,
        in_specs=[in_smem(), in_hbm(), in_hbm()],
        out_specs=[in_vmem()] * 2,
        out_shape=[
            pltpu.VMEM((early * BLOCK, width), bf16),
            pltpu.VMEM((blocks, width), jnp.float32),
        ],
        scratch_shapes=[
            pltpu.VMEM(block_mask.shape, jnp.int32),
            pltpu.SemaphoreType.DMA,
            pltpu.SemaphoreType.DMA((early,)),
        ],
        compiler_params=params(),
        cost_estimate=cost(early * BLOCK * width, 2 * early * BLOCK * width),
        name="spread_and_keep",
    )(place, weight, block_mask)

    held = {0: grad_output}
    for j in (2, -2):
        if abs(j) < n_chips // 2 or j == n_chips // 2:
            held[j] = send_ring(grad_output, j)
    far = [j for j in held if j]
    spread, again = lax.optimization_barrier((spread, grad_output))
    held[1], held[-1] = send_ring(again, 1), send_ring(again, -1)
    acts = [inputs] + [send_row(inputs, k) for k in range(1, n_rows)]

    kepts = [kept_early]
    if early < piece_blocks:
        late = piece_blocks - early
        kept_late = pl.pallas_call(
            functools.partial(keep_kernel, early),
            in_specs=[in_vmem(), in_hbm()],
            out_specs=in_vmem(),
            out_shape=pltpu.VMEM((late * BLOCK, width), bf16),
            scratch_shapes=[pltpu.SemaphoreType.DMA((late,))],
            compiler_params=params(),
            cost_estimate=cost(late * BLOCK * width, 2 * late * BLOCK * width),
            name="keep",
        )(spread, weight)
        kepts.append(kept_late)
    kepts[-1], *ready = lax.optimization_barrier((kepts[-1], *(held[j] for j in far)))
    held.update(zip(far, ready, strict=True))
    for j in range(3, n_chips // 2 + 1):
        by = 1 if j % 2 else 2
        held[j] = send_ring(held[j - by], by)
        if 2 * j < n_chips:
            held[-j] = send_ring(held[by - j], -by)

    *acts, held[1], held[-1] = lax.optimization_barrier((*acts, held[1], held[-1]))
    later = n_pieces - 1
    acts_turned, *rest = pl.pallas_call(
        functools.partial(turn_kernel, n_rows, piece_blocks),
        in_specs=[in_vmem()] * n_rows + [in_hbm()],
        out_specs=[in_vmem()] * (1 + later),
        out_shape=[jax.ShapeDtypeStruct((hidden, all_tokens), bf16)]
        + [pltpu.VMEM((piece, width), bf16)] * later,
        scratch_shapes=[pltpu.SemaphoreType.DMA((piece_blocks,))] * later,
        compiler_params=params(),
        cost_estimate=cost(all_tokens * hidden, 4 * all_tokens * hidden),
        name="turn",
    )(*acts, weight)
    first = [j for j in reach if abs(j) == 1]
    last = [j for j in reach if abs(j) > 2]
    acts_turned, *ready = lax.optimization_barrier(
        (acts_turned, *(send_core(held[j]) for j in first), *(held[j] for j in last))
    )
    across = dict(zip(first, ready[: len(first)], strict=True))
    ready = ready[len(first) :]
    held.update(zip(last, ready, strict=True))
    shards = []
    for j in reach:
        shards += [held[j], across[j] if j in across else send_core(held[j])]

    n_shards = len(shards)
    code_rows = -(-(piece // BLOCK) // 16) * 16
    sent_shape = jax.ShapeDtypeStruct((piece + code_rows, tokens), jnp.int16)
    own_shape = jax.ShapeDtypeStruct((piece, tokens), jnp.float32)
    small_cost = cost(piece * width, piece * width // 8)
    full, turned, own, *coded = pl.pallas_call(
        functools.partial(
            first_terms_kernel, n_shards, len(kepts), n_parts, tokens // shard_rows, chunk
        ),
        in_specs=[in_smem()] * 2 + [in_vmem()] * (n_shards + len(kepts)),
        out_specs=[in_vmem()] * (3 + n_parts),
        out_shape=[
            jax.ShapeDtypeStruct((all_tokens, width), bf16),
            jax.ShapeDtypeStruct((width, all_tokens), bf16),
            own_shape,
        ]
        + [sent_shape] * n_parts,
        scratch_shapes=[pltpu.VMEM((piece, all_tokens), jnp.float32)],
        compiler_params=params(),
        cost_estimate=small_cost,
        name="first_terms",
    )(place, jnp.array(table, jnp.int32), *shards, *kepts)
    owns = [own]
    parts = [send_row(coded[k], k + 1) for k in range(n_parts)]

    if n_pieces > 1:
        own, *coded = pl.pallas_call(
            functools.partial(more_terms_kernel, n_parts, piece_blocks, chunk),
            in_specs=[in_vmem()] * 3,
            out_specs=[in_vmem()] * (1 + n_parts),
            out_shape=[own_shape] + [sent_shape] * n_parts,
            scratch_shapes=[pltpu.VMEM((piece, all_tokens), jnp.float32)],
            compiler_params=params(),
            cost_estimate=small_cost,
            name="more_terms",
        )(turned, rest[0], spread)
        owns.append(own)
        parts += [send_row(coded[k], k + 1) for k in range(n_parts)]

    grad_weight = pl.pallas_call(
        functools.partial(weight_grad_kernel, chunk),
        in_specs=[in_vmem()] * 3,
        out_specs=in_hbm(),
        out_shape=jax.ShapeDtypeStruct((hidden, width), bf16),
        scratch_shapes=[
            pltpu.VMEM((hidden, width), bf16),
            pltpu.SemaphoreType.DMA((blocks,)),
        ],
        compiler_params=params(),
        cost_estimate=small_cost,
        name="weight_grad",
    )(acts_turned, full, spread)

    grad_input = None
    for p in range(n_pieces):
        operands = [owns[p], *parts[p * n_parts : (p + 1) * n_parts]]
        specs = [in_vmem()] * len(operands)
        if p:
            operands.append(grad_input)
            specs.append(in_hbm())
        grad_input = pl.pallas_call(
            functools.partial(finish_kernel, n_parts),
            grid=(1,),
            in_specs=specs,
            out_specs=pl.BlockSpec((tokens, piece), lambda i, p=p: (0, p)),
            out_shape=jax.ShapeDtypeStruct((tokens, hidden), bf16),
            input_output_aliases={len(operands) - 1: 0} if p else {},
            compiler_params=params(),
            name="add_terms",
        )(*operands)
    return (grad_input, grad_weight)


def solution(mesh):
    return jax.shard_map(
        functools.partial(per_device, mesh.shape["row"], mesh.shape["col"]),
        mesh=mesh,
        in_specs=(P("col", "row"), P("row", "col"), P("col", "row"), P("col", None)),
        out_specs=(P("row", "col"), P("col", "row")),
        check_vma=False,
    )
```

```python
import functools

import jax
import jax.numpy as jnp
from jax import lax
from jax.experimental import pallas as pl
from jax.experimental.pallas import tpu as pltpu
from jax.sharding import PartitionSpec as P

BLOCK = 128
CODE = 32700.0
STEPS = 64.0
VMEM_LIMIT = 24 * 1024 * 1024


def chip_ring(cols):
    half, fast = cols // 2, 1
    while half % (fast * 2) == 0 and fast * 2 * fast * 2 <= half:
        fast *= 2
    slow = half // fast
    ring = []
    for s in range(slow):
        along = range(1, fast) if s % 2 == 0 else range(fast - 1, 0, -1)
        ring += [s * fast + f for f in along]
    ring += [s * fast for s in range(slow - 1, -1, -1)]
    return ring


def encode(part):
    top = jnp.max(jnp.abs(part), axis=0, keepdims=True)
    code = jnp.ceil(STEPS * jnp.log2(jnp.maximum(top, 1e-30)))
    scaled = part * (jnp.exp2(code * (-1.0 / STEPS)) * CODE)
    whole = jnp.clip(jnp.round(scaled), -32767.0, 32767.0)
    return whole.astype(jnp.int32), code.astype(jnp.int32)


def wide_mask(mask, first, width):
    cols = mask.shape[1]
    of_column = first + lax.broadcasted_iota(jnp.int32, (cols, width), 1) // BLOCK
    spread = of_column == lax.broadcasted_iota(jnp.int32, (cols, width), 0)
    return jnp.dot(
        mask.astype(jnp.float32).astype(jnp.bfloat16),
        spread.astype(jnp.float32).astype(jnp.bfloat16),
        preferred_element_type=jnp.float32,
    )


def spread_and_keep_kernel(place, weight, mask, kept, spread, mask_here, mask_sem, sems):
    rows, width = kept.shape
    mask_copy = pltpu.make_async_copy(mask, mask_here, mask_sem)
    mask_copy.start()
    fetch(weight, 0, kept, sems)
    mask_copy.wait()
    spread[...] = wide_mask(mask_here[...], place[0] * (width // BLOCK), width)
    drop_blocks(weight, 0, kept, spread, sems)


def keep_kernel(first, spread, weight, kept, sems):
    fetch(weight, first, kept, sems)
    drop_blocks(weight, first, kept, spread, sems)


def row_copy(weight, first, here, sems, block):
    to = pl.multiple_of(block * BLOCK, BLOCK)
    at = pl.multiple_of((first + block) * BLOCK, BLOCK)
    return pltpu.make_async_copy(
        weight.at[pl.ds(at, BLOCK), :], here.at[pl.ds(to, BLOCK), :], sems.at[block]
    )


def fetch(weight, first, here, sems):
    blocks = here.shape[0] // BLOCK
    lax.fori_loop(0, blocks, lambda b, _: (row_copy(weight, first, here, sems, b).start(), 0)[1], 0)


def fetched(weight, first, here, sems):
    blocks = here.shape[0] // BLOCK
    lax.fori_loop(0, blocks, lambda b, _: (row_copy(weight, first, here, sems, b).wait(), 0)[1], 0)


def drop_blocks(weight, first, kept, spread, sems):
    def one(b, _):
        row_copy(weight, first, kept, sems, b).wait()
        at = pl.ds(pl.multiple_of(b * BLOCK, BLOCK), BLOCK)
        kept[at, :] = kept[at, :] * spread[pl.ds(first + b, 1), :].astype(kept.dtype)
        return 0

    lax.fori_loop(0, kept.shape[0] // BLOCK, one, 0)


def turn_kernel(n_rows, first, *refs):
    acts, (weight, out, *rest) = refs[:n_rows], refs[n_rows:]
    if rest:
        fetch(weight, first, *rest)
    tokens, hidden = acts[0].shape
    for k in range(n_rows):
        place = (n_rows - k) % n_rows
        for c in range(0, hidden, BLOCK):
            out[c : c + BLOCK, place * tokens : (place + 1) * tokens] = acts[k][:, c : c + BLOCK].T
    if rest:
        fetched(weight, first, *rest)


def store_terms(total, own, outs):
    rows, tokens = own.shape
    own[...] = total[:, :tokens]
    for k, out in enumerate(outs):
        of_code = lax.broadcasted_iota(jnp.int32, (out.shape[0] - rows, tokens), 0)
        codes = jnp.zeros(of_code.shape, jnp.int32)
        for b in range(rows // BLOCK):
            at = slice(b * BLOCK, (b + 1) * BLOCK)
            whole, code = encode(total[at, (k + 1) * tokens : (k + 2) * tokens])
            out[at, :] = whole.astype(jnp.int16)
            codes = jnp.where(of_code == b, code, codes)
        out[rows:, :] = codes.astype(jnp.int16)


def first_terms_kernel(n_shards, n_kept, n_parts, shift, chunk, place, table, *refs):
    shards, kepts = refs[:n_shards], refs[n_shards : n_shards + n_kept]
    full, turned, own, *outs, total = refs[n_shards + n_kept :]
    rows = shards[0].shape[0]
    n_cols = table.shape[0]
    for n, shard in enumerate(shards):
        to = lax.rem(table[place[1], n] + n_cols - place[0] * shift, n_cols)
        full[pl.ds(pl.multiple_of(to * rows, rows), rows), :] = shard[...]
    for c in range(0, full.shape[1], chunk):
        cols = slice(c, c + chunk)
        turned[cols, :] = full[:, cols].T
        at = 0
        for kept in kepts:
            to = slice(at, at + kept.shape[0])
            terms = jnp.dot(kept[:, cols], turned[cols, :], preferred_element_type=jnp.float32)
            total[to, :] = terms if c == 0 else total[to, :] + terms
            at += kept.shape[0]
    store_terms(total, own, outs)


def more_terms_kernel(n_parts, first, chunk, turned, weight, spread, own, *refs):
    outs, (total,) = refs[:n_parts], refs[n_parts:]
    blocks = own.shape[0] // BLOCK
    for c in range(0, weight.shape[1], chunk):
        cols = slice(c, c + chunk)
        factors = spread[first : first + blocks, cols].astype(jnp.bfloat16)
        kept = jnp.concatenate(
            [weight[b * BLOCK : (b + 1) * BLOCK, cols] * factors[b : b + 1, :] for b in range(blocks)],
            axis=0,
        )
        terms = jnp.dot(kept, turned[cols, :], preferred_element_type=jnp.float32)
        total[...] = terms if c == 0 else total[...] + terms
    store_terms(total, own, outs)


def weight_grad_kernel(begin, chunk, acts, full, spread, *refs):
    out, held, sems = refs[-3:]
    blocks = held.shape[0] // BLOCK
    pair = 2 if blocks % 2 == 0 else 1
    copies = []
    for first in range(0, blocks, pair):
        left = acts[(begin + first) * BLOCK : (begin + first + pair) * BLOCK, :]
        for c in range(0, held.shape[1], chunk):
            cols = slice(c, c + chunk)
            product = jnp.dot(left, full[:, cols], preferred_element_type=jnp.float32)
            for b in range(pair):
                part = product[b * BLOCK : (b + 1) * BLOCK, :].astype(out.dtype)
                block = begin + first + b
                factor = spread[block : block + 1, cols].astype(out.dtype)
                held[(first + b) * BLOCK : (first + b + 1) * BLOCK, cols] = part * factor
        for b in range(first, first + pair):
            here, there = pl.ds(b * BLOCK, BLOCK), pl.ds((begin + b) * BLOCK, BLOCK)
            copies.append(pltpu.make_async_copy(held.at[here, :], out.at[there, :], sems.at[b]))
            copies[-1].start()
    for copy in copies:
        copy.wait()


def finish_kernel(first, n_parts, own, *refs):
    parts, (*_, out, held, sem) = refs[:n_parts], refs[n_parts:]
    rows = own.shape[0]
    scales = []
    for part in parts:
        code = part[rows:, :].astype(jnp.int32).astype(jnp.float32)
        scales.append(jnp.exp2(code * (1.0 / STEPS)) * (1.0 / CODE))
    for b in range(rows // BLOCK):
        at = slice(b * BLOCK, (b + 1) * BLOCK)
        total = own[at, :]
        for part, scale in zip(parts, scales, strict=True):
            got = part[at, :].astype(jnp.int32).astype(jnp.float32)
            total = total + got * scale[b : b + 1, :]
        held[:, at] = total.T.astype(out.dtype)
    copy = pltpu.make_async_copy(held, out.at[:, pl.ds(first, rows)], sem)
    copy.start()
    copy.wait()


def in_vmem():
    return pl.BlockSpec(memory_space=pltpu.VMEM)


def in_smem():
    return pl.BlockSpec(memory_space=pltpu.SMEM)


def in_hbm():
    return pl.BlockSpec(memory_space=pl.ANY)


def params():
    return pltpu.CompilerParams(vmem_limit_bytes=VMEM_LIMIT)


def cost(flops, nbytes):
    return pl.CostEstimate(flops=flops, bytes_accessed=nbytes, transcendentals=0)


def per_device(n_rows, n_cols, grad_output, inputs, weight, block_mask):
    row, col = lax.axis_index("row"), lax.axis_index("col")
    hidden, width = weight.shape
    blocks = hidden // BLOCK
    n_pieces = 2 if blocks > 7 else 1
    sizes = [hidden] if n_pieces == 1 else [(blocks + 1) // 2 * BLOCK, blocks // 2 * BLOCK]
    piece, rest_rows = sizes[0], sizes[-1]
    n_parts = n_rows - 1
    tokens = inputs.shape[0]
    shard_rows = grad_output.shape[0]
    all_tokens = tokens * n_rows
    chunk = min(512, width)
    bf16 = jnp.bfloat16

    ring = chip_ring(n_cols)
    n_chips = len(ring)

    def send_ring(x, by):
        perm = []
        for p in range(n_chips):
            for core in range(2):
                q = (p + (by if core == 0 else -by)) % n_chips
                perm.append((ring[p] * 2 + core, ring[q] * 2 + core))
        return lax.ppermute(x, "col", perm)

    def send_core(x):
        return lax.ppermute(x, "col", [(c, c ^ 1) for c in range(n_cols)])

    def send_row(x, by):
        return lax.ppermute(x, "row", [(r, (r + by) % n_rows) for r in range(n_rows)])

    reach = [0]
    for j in range(1, n_chips // 2 + 1):
        reach += [j] if 2 * j == n_chips else [j, -j]
    steps = [(j, other) for j in reach for other in range(2)]
    table = []
    for c in range(n_cols):
        p, core = ring.index(c // 2), c % 2
        line = []
        for j, other in steps:
            of_core = core ^ other
            q = (p - j if of_core == 0 else p + j) % n_chips
            line.append(ring[q] * 2 + of_core)
        table.append(line)
    place = jnp.stack([row, col]).astype(jnp.int32)

    weight = pltpu.with_memory_space_constraint(weight, pltpu.HBM)
    block_mask = pltpu.with_memory_space_constraint(block_mask, pltpu.HBM)
    piece_blocks = piece // BLOCK
    early = max(1, piece_blocks * 3 // 7)
    kept_early, spread = pl.pallas_call(
        spread_and_keep_kernel,
        in_specs=[in_smem(), in_hbm(), in_hbm()],
        out_specs=[in_vmem()] * 2,
        out_shape=[
            pltpu.VMEM((early * BLOCK, width), bf16),
            pltpu.VMEM((blocks, width), jnp.float32),
        ],
        scratch_shapes=[
            pltpu.VMEM(block_mask.shape, jnp.int32),
            pltpu.SemaphoreType.DMA,
            pltpu.SemaphoreType.DMA((early,)),
        ],
        compiler_params=params(),
        cost_estimate=cost(early * BLOCK * width, 2 * early * BLOCK * width),
        name="spread_and_keep",
    )(place, weight, block_mask)

    held = {0: grad_output}
    for j in (2, -2):
        if abs(j) < n_chips // 2 or j == n_chips // 2:
            held[j] = send_ring(grad_output, j)
    far = [j for j in held if j]
    spread, again = lax.optimization_barrier((spread, grad_output))
    held[1], held[-1] = send_ring(again, 1), send_ring(again, -1)
    acts = [inputs] + [send_row(inputs, k) for k in range(1, n_rows)]

    kepts = [kept_early]
    if early < piece_blocks:
        late = piece_blocks - early
        kept_late = pl.pallas_call(
            functools.partial(keep_kernel, early),
            in_specs=[in_vmem(), in_hbm()],
            out_specs=in_vmem(),
            out_shape=pltpu.VMEM((late * BLOCK, width), bf16),
            scratch_shapes=[pltpu.SemaphoreType.DMA((late,))],
            compiler_params=params(),
            cost_estimate=cost(late * BLOCK * width, 2 * late * BLOCK * width),
            name="keep",
        )(spread, weight)
        kepts.append(kept_late)
    kepts[-1], *ready = lax.optimization_barrier((kepts[-1], *(held[j] for j in far)))
    held.update(zip(far, ready, strict=True))
    for j in range(3, n_chips // 2 + 1):
        by = 1 if j % 2 else 2
        held[j] = send_ring(held[j - by], by)
        if 2 * j < n_chips:
            held[-j] = send_ring(held[by - j], -by)

    *acts, held[1], held[-1] = lax.optimization_barrier((*acts, held[1], held[-1]))
    later = n_pieces - 1
    acts_turned, *rest = pl.pallas_call(
        functools.partial(turn_kernel, n_rows, piece_blocks),
        in_specs=[in_vmem()] * n_rows + [in_hbm()],
        out_specs=[in_vmem()] * (1 + later),
        out_shape=[jax.ShapeDtypeStruct((hidden, all_tokens), bf16)]
        + [pltpu.VMEM((rest_rows, width), bf16)] * later,
        scratch_shapes=[pltpu.SemaphoreType.DMA((rest_rows // BLOCK,))] * later,
        compiler_params=params(),
        cost_estimate=cost(all_tokens * hidden, 4 * all_tokens * hidden),
        name="turn",
    )(*acts, weight)
    first = [j for j in reach if abs(j) == 1]
    last = [j for j in reach if abs(j) != 1]
    acts_turned, *ready = lax.optimization_barrier(
        (acts_turned, *(send_core(held[j]) for j in first), *(held[j] for j in last))
    )
    across = dict(zip(first, ready[: len(first)], strict=True))
    ready = ready[len(first) :]
    held.update(zip(last, ready, strict=True))
    shards = []
    for j in reach:
        shards += [held[j], across[j] if j in across else send_core(held[j])]

    n_shards = len(shards)
    def out_shapes(rows):
        code_rows = -(-(rows // BLOCK) // 16) * 16
        sent_shape = jax.ShapeDtypeStruct((rows + code_rows, tokens), jnp.int16)
        return [jax.ShapeDtypeStruct((rows, tokens), jnp.float32)] + [sent_shape] * n_parts

    small_cost = cost(piece * width, piece * width // 8)
    full, turned, own, *coded = pl.pallas_call(
        functools.partial(
            first_terms_kernel, n_shards, len(kepts), n_parts, tokens // shard_rows, chunk
        ),
        in_specs=[in_smem()] * 2 + [in_vmem()] * (n_shards + len(kepts)),
        out_specs=[in_vmem()] * (3 + n_parts),
        out_shape=[
            jax.ShapeDtypeStruct((all_tokens, width), bf16),
            jax.ShapeDtypeStruct((width, all_tokens), bf16),
        ]
        + out_shapes(piece),
        scratch_shapes=[pltpu.VMEM((piece, all_tokens), jnp.float32)],
        compiler_params=params(),
        cost_estimate=small_cost,
        name="first_terms",
    )(place, jnp.array(table, jnp.int32), *shards, *kepts)
    owns = [own]
    parts = [send_row(coded[k], k + 1) for k in range(n_parts)]

    if n_pieces > 1:
        own, *coded = pl.pallas_call(
            functools.partial(more_terms_kernel, n_parts, piece_blocks, chunk),
            in_specs=[in_vmem()] * 3,
            out_specs=[in_vmem()] * (1 + n_parts),
            out_shape=out_shapes(rest_rows),
            scratch_shapes=[pltpu.VMEM((rest_rows, all_tokens), jnp.float32)],
            compiler_params=params(),
            cost_estimate=small_cost,
            name="more_terms",
        )(turned, rest[0], spread)
        owns.append(own)
        parts += [send_row(coded[k], k + 1) for k in range(n_parts)]

    def weight_grad(begin, count, so_far):
        return pl.pallas_call(
            functools.partial(weight_grad_kernel, begin, chunk),
            in_specs=[in_vmem()] * 3 + [in_hbm()] * len(so_far),
            out_specs=in_hbm(),
            out_shape=jax.ShapeDtypeStruct((hidden, width), bf16),
            scratch_shapes=[
                pltpu.VMEM((count * BLOCK, width), bf16),
                pltpu.SemaphoreType.DMA((count,)),
            ],
            input_output_aliases={3: 0} if so_far else {},
            compiler_params=params(),
            cost_estimate=small_cost,
            name="weight_grad",
        )(acts_turned, full, spread, *so_far)

    def finish(p, so_far):
        operands = [owns[p], *parts[p * n_parts : (p + 1) * n_parts], *so_far]
        return pl.pallas_call(
            functools.partial(finish_kernel, sum(sizes[:p]), n_parts),
            in_specs=[in_vmem()] * (1 + n_parts) + [in_hbm()] * len(so_far),
            out_specs=in_hbm(),
            out_shape=jax.ShapeDtypeStruct((tokens, hidden), bf16),
            scratch_shapes=[pltpu.VMEM((tokens, sizes[p]), bf16), pltpu.SemaphoreType.DMA],
            input_output_aliases={1 + n_parts: 0} if so_far else {},
            compiler_params=params(),
            name="add_terms",
        )(*operands)

    grad_weight = weight_grad(0, blocks, ())
    grad_input = finish(0, ())
    for p in range(1, n_pieces):
        grad_input = finish(p, (grad_input,))
    return (grad_input, grad_weight)


def solution(mesh):
    return jax.shard_map(
        functools.partial(per_device, mesh.shape["row"], mesh.shape["col"]),
        mesh=mesh,
        in_specs=(P("col", "row"), P("row", "col"), P("col", "row"), P("col", None)),
        out_specs=(P("row", "col"), P("col", "row")),
        check_vma=False,
    )
```

```python
import functools

import jax
import jax.numpy as jnp
from jax import lax
from jax.experimental import pallas as pl
from jax.experimental.pallas import tpu as pltpu
from jax.sharding import PartitionSpec as P

BLOCK = 128
CODE = 32700.0
STEPS = 64.0
VMEM_LIMIT = 24 * 1024 * 1024


def chip_ring(cols):
    half, fast = cols // 2, 1
    while half % (fast * 2) == 0 and fast * 2 * fast * 2 <= half:
        fast *= 2
    slow = half // fast
    ring = []
    for s in range(slow):
        along = range(1, fast) if s % 2 == 0 else range(fast - 1, 0, -1)
        ring += [s * fast + f for f in along]
    ring += [s * fast for s in range(slow - 1, -1, -1)]
    return ring


def encode(part):
    top = jnp.max(jnp.abs(part), axis=0, keepdims=True)
    code = jnp.ceil(STEPS * jnp.log2(jnp.maximum(top, 1e-30)))
    scaled = part * (jnp.exp2(code * (-1.0 / STEPS)) * CODE)
    whole = jnp.clip(jnp.round(scaled), -32767.0, 32767.0)
    return whole.astype(jnp.int32), code.astype(jnp.int32)


def wide_mask(mask, first, width):
    cols = mask.shape[1]
    of_column = first + lax.broadcasted_iota(jnp.int32, (cols, width), 1) // BLOCK
    spread = of_column == lax.broadcasted_iota(jnp.int32, (cols, width), 0)
    return jnp.dot(
        mask.astype(jnp.float32).astype(jnp.bfloat16),
        spread.astype(jnp.float32).astype(jnp.bfloat16),
        preferred_element_type=jnp.float32,
    )


def spread_and_keep_kernel(place, weight, mask, kept, spread, mask_here, mask_sem, sems):
    rows, width = kept.shape
    mask_copy = pltpu.make_async_copy(mask, mask_here, mask_sem)
    mask_copy.start()
    fetch(weight, 0, kept, sems)
    mask_copy.wait()
    spread[...] = wide_mask(mask_here[...], place[0] * (width // BLOCK), width)
    drop_blocks(weight, 0, kept, spread, sems)


def keep_kernel(first, spread, weight, kept, sems):
    fetch(weight, first, kept, sems)
    drop_blocks(weight, first, kept, spread, sems)


def row_copy(weight, first, here, sems, block):
    to = pl.multiple_of(block * BLOCK, BLOCK)
    at = pl.multiple_of((first + block) * BLOCK, BLOCK)
    return pltpu.make_async_copy(
        weight.at[pl.ds(at, BLOCK), :], here.at[pl.ds(to, BLOCK), :], sems.at[block]
    )


def fetch(weight, first, here, sems):
    blocks = here.shape[0] // BLOCK
    lax.fori_loop(0, blocks, lambda b, _: (row_copy(weight, first, here, sems, b).start(), 0)[1], 0)


def fetched(weight, first, here, sems):
    blocks = here.shape[0] // BLOCK
    lax.fori_loop(0, blocks, lambda b, _: (row_copy(weight, first, here, sems, b).wait(), 0)[1], 0)


def drop_blocks(weight, first, kept, spread, sems):
    def one(b, _):
        row_copy(weight, first, kept, sems, b).wait()
        at = pl.ds(pl.multiple_of(b * BLOCK, BLOCK), BLOCK)
        kept[at, :] = kept[at, :] * spread[pl.ds(first + b, 1), :].astype(kept.dtype)
        return 0

    lax.fori_loop(0, kept.shape[0] // BLOCK, one, 0)


def turn_kernel(n_rows, *refs):
    acts, out = refs[:n_rows], refs[n_rows]
    tokens, hidden = acts[0].shape
    for k in range(n_rows):
        place = (n_rows - k) % n_rows
        for c in range(0, hidden, BLOCK):
            out[c : c + BLOCK, place * tokens : (place + 1) * tokens] = acts[k][:, c : c + BLOCK].T


def store_terms(total, own, outs):
    rows, tokens = own.shape
    own[...] = total[:, :tokens]
    for k, out in enumerate(outs):
        of_code = lax.broadcasted_iota(jnp.int32, (out.shape[0] - rows, tokens), 0)
        codes = jnp.zeros(of_code.shape, jnp.int32)
        for b in range(rows // BLOCK):
            at = slice(b * BLOCK, (b + 1) * BLOCK)
            whole, code = encode(total[at, (k + 1) * tokens : (k + 2) * tokens])
            out[at, :] = whole.astype(jnp.int16)
            codes = jnp.where(of_code == b, code, codes)
        out[rows:, :] = codes.astype(jnp.int16)


def fetch_kernel(first, weight, out, sems):
    fetch(weight, first, out, sems)
    fetched(weight, first, out, sems)


def first_terms_kernel(n_shards, n_kept, n_parts, shift, chunk, place, table, *refs):
    shards, kepts = refs[:n_shards], refs[n_shards : n_shards + n_kept]
    full, turned, own, *outs, total = refs[n_shards + n_kept :]
    rows = shards[0].shape[0]
    n_cols = table.shape[0]
    for n, shard in enumerate(shards):
        to = lax.rem(table[place[1], n] + n_cols - place[0] * shift, n_cols)
        full[pl.ds(pl.multiple_of(to * rows, rows), rows), :] = shard[...]
    for c in range(0, full.shape[1], chunk):
        cols = slice(c, c + chunk)
        turned[cols, :] = full[:, cols].T
        at = 0
        for kept in kepts:
            to = slice(at, at + kept.shape[0])
            terms = jnp.dot(kept[:, cols], turned[cols, :], preferred_element_type=jnp.float32)
            total[to, :] = terms if c == 0 else total[to, :] + terms
            at += kept.shape[0]
    store_terms(total, own, outs)


def more_terms_kernel(n_parts, first, chunk, turned, weight, spread, _, own, *refs):
    outs, (total,) = refs[:n_parts], refs[n_parts:]
    blocks = own.shape[0] // BLOCK
    for c in range(0, weight.shape[1], chunk):
        cols = slice(c, c + chunk)
        factors = spread[first : first + blocks, cols].astype(jnp.bfloat16)
        kept = jnp.concatenate(
            [weight[b * BLOCK : (b + 1) * BLOCK, cols] * factors[b : b + 1, :] for b in range(blocks)],
            axis=0,
        )
        terms = jnp.dot(kept, turned[cols, :], preferred_element_type=jnp.float32)
        total[...] = terms if c == 0 else total[...] + terms
    store_terms(total, own, outs)


def weight_grad_kernel(chunk, acts, full, spread, out, held, sems):
    hidden, width = out.shape
    blocks = hidden // BLOCK
    pair = 2 if blocks % 2 == 0 else 1
    copies = []
    for first in range(0, blocks, pair):
        left = acts[first * BLOCK : (first + pair) * BLOCK, :]
        for c in range(0, width, chunk):
            cols = slice(c, c + chunk)
            product = jnp.dot(left, full[:, cols], preferred_element_type=jnp.float32)
            for b in range(pair):
                part = product[b * BLOCK : (b + 1) * BLOCK, :].astype(out.dtype)
                factor = spread[first + b : first + b + 1, cols].astype(out.dtype)
                held[(first + b) * BLOCK : (first + b + 1) * BLOCK, cols] = part * factor
        for b in range(first, first + pair):
            at = pl.ds(b * BLOCK, BLOCK)
            copies.append(pltpu.make_async_copy(held.at[at, :], out.at[at, :], sems.at[b]))
            copies[-1].start()
    for copy in copies:
        copy.wait()


def finish_kernel(n_parts, own, *refs):
    parts, out = refs[:n_parts], refs[-1]
    rows = own.shape[0]
    scales = []
    for part in parts:
        code = part[rows:, :].astype(jnp.int32).astype(jnp.float32)
        scales.append(jnp.exp2(code * (1.0 / STEPS)) * (1.0 / CODE))
    for b in range(rows // BLOCK):
        at = slice(b * BLOCK, (b + 1) * BLOCK)
        total = own[at, :]
        for part, scale in zip(parts, scales, strict=True):
            got = part[at, :].astype(jnp.int32).astype(jnp.float32)
            total = total + got * scale[b : b + 1, :]
        out[:, at] = total.T.astype(out.dtype)


def in_vmem():
    return pl.BlockSpec(memory_space=pltpu.VMEM)


def in_smem():
    return pl.BlockSpec(memory_space=pltpu.SMEM)


def in_hbm():
    return pl.BlockSpec(memory_space=pl.ANY)


def params():
    return pltpu.CompilerParams(vmem_limit_bytes=VMEM_LIMIT)


def cost(flops, nbytes):
    return pl.CostEstimate(flops=flops, bytes_accessed=nbytes, transcendentals=0)


def per_device(n_rows, n_cols, grad_output, inputs, weight, block_mask):
    row, col = lax.axis_index("row"), lax.axis_index("col")
    hidden, width = weight.shape
    blocks = hidden // BLOCK
    n_pieces = 2 if blocks % 2 == 0 else 1
    piece = hidden // n_pieces
    n_parts = n_rows - 1
    tokens = inputs.shape[0]
    shard_rows = grad_output.shape[0]
    all_tokens = tokens * n_rows
    chunk = min(512, width)
    bf16 = jnp.bfloat16

    ring = chip_ring(n_cols)
    n_chips = len(ring)

    def send_ring(x, by):
        perm = []
        for p in range(n_chips):
            for core in range(2):
                q = (p + (by if core == 0 else -by)) % n_chips
                perm.append((ring[p] * 2 + core, ring[q] * 2 + core))
        return lax.ppermute(x, "col", perm)

    def send_core(x):
        return lax.ppermute(x, "col", [(c, c ^ 1) for c in range(n_cols)])

    def send_row(x, by):
        return lax.ppermute(x, "row", [(r, (r + by) % n_rows) for r in range(n_rows)])

    reach = [0]
    for j in range(1, n_chips // 2 + 1):
        reach += [j] if 2 * j == n_chips else [j, -j]
    steps = [(j, other) for j in reach for other in range(2)]
    table = []
    for c in range(n_cols):
        p, core = ring.index(c // 2), c % 2
        line = []
        for j, other in steps:
            of_core = core ^ other
            q = (p - j if of_core == 0 else p + j) % n_chips
            line.append(ring[q] * 2 + of_core)
        table.append(line)
    place = jnp.stack([row, col]).astype(jnp.int32)

    weight = pltpu.with_memory_space_constraint(weight, pltpu.HBM)
    block_mask = pltpu.with_memory_space_constraint(block_mask, pltpu.HBM)
    piece_blocks = piece // BLOCK
    early = max(1, piece_blocks * 3 // 7)
    kept_early, spread = pl.pallas_call(
        spread_and_keep_kernel,
        in_specs=[in_smem(), in_hbm(), in_hbm()],
        out_specs=[in_vmem()] * 2,
        out_shape=[
            pltpu.VMEM((early * BLOCK, width), bf16),
            pltpu.VMEM((blocks, width), jnp.float32),
        ],
        scratch_shapes=[
            pltpu.VMEM(block_mask.shape, jnp.int32),
            pltpu.SemaphoreType.DMA,
            pltpu.SemaphoreType.DMA((early,)),
        ],
        compiler_params=params(),
        cost_estimate=cost(early * BLOCK * width, 2 * early * BLOCK * width),
        name="spread_and_keep",
    )(place, weight, block_mask)

    held = {0: grad_output}
    for j in (2, -2):
        if abs(j) < n_chips // 2 or j == n_chips // 2:
            held[j] = send_ring(grad_output, j)
    far = [j for j in held if j]
    spread, again = lax.optimization_barrier((spread, grad_output))
    held[1], held[-1] = send_ring(again, 1), send_ring(again, -1)
    kepts = [kept_early]
    if early < piece_blocks:
        late = piece_blocks - early
        kept_late = pl.pallas_call(
            functools.partial(keep_kernel, early),
            in_specs=[in_vmem(), in_hbm()],
            out_specs=in_vmem(),
            out_shape=pltpu.VMEM((late * BLOCK, width), bf16),
            scratch_shapes=[pltpu.SemaphoreType.DMA((late,))],
            compiler_params=params(),
            cost_estimate=cost(late * BLOCK * width, 2 * late * BLOCK * width),
            name="keep",
        )(spread, weight)
        kepts.append(kept_late)
    kepts[-1], inputs, *ready = lax.optimization_barrier(
        (kepts[-1], inputs, *(held[j] for j in far))
    )
    held.update(zip(far, ready, strict=True))
    acts = [inputs] + [send_row(inputs, k) for k in range(1, n_rows)]
    for j in range(3, n_chips // 2 + 1):
        by = 1 if j % 2 else 2
        held[j] = send_ring(held[j - by], by)
        if 2 * j < n_chips:
            held[-j] = send_ring(held[by - j], -by)

    if n_pieces > 1:
        weight, held[1], held[-1] = lax.optimization_barrier((weight, held[1], held[-1]))
        rest = pl.pallas_call(
            functools.partial(fetch_kernel, piece_blocks),
            in_specs=[in_hbm()],
            out_specs=in_vmem(),
            out_shape=pltpu.VMEM((piece, width), bf16),
            scratch_shapes=[pltpu.SemaphoreType.DMA((piece_blocks,))],
            compiler_params=params(),
            cost_estimate=cost(1 << 34, 2 * piece * width),
            name="fetch",
        )(weight)
        first = [j for j in reach if abs(j) < 3 or j == 3]
        rest, *ready = lax.optimization_barrier((rest, *(held[j] for j in first)))
        held.update(zip(first, ready, strict=True))
    shards = []
    for j in reach:
        shards += [held[j], send_core(held[j])]
    acts_turned = pl.pallas_call(
        functools.partial(turn_kernel, n_rows),
        in_specs=[in_vmem()] * n_rows,
        out_specs=in_vmem(),
        out_shape=jax.ShapeDtypeStruct((hidden, all_tokens), bf16),
        compiler_params=params(),
        cost_estimate=cost(all_tokens * hidden, 4 * all_tokens * hidden),
        name="turn",
    )(*acts)

    n_shards = len(shards)
    code_rows = -(-(piece // BLOCK) // 16) * 16
    sent_shape = jax.ShapeDtypeStruct((piece + code_rows, tokens), jnp.int16)
    own_shape = jax.ShapeDtypeStruct((piece, tokens), jnp.float32)
    small_cost = cost(piece * width, piece * width // 8)
    full, turned, own, *coded = pl.pallas_call(
        functools.partial(
            first_terms_kernel, n_shards, len(kepts), n_parts, tokens // shard_rows, chunk
        ),
        in_specs=[in_smem()] * 2 + [in_vmem()] * (n_shards + len(kepts)),
        out_specs=[in_vmem()] * (3 + n_parts),
        out_shape=[
            jax.ShapeDtypeStruct((all_tokens, width), bf16),
            jax.ShapeDtypeStruct((width, all_tokens), bf16),
            own_shape,
        ]
        + [sent_shape] * n_parts,
        scratch_shapes=[pltpu.VMEM((piece, all_tokens), jnp.float32)],
        compiler_params=params(),
        cost_estimate=small_cost,
        name="first_terms",
    )(place, jnp.array(table, jnp.int32), *shards, *kepts)
    owns = [own]
    parts = [send_row(coded[k], k + 1) for k in range(n_parts)]

    if n_pieces > 1:
        own, *coded = pl.pallas_call(
            functools.partial(more_terms_kernel, n_parts, piece_blocks, chunk),
            in_specs=[in_vmem()] * 3 + [in_hbm()],
            out_specs=[in_vmem()] * (1 + n_parts),
            out_shape=[own_shape] + [sent_shape] * n_parts,
            scratch_shapes=[pltpu.VMEM((piece, all_tokens), jnp.float32)],
            compiler_params=params(),
            cost_estimate=small_cost,
            name="more_terms",
        )(turned, rest, spread, acts_turned)
        owns.append(own)
        parts += [send_row(coded[k], k + 1) for k in range(n_parts)]

    grad_weight = pl.pallas_call(
        functools.partial(weight_grad_kernel, chunk),
        in_specs=[in_vmem()] * 3,
        out_specs=in_hbm(),
        out_shape=jax.ShapeDtypeStruct((hidden, width), bf16),
        scratch_shapes=[
            pltpu.VMEM((hidden, width), bf16),
            pltpu.SemaphoreType.DMA((blocks,)),
        ],
        compiler_params=params(),
        cost_estimate=small_cost,
        name="weight_grad",
    )(acts_turned, full, spread)

    grad_input = None
    for p in range(n_pieces):
        operands = [owns[p], *parts[p * n_parts : (p + 1) * n_parts]]
        specs = [in_vmem()] * len(operands)
        if p:
            operands.append(grad_input)
            specs.append(in_hbm())
        grad_input = pl.pallas_call(
            functools.partial(finish_kernel, n_parts),
            grid=(1,),
            in_specs=specs,
            out_specs=pl.BlockSpec((tokens, piece), lambda i, p=p: (0, p)),
            out_shape=jax.ShapeDtypeStruct((tokens, hidden), bf16),
            input_output_aliases={len(operands) - 1: 0} if p else {},
            compiler_params=params(),
            name="add_terms",
        )(*operands)
    return (grad_input, grad_weight)


def solution(mesh):
    return jax.shard_map(
        functools.partial(per_device, mesh.shape["row"], mesh.shape["col"]),
        mesh=mesh,
        in_specs=(P("col", "row"), P("row", "col"), P("col", "row"), P("col", None)),
        out_specs=(P("row", "col"), P("col", "row")),
        check_vma=False,
    )
```

```python
import functools

import jax
import jax.numpy as jnp
from jax import lax
from jax.experimental import pallas as pl
from jax.experimental.pallas import tpu as pltpu
from jax.sharding import PartitionSpec as P

BLOCK = 128
CODE = 32700.0
STEPS = 64.0
VMEM_LIMIT = 24 * 1024 * 1024


def chip_ring(cols):
    half, fast = cols // 2, 1
    while half % (fast * 2) == 0 and fast * 2 * fast * 2 <= half:
        fast *= 2
    slow = half // fast
    ring = []
    for s in range(slow):
        along = range(1, fast) if s % 2 == 0 else range(fast - 1, 0, -1)
        ring += [s * fast + f for f in along]
    ring += [s * fast for s in range(slow - 1, -1, -1)]
    return ring


def encode(part):
    top = jnp.max(jnp.abs(part), axis=0, keepdims=True)
    code = jnp.ceil(STEPS * jnp.log2(jnp.maximum(top, 1e-30)))
    scaled = part * (jnp.exp2(code * (-1.0 / STEPS)) * CODE)
    whole = jnp.clip(jnp.round(scaled), -32767.0, 32767.0)
    return whole.astype(jnp.int32), code.astype(jnp.int32)


def wide_mask(mask, first, width):
    cols = mask.shape[1]
    of_column = first + lax.broadcasted_iota(jnp.int32, (cols, width), 1) // BLOCK
    spread = of_column == lax.broadcasted_iota(jnp.int32, (cols, width), 0)
    return jnp.dot(
        mask.astype(jnp.float32).astype(jnp.bfloat16),
        spread.astype(jnp.float32).astype(jnp.bfloat16),
        preferred_element_type=jnp.float32,
    )


def spread_and_keep_kernel(place, weight, mask, kept, spread, mask_here, mask_sem, sems):
    rows, width = kept.shape
    mask_copy = pltpu.make_async_copy(mask, mask_here, mask_sem)
    mask_copy.start()
    fetch(weight, 0, kept, sems)
    mask_copy.wait()
    spread[...] = wide_mask(mask_here[...], place[0] * (width // BLOCK), width)
    drop_blocks(weight, 0, kept, spread, sems)


def keep_kernel(first, spread, weight, kept, sems):
    fetch(weight, first, kept, sems)
    drop_blocks(weight, first, kept, spread, sems)


def row_copy(weight, first, here, sems, block):
    to = pl.multiple_of(block * BLOCK, BLOCK)
    at = pl.multiple_of((first + block) * BLOCK, BLOCK)
    return pltpu.make_async_copy(
        weight.at[pl.ds(at, BLOCK), :], here.at[pl.ds(to, BLOCK), :], sems.at[block]
    )


def fetch(weight, first, here, sems):
    blocks = here.shape[0] // BLOCK
    lax.fori_loop(0, blocks, lambda b, _: (row_copy(weight, first, here, sems, b).start(), 0)[1], 0)


def fetched(weight, first, here, sems):
    blocks = here.shape[0] // BLOCK
    lax.fori_loop(0, blocks, lambda b, _: (row_copy(weight, first, here, sems, b).wait(), 0)[1], 0)


def drop_blocks(weight, first, kept, spread, sems):
    def one(b, _):
        row_copy(weight, first, kept, sems, b).wait()
        at = pl.ds(pl.multiple_of(b * BLOCK, BLOCK), BLOCK)
        kept[at, :] = kept[at, :] * spread[pl.ds(first + b, 1), :].astype(kept.dtype)
        return 0

    lax.fori_loop(0, kept.shape[0] // BLOCK, one, 0)


def pack_kernel(*refs):
    shards, out = refs[:-1], refs[-1]
    rows = shards[0].shape[0]
    for n, shard in enumerate(shards):
        out[n * rows : (n + 1) * rows, :] = shard[...]


def turn_kernel(*refs):
    acts, out = refs[:-1], refs[-1]
    tokens, hidden = acts[0].shape
    for k, act in enumerate(acts):
        place = (len(acts) - k) % len(acts)
        for c in range(0, hidden, BLOCK):
            out[c : c + BLOCK, place * tokens : (place + 1) * tokens] = act[:, c : c + BLOCK].T


def store_terms(total, own, outs):
    rows, tokens = own.shape
    own[...] = total[:, :tokens]
    for k, out in enumerate(outs):
        of_code = lax.broadcasted_iota(jnp.int32, (out.shape[0] - rows, tokens), 0)
        codes = jnp.zeros(of_code.shape, jnp.int32)
        for b in range(rows // BLOCK):
            at = slice(b * BLOCK, (b + 1) * BLOCK)
            whole, code = encode(total[at, (k + 1) * tokens : (k + 2) * tokens])
            out[at, :] = whole.astype(jnp.int16)
            codes = jnp.where(of_code == b, code, codes)
        out[rows:, :] = codes.astype(jnp.int16)


def fetch_kernel(first, weight, out, sems):
    fetch(weight, first, out, sems)
    fetched(weight, first, out, sems)


def first_terms_kernel(n_shards, n_kept, n_parts, shift, chunk, place, table, *refs):
    shards, kepts = refs[:n_shards], refs[n_shards : n_shards + n_kept]
    full, turned, own, *outs, total = refs[n_shards + n_kept :]
    rows = shards[0].shape[0]
    n_cols = table.shape[0]
    slots = [(shard, at) for shard in shards for at in range(0, shard.shape[0], rows)]
    for n, (shard, at) in enumerate(slots):
        to = lax.rem(table[place[1], n] + n_cols - place[0] * shift, n_cols)
        full[pl.ds(pl.multiple_of(to * rows, rows), rows), :] = shard[at : at + rows, :]
    for c in range(0, full.shape[1], chunk):
        cols = slice(c, c + chunk)
        turned[cols, :] = full[:, cols].T
        at = 0
        for kept in kepts:
            to = slice(at, at + kept.shape[0])
            terms = jnp.dot(kept[:, cols], turned[cols, :], preferred_element_type=jnp.float32)
            total[to, :] = terms if c == 0 else total[to, :] + terms
            at += kept.shape[0]
    store_terms(total, own, outs)


def more_terms_kernel(n_parts, first, chunk, turned, weight, spread, *refs):
    acts, (own, *outs, acts_turned, total) = refs[: n_parts + 1], refs[n_parts + 1 :]
    blocks = own.shape[0] // BLOCK
    for c in range(0, weight.shape[1], chunk):
        cols = slice(c, c + chunk)
        factors = spread[first : first + blocks, cols].astype(jnp.bfloat16)
        kept = jnp.concatenate(
            [weight[b * BLOCK : (b + 1) * BLOCK, cols] * factors[b : b + 1, :] for b in range(blocks)],
            axis=0,
        )
        terms = jnp.dot(kept, turned[cols, :], preferred_element_type=jnp.float32)
        total[...] = terms if c == 0 else total[...] + terms
    store_terms(total, own, outs)
    turn_kernel(*acts, acts_turned)


def weight_grad_kernel(chunk, acts, full, spread, out, held, sems):
    hidden, width = out.shape
    blocks = hidden // BLOCK
    pair = 2 if blocks % 2 == 0 else 1
    copies = []
    for first in range(0, blocks, pair):
        left = acts[first * BLOCK : (first + pair) * BLOCK, :]
        for c in range(0, width, chunk):
            cols = slice(c, c + chunk)
            product = jnp.dot(left, full[:, cols], preferred_element_type=jnp.float32)
            for b in range(pair):
                part = product[b * BLOCK : (b + 1) * BLOCK, :].astype(out.dtype)
                factor = spread[first + b : first + b + 1, cols].astype(out.dtype)
                held[(first + b) * BLOCK : (first + b + 1) * BLOCK, cols] = part * factor
        for b in range(first, first + pair):
            at = pl.ds(b * BLOCK, BLOCK)
            copies.append(pltpu.make_async_copy(held.at[at, :], out.at[at, :], sems.at[b]))
            copies[-1].start()
    for copy in copies:
        copy.wait()


def finish_kernel(n_parts, own, *refs):
    parts, out = refs[:n_parts], refs[-1]
    rows = own.shape[0]
    scales = []
    for part in parts:
        code = part[rows:, :].astype(jnp.int32).astype(jnp.float32)
        scales.append(jnp.exp2(code * (1.0 / STEPS)) * (1.0 / CODE))
    for b in range(rows // BLOCK):
        at = slice(b * BLOCK, (b + 1) * BLOCK)
        total = own[at, :]
        for part, scale in zip(parts, scales, strict=True):
            got = part[at, :].astype(jnp.int32).astype(jnp.float32)
            total = total + got * scale[b : b + 1, :]
        out[:, at] = total.T.astype(out.dtype)


def in_vmem():
    return pl.BlockSpec(memory_space=pltpu.VMEM)


def in_smem():
    return pl.BlockSpec(memory_space=pltpu.SMEM)


def in_hbm():
    return pl.BlockSpec(memory_space=pl.ANY)


def params():
    return pltpu.CompilerParams(vmem_limit_bytes=VMEM_LIMIT)


def cost(flops, nbytes):
    return pl.CostEstimate(flops=flops, bytes_accessed=nbytes, transcendentals=0)


def per_device(n_rows, n_cols, grad_output, inputs, weight, block_mask):
    row, col = lax.axis_index("row"), lax.axis_index("col")
    hidden, width = weight.shape
    blocks = hidden // BLOCK
    n_pieces = 2 if blocks % 2 == 0 else 1
    piece = hidden // n_pieces
    n_parts = n_rows - 1
    tokens = inputs.shape[0]
    shard_rows = grad_output.shape[0]
    all_tokens = tokens * n_rows
    chunk = min(512, width)
    bf16 = jnp.bfloat16

    ring = chip_ring(n_cols)
    n_chips = len(ring)

    def send_ring(x, by):
        perm = []
        for p in range(n_chips):
            for core in range(2):
                q = (p + (by if core == 0 else -by)) % n_chips
                perm.append((ring[p] * 2 + core, ring[q] * 2 + core))
        return lax.ppermute(x, "col", perm)

    def send_core(x):
        return lax.ppermute(x, "col", [(c, c ^ 1) for c in range(n_cols)])

    def send_row(x, by):
        return lax.ppermute(x, "row", [(r, (r + by) % n_rows) for r in range(n_rows)])

    reach = [0]
    for j in range(1, n_chips // 2 + 1):
        reach += [j] if 2 * j == n_chips else [j, -j]
    near = [j for j in reach if abs(j) < 3]
    last = [j for j in reach if abs(j) > 2]
    steps = [(j, other) for other in range(2) for j in near]
    steps += [(j, other) for j in last for other in range(2)]
    table = []
    for c in range(n_cols):
        p, core = ring.index(c // 2), c % 2
        line = []
        for j, other in steps:
            of_core = core ^ other
            q = (p - j if of_core == 0 else p + j) % n_chips
            line.append(ring[q] * 2 + of_core)
        table.append(line)
    place = jnp.stack([row, col]).astype(jnp.int32)

    weight = pltpu.with_memory_space_constraint(weight, pltpu.HBM)
    block_mask = pltpu.with_memory_space_constraint(block_mask, pltpu.HBM)
    piece_blocks = piece // BLOCK
    early = max(1, piece_blocks * 3 // 7)
    kept_early, spread = pl.pallas_call(
        spread_and_keep_kernel,
        in_specs=[in_smem(), in_hbm(), in_hbm()],
        out_specs=[in_vmem()] * 2,
        out_shape=[
            pltpu.VMEM((early * BLOCK, width), bf16),
            pltpu.VMEM((blocks, width), jnp.float32),
        ],
        scratch_shapes=[
            pltpu.VMEM(block_mask.shape, jnp.int32),
            pltpu.SemaphoreType.DMA,
            pltpu.SemaphoreType.DMA((early,)),
        ],
        compiler_params=params(),
        cost_estimate=cost(early * BLOCK * width, 2 * early * BLOCK * width),
        name="spread_and_keep",
    )(place, weight, block_mask)

    held = {0: grad_output}
    for j in (2, -2):
        if abs(j) < n_chips // 2 or j == n_chips // 2:
            held[j] = send_ring(grad_output, j)
    far = [j for j in held if j]
    spread, again = lax.optimization_barrier((spread, grad_output))
    held[1], held[-1] = send_ring(again, 1), send_ring(again, -1)
    kepts = [kept_early]
    if early < piece_blocks:
        late = piece_blocks - early
        kept_late = pl.pallas_call(
            functools.partial(keep_kernel, early),
            in_specs=[in_vmem(), in_hbm()],
            out_specs=in_vmem(),
            out_shape=pltpu.VMEM((late * BLOCK, width), bf16),
            scratch_shapes=[pltpu.SemaphoreType.DMA((late,))],
            compiler_params=params(),
            cost_estimate=cost(late * BLOCK * width, 2 * late * BLOCK * width),
            name="keep",
        )(spread, weight)
        kepts.append(kept_late)
    kepts[-1], inputs, *ready = lax.optimization_barrier(
        (kepts[-1], inputs, *(held[j] for j in far))
    )
    held.update(zip(far, ready, strict=True))
    acts = [inputs] + [send_row(inputs, k) for k in range(1, n_rows)]
    for j in range(3, n_chips // 2 + 1):
        by = 1 if j % 2 else 2
        held[j] = send_ring(held[j - by], by)
        if 2 * j < n_chips:
            held[-j] = send_ring(held[by - j], -by)

    if n_pieces > 1:
        weight, held[1], held[-1] = lax.optimization_barrier((weight, held[1], held[-1]))
        rest = pl.pallas_call(
            functools.partial(fetch_kernel, piece_blocks),
            in_specs=[in_hbm()],
            out_specs=in_vmem(),
            out_shape=pltpu.VMEM((piece, width), bf16),
            scratch_shapes=[pltpu.SemaphoreType.DMA((piece_blocks,))],
            compiler_params=params(),
            cost_estimate=cost(1 << 34, 2 * piece * width),
            name="fetch",
        )(weight)
        rest, *ready = lax.optimization_barrier((rest, *(held[j] for j in last)))
        held.update(zip(last, ready, strict=True))
    packed = pl.pallas_call(
        pack_kernel,
        in_specs=[in_vmem()] * len(near),
        out_specs=in_vmem(),
        out_shape=jax.ShapeDtypeStruct((len(near) * shard_rows, width), bf16),
        compiler_params=params(),
        name="pack",
    )(*(held[j] for j in near))
    shards = [held[j] for j in near] + [send_core(packed)]
    for j in last:
        shards += [held[j], send_core(held[j])]
    n_shards = len(shards)
    code_rows = -(-(piece // BLOCK) // 16) * 16
    sent_shape = jax.ShapeDtypeStruct((piece + code_rows, tokens), jnp.int16)
    own_shape = jax.ShapeDtypeStruct((piece, tokens), jnp.float32)
    small_cost = cost(piece * width, piece * width // 8)
    full, turned, own, *coded = pl.pallas_call(
        functools.partial(
            first_terms_kernel, n_shards, len(kepts), n_parts, tokens // shard_rows, chunk
        ),
        in_specs=[in_smem()] * 2 + [in_vmem()] * (n_shards + len(kepts)),
        out_specs=[in_vmem()] * (3 + n_parts),
        out_shape=[
            jax.ShapeDtypeStruct((all_tokens, width), bf16),
            jax.ShapeDtypeStruct((width, all_tokens), bf16),
            own_shape,
        ]
        + [sent_shape] * n_parts,
        scratch_shapes=[pltpu.VMEM((piece, all_tokens), jnp.float32)],
        compiler_params=params(),
        cost_estimate=small_cost,
        name="first_terms",
    )(place, jnp.array(table, jnp.int32), *shards, *kepts)
    owns = [own]
    parts = [send_row(coded[k], k + 1) for k in range(n_parts)]

    acts_shape = jax.ShapeDtypeStruct((hidden, all_tokens), bf16)
    if n_pieces > 1:
        own, *coded, acts_turned = pl.pallas_call(
            functools.partial(more_terms_kernel, n_parts, piece_blocks, chunk),
            in_specs=[in_vmem()] * (3 + n_rows),
            out_specs=[in_vmem()] * (2 + n_parts),
            out_shape=[own_shape] + [sent_shape] * n_parts + [acts_shape],
            scratch_shapes=[pltpu.VMEM((piece, all_tokens), jnp.float32)],
            compiler_params=params(),
            cost_estimate=small_cost,
            name="more_terms",
        )(turned, rest, spread, *acts)
        owns.append(own)
        parts += [send_row(coded[k], k + 1) for k in range(n_parts)]
    else:
        acts_turned = pl.pallas_call(
            turn_kernel,
            in_specs=[in_vmem()] * n_rows,
            out_specs=in_vmem(),
            out_shape=acts_shape,
            compiler_params=params(),
            name="turn",
        )(*acts)

    grad_weight = pl.pallas_call(
        functools.partial(weight_grad_kernel, chunk),
        in_specs=[in_vmem()] * 3,
        out_specs=in_hbm(),
        out_shape=jax.ShapeDtypeStruct((hidden, width), bf16),
        scratch_shapes=[
            pltpu.VMEM((hidden, width), bf16),
            pltpu.SemaphoreType.DMA((blocks,)),
        ],
        compiler_params=params(),
        cost_estimate=small_cost,
        name="weight_grad",
    )(acts_turned, full, spread)

    grad_input = None
    for p in range(n_pieces):
        operands = [owns[p], *parts[p * n_parts : (p + 1) * n_parts]]
        specs = [in_vmem()] * len(operands)
        if p:
            operands.append(grad_input)
            specs.append(in_hbm())
        grad_input = pl.pallas_call(
            functools.partial(finish_kernel, n_parts),
            grid=(1,),
            in_specs=specs,
            out_specs=pl.BlockSpec((tokens, piece), lambda i, p=p: (0, p)),
            out_shape=jax.ShapeDtypeStruct((tokens, hidden), bf16),
            input_output_aliases={len(operands) - 1: 0} if p else {},
            compiler_params=params(),
            name="add_terms",
        )(*operands)
    return (grad_input, grad_weight)


def solution(mesh):
    return jax.shard_map(
        functools.partial(per_device, mesh.shape["row"], mesh.shape["col"]),
        mesh=mesh,
        in_specs=(P("col", "row"), P("row", "col"), P("col", "row"), P("col", None)),
        out_specs=(P("row", "col"), P("col", "row")),
        check_vma=False,
    )
```

```python
import functools

import jax
import jax.numpy as jnp
from jax import lax
from jax.experimental import pallas as pl
from jax.experimental.pallas import tpu as pltpu
from jax.sharding import PartitionSpec as P

BLOCK = 128
CODE = 32700.0
STEPS = 64.0
VMEM_LIMIT = 24 * 1024 * 1024


def chip_ring(cols):
    half, fast = cols // 2, 1
    while half % (fast * 2) == 0 and fast * 2 * fast * 2 <= half:
        fast *= 2
    slow = half // fast
    ring = []
    for s in range(slow):
        along = range(1, fast) if s % 2 == 0 else range(fast - 1, 0, -1)
        ring += [s * fast + f for f in along]
    ring += [s * fast for s in range(slow - 1, -1, -1)]
    return ring


def encode(part):
    top = jnp.max(jnp.abs(part), axis=0, keepdims=True)
    code = jnp.ceil(STEPS * jnp.log2(jnp.maximum(top, 1e-30)))
    scaled = part * (jnp.exp2(code * (-1.0 / STEPS)) * CODE)
    whole = jnp.clip(jnp.round(scaled), -32767.0, 32767.0)
    return whole.astype(jnp.int32), code.astype(jnp.int32)


def wide_mask(mask, first, width):
    cols = mask.shape[1]
    of_column = first + lax.broadcasted_iota(jnp.int32, (cols, width), 1) // BLOCK
    spread = of_column == lax.broadcasted_iota(jnp.int32, (cols, width), 0)
    return jnp.dot(
        mask.astype(jnp.float32).astype(jnp.bfloat16),
        spread.astype(jnp.float32).astype(jnp.bfloat16),
        preferred_element_type=jnp.float32,
    )


def spread_and_keep_kernel(place, weight, mask, kept, spread, mask_here, mask_sem, sems):
    rows, width = kept.shape
    mask_copy = pltpu.make_async_copy(mask, mask_here, mask_sem)
    mask_copy.start()
    fetch(weight, 0, kept, sems)
    mask_copy.wait()
    spread[...] = wide_mask(mask_here[...], place[0] * (width // BLOCK), width)
    drop_blocks(weight, 0, kept, spread, sems)


def keep_kernel(first, spread, weight, kept, sems):
    fetch(weight, first, kept, sems)
    drop_blocks(weight, first, kept, spread, sems)


def row_copy(weight, first, here, sems, block):
    to = pl.multiple_of(block * BLOCK, BLOCK)
    at = pl.multiple_of((first + block) * BLOCK, BLOCK)
    return pltpu.make_async_copy(
        weight.at[pl.ds(at, BLOCK), :], here.at[pl.ds(to, BLOCK), :], sems.at[block]
    )


def fetch(weight, first, here, sems):
    blocks = here.shape[0] // BLOCK
    lax.fori_loop(0, blocks, lambda b, _: (row_copy(weight, first, here, sems, b).start(), 0)[1], 0)


def fetched(weight, first, here, sems):
    blocks = here.shape[0] // BLOCK
    lax.fori_loop(0, blocks, lambda b, _: (row_copy(weight, first, here, sems, b).wait(), 0)[1], 0)


def drop_blocks(weight, first, kept, spread, sems):
    def one(b, _):
        row_copy(weight, first, kept, sems, b).wait()
        at = pl.ds(pl.multiple_of(b * BLOCK, BLOCK), BLOCK)
        kept[at, :] = kept[at, :] * spread[pl.ds(first + b, 1), :].astype(kept.dtype)
        return 0

    lax.fori_loop(0, kept.shape[0] // BLOCK, one, 0)


def pack_kernel(*refs):
    shards, out = refs[:-1], refs[-1]
    rows = shards[0].shape[0]
    for n, shard in enumerate(shards):
        out[n * rows : (n + 1) * rows, :] = shard[...]


def turn_kernel(*refs):
    acts, out = refs[:-1], refs[-1]
    tokens, hidden = acts[0].shape
    for k, act in enumerate(acts):
        place = (len(acts) - k) % len(acts)
        for c in range(0, hidden, BLOCK):
            out[c : c + BLOCK, place * tokens : (place + 1) * tokens] = act[:, c : c + BLOCK].T


def store_terms(total, own, outs):
    rows, tokens = own.shape
    own[...] = total[:, :tokens]
    for k, out in enumerate(outs):
        of_code = lax.broadcasted_iota(jnp.int32, (out.shape[0] - rows, tokens), 0)
        codes = jnp.zeros(of_code.shape, jnp.int32)
        for b in range(rows // BLOCK):
            at = slice(b * BLOCK, (b + 1) * BLOCK)
            whole, code = encode(total[at, (k + 1) * tokens : (k + 2) * tokens])
            out[at, :] = whole.astype(jnp.int16)
            codes = jnp.where(of_code == b, code, codes)
        out[rows:, :] = codes.astype(jnp.int16)


def fetch_kernel(first, weight, out, sems):
    fetch(weight, first, out, sems)
    fetched(weight, first, out, sems)


def first_terms_kernel(n_shards, n_kept, n_parts, shift, chunk, place, table, *refs):
    shards, kepts = refs[:n_shards], refs[n_shards : n_shards + n_kept]
    full, turned, own, *outs, total = refs[n_shards + n_kept :]
    rows = shards[0].shape[0]
    n_cols = table.shape[0]
    slots = [(shard, at) for shard in shards for at in range(0, shard.shape[0], rows)]
    for n, (shard, at) in enumerate(slots):
        to = lax.rem(table[place[1], n] + n_cols - place[0] * shift, n_cols)
        full[pl.ds(pl.multiple_of(to * rows, rows), rows), :] = shard[at : at + rows, :]
    for c in range(0, full.shape[1], chunk):
        cols = slice(c, c + chunk)
        turned[cols, :] = full[:, cols].T
        at = 0
        for kept in kepts:
            to = slice(at, at + kept.shape[0])
            terms = jnp.dot(kept[:, cols], turned[cols, :], preferred_element_type=jnp.float32)
            total[to, :] = terms if c == 0 else total[to, :] + terms
            at += kept.shape[0]
    store_terms(total, own, outs)


def more_terms_kernel(n_parts, first, chunk, turned, weight, spread, *refs):
    acts, (own, *outs, acts_turned, total) = refs[: n_parts + 1], refs[n_parts + 1 :]
    blocks = own.shape[0] // BLOCK
    for c in range(0, weight.shape[1], chunk):
        cols = slice(c, c + chunk)
        factors = spread[first : first + blocks, cols].astype(jnp.bfloat16)
        kept = jnp.concatenate(
            [weight[b * BLOCK : (b + 1) * BLOCK, cols] * factors[b : b + 1, :] for b in range(blocks)],
            axis=0,
        )
        terms = jnp.dot(kept, turned[cols, :], preferred_element_type=jnp.float32)
        total[...] = terms if c == 0 else total[...] + terms
    store_terms(total, own, outs)
    turn_kernel(*acts, acts_turned)


def weight_grad_kernel(chunk, acts, full, spread, out, held, sems):
    hidden, width = out.shape
    blocks = hidden // BLOCK
    pair = 2 if blocks % 2 == 0 else 1
    copies = []
    for first in range(0, blocks, pair):
        left = acts[first * BLOCK : (first + pair) * BLOCK, :]
        for c in range(0, width, chunk):
            cols = slice(c, c + chunk)
            product = jnp.dot(left, full[:, cols], preferred_element_type=jnp.float32)
            for b in range(pair):
                part = product[b * BLOCK : (b + 1) * BLOCK, :].astype(out.dtype)
                factor = spread[first + b : first + b + 1, cols].astype(out.dtype)
                held[(first + b) * BLOCK : (first + b + 1) * BLOCK, cols] = part * factor
        for b in range(first, first + pair):
            at = pl.ds(b * BLOCK, BLOCK)
            copies.append(pltpu.make_async_copy(held.at[at, :], out.at[at, :], sems.at[b]))
            copies[-1].start()
    for copy in copies:
        copy.wait()


def finish_kernel(n_parts, own, *refs):
    parts, out = refs[:n_parts], refs[-1]
    rows = own.shape[0]
    scales = []
    for part in parts:
        code = part[rows:, :].astype(jnp.int32).astype(jnp.float32)
        scales.append(jnp.exp2(code * (1.0 / STEPS)) * (1.0 / CODE))
    for b in range(rows // BLOCK):
        at = slice(b * BLOCK, (b + 1) * BLOCK)
        total = own[at, :]
        for part, scale in zip(parts, scales, strict=True):
            got = part[at, :].astype(jnp.int32).astype(jnp.float32)
            total = total + got * scale[b : b + 1, :]
        out[:, at] = total.T.astype(out.dtype)


def in_vmem():
    return pl.BlockSpec(memory_space=pltpu.VMEM)


def in_smem():
    return pl.BlockSpec(memory_space=pltpu.SMEM)


def in_hbm():
    return pl.BlockSpec(memory_space=pl.ANY)


def params():
    return pltpu.CompilerParams(vmem_limit_bytes=VMEM_LIMIT)


def cost(flops, nbytes):
    return pl.CostEstimate(flops=flops, bytes_accessed=nbytes, transcendentals=0)


def per_device(n_rows, n_cols, grad_output, inputs, weight, block_mask):
    row, col = lax.axis_index("row"), lax.axis_index("col")
    hidden, width = weight.shape
    blocks = hidden // BLOCK
    n_pieces = 2 if blocks % 2 == 0 else 1
    piece = hidden // n_pieces
    n_parts = n_rows - 1
    tokens = inputs.shape[0]
    shard_rows = grad_output.shape[0]
    all_tokens = tokens * n_rows
    chunk = min(512, width)
    bf16 = jnp.bfloat16

    ring = chip_ring(n_cols)
    n_chips = len(ring)

    def send_ring(x, by):
        perm = []
        for p in range(n_chips):
            for core in range(2):
                q = (p + (by if core == 0 else -by)) % n_chips
                perm.append((ring[p] * 2 + core, ring[q] * 2 + core))
        return lax.ppermute(x, "col", perm)

    def send_core(x):
        return lax.ppermute(x, "col", [(c, c ^ 1) for c in range(n_cols)])

    def send_row(x, by):
        return lax.ppermute(x, "row", [(r, (r + by) % n_rows) for r in range(n_rows)])

    reach = [0]
    for j in range(1, n_chips // 2 + 1):
        reach += [j] if 2 * j == n_chips else [j, -j]
    near = [j for j in reach if abs(j) < 3]
    last = [j for j in reach if abs(j) > 2]
    steps = [(j, other) for other in range(2) for j in near]
    steps += [(j, other) for j in last for other in range(2)]
    table = []
    for c in range(n_cols):
        p, core = ring.index(c // 2), c % 2
        line = []
        for j, other in steps:
            of_core = core ^ other
            q = (p - j if of_core == 0 else p + j) % n_chips
            line.append(ring[q] * 2 + of_core)
        table.append(line)
    place = jnp.stack([row, col]).astype(jnp.int32)

    weight = pltpu.with_memory_space_constraint(weight, pltpu.HBM)
    block_mask = pltpu.with_memory_space_constraint(block_mask, pltpu.HBM)
    piece_blocks = piece // BLOCK
    early = max(1, piece_blocks * 3 // 7)
    kept_early, spread = pl.pallas_call(
        spread_and_keep_kernel,
        in_specs=[in_smem(), in_hbm(), in_hbm()],
        out_specs=[in_vmem()] * 2,
        out_shape=[
            pltpu.VMEM((early * BLOCK, width), bf16),
            pltpu.VMEM((blocks, width), jnp.float32),
        ],
        scratch_shapes=[
            pltpu.VMEM(block_mask.shape, jnp.int32),
            pltpu.SemaphoreType.DMA,
            pltpu.SemaphoreType.DMA((early,)),
        ],
        compiler_params=params(),
        cost_estimate=cost(1 << 34, BLOCK),
        name="spread_and_keep",
    )(place, weight, block_mask)

    held = {0: grad_output}
    for j in (2, -2):
        if abs(j) < n_chips // 2 or j == n_chips // 2:
            held[j] = send_ring(grad_output, j)
    far = [j for j in held if j]
    spread, again = lax.optimization_barrier((spread, grad_output))
    held[1], held[-1] = send_ring(again, 1), send_ring(again, -1)
    kepts = [kept_early]
    if early < piece_blocks:
        late = piece_blocks - early
        kept_late = pl.pallas_call(
            functools.partial(keep_kernel, early),
            in_specs=[in_vmem(), in_hbm()],
            out_specs=in_vmem(),
            out_shape=pltpu.VMEM((late * BLOCK, width), bf16),
            scratch_shapes=[pltpu.SemaphoreType.DMA((late,))],
            compiler_params=params(),
            cost_estimate=cost(BLOCK, BLOCK),
            name="keep",
        )(spread, weight)
        kepts.append(kept_late)
    kepts[-1], *ready = lax.optimization_barrier((kepts[-1], *(held[j] for j in far)))
    held.update(zip(far, ready, strict=True))
    acts = [inputs] + [send_row(inputs, k) for k in range(1, n_rows)]
    for j in range(3, n_chips // 2 + 1):
        by = 1 if j % 2 else 2
        held[j] = send_ring(held[j - by], by)
        if 2 * j < n_chips:
            held[-j] = send_ring(held[by - j], -by)

    if n_pieces > 1:
        weight, held[1], held[-1], *acts = lax.optimization_barrier(
            (weight, held[1], held[-1], *acts)
        )
        rest = pl.pallas_call(
            functools.partial(fetch_kernel, piece_blocks),
            in_specs=[in_hbm()],
            out_specs=in_vmem(),
            out_shape=pltpu.VMEM((piece, width), bf16),
            scratch_shapes=[pltpu.SemaphoreType.DMA((piece_blocks,))],
            compiler_params=params(),
            cost_estimate=cost(1 << 34, 2 * piece * width),
            name="fetch",
        )(weight)
        rest, *ready = lax.optimization_barrier((rest, *(held[j] for j in last)))
        held.update(zip(last, ready, strict=True))
    packed = pl.pallas_call(
        pack_kernel,
        in_specs=[in_vmem()] * len(near),
        out_specs=in_vmem(),
        out_shape=jax.ShapeDtypeStruct((len(near) * shard_rows, width), bf16),
        compiler_params=params(),
        name="pack",
    )(*(held[j] for j in near))
    shards = [held[j] for j in near] + [send_core(packed)]
    for j in last:
        shards += [held[j], send_core(held[j])]
    n_shards = len(shards)
    code_rows = -(-(piece // BLOCK) // 16) * 16
    sent_shape = jax.ShapeDtypeStruct((piece + code_rows, tokens), jnp.int16)
    own_shape = jax.ShapeDtypeStruct((piece, tokens), jnp.float32)
    small_cost = cost(piece * width, piece * width // 8)
    full, turned, own, *coded = pl.pallas_call(
        functools.partial(
            first_terms_kernel, n_shards, len(kepts), n_parts, tokens // shard_rows, chunk
        ),
        in_specs=[in_smem()] * 2 + [in_vmem()] * (n_shards + len(kepts)),
        out_specs=[in_vmem()] * (3 + n_parts),
        out_shape=[
            jax.ShapeDtypeStruct((all_tokens, width), bf16),
            jax.ShapeDtypeStruct((width, all_tokens), bf16),
            own_shape,
        ]
        + [sent_shape] * n_parts,
        scratch_shapes=[pltpu.VMEM((piece, all_tokens), jnp.float32)],
        compiler_params=params(),
        cost_estimate=small_cost,
        name="first_terms",
    )(place, jnp.array(table, jnp.int32), *shards, *kepts)
    owns = [own]
    parts = [send_row(coded[k], k + 1) for k in range(n_parts)]

    acts_shape = jax.ShapeDtypeStruct((hidden, all_tokens), bf16)
    if n_pieces > 1:
        own, *coded, acts_turned = pl.pallas_call(
            functools.partial(more_terms_kernel, n_parts, piece_blocks, chunk),
            in_specs=[in_vmem()] * (3 + n_rows),
            out_specs=[in_vmem()] * (2 + n_parts),
            out_shape=[own_shape] + [sent_shape] * n_parts + [acts_shape],
            scratch_shapes=[pltpu.VMEM((piece, all_tokens), jnp.float32)],
            compiler_params=params(),
            cost_estimate=small_cost,
            name="more_terms",
        )(turned, rest, spread, *acts)
        owns.append(own)
        parts += [send_row(coded[k], k + 1) for k in range(n_parts)]
    else:
        acts_turned = pl.pallas_call(
            turn_kernel,
            in_specs=[in_vmem()] * n_rows,
            out_specs=in_vmem(),
            out_shape=acts_shape,
            compiler_params=params(),
            name="turn",
        )(*acts)

    grad_weight = pl.pallas_call(
        functools.partial(weight_grad_kernel, chunk),
        in_specs=[in_vmem()] * 3,
        out_specs=in_hbm(),
        out_shape=jax.ShapeDtypeStruct((hidden, width), bf16),
        scratch_shapes=[
            pltpu.VMEM((hidden, width), bf16),
            pltpu.SemaphoreType.DMA((blocks,)),
        ],
        compiler_params=params(),
        cost_estimate=small_cost,
        name="weight_grad",
    )(acts_turned, full, spread)

    grad_input = None
    for p in range(n_pieces):
        operands = [owns[p], *parts[p * n_parts : (p + 1) * n_parts]]
        specs = [in_vmem()] * len(operands)
        if p:
            operands.append(grad_input)
            specs.append(in_hbm())
        grad_input = pl.pallas_call(
            functools.partial(finish_kernel, n_parts),
            grid=(1,),
            in_specs=specs,
            out_specs=pl.BlockSpec((tokens, piece), lambda i, p=p: (0, p)),
            out_shape=jax.ShapeDtypeStruct((tokens, hidden), bf16),
            input_output_aliases={len(operands) - 1: 0} if p else {},
            compiler_params=params(),
            name="add_terms",
        )(*operands)
    return (grad_input, grad_weight)


def solution(mesh):
    return jax.shard_map(
        functools.partial(per_device, mesh.shape["row"], mesh.shape["col"]),
        mesh=mesh,
        in_specs=(P("col", "row"), P("row", "col"), P("col", "row"), P("col", None)),
        out_specs=(P("row", "col"), P("col", "row")),
        check_vma=False,
    )
```

```python
import functools

import jax
import jax.numpy as jnp
from jax import lax
from jax.experimental import pallas as pl
from jax.experimental.pallas import tpu as pltpu
from jax.sharding import PartitionSpec as P

BLOCK = 128
CODE = 32700.0
STEPS = 64.0
VMEM_LIMIT = 24 * 1024 * 1024


def chip_ring(cols):
    half, fast = cols // 2, 1
    while half % (fast * 2) == 0 and fast * 2 * fast * 2 <= half:
        fast *= 2
    slow = half // fast
    ring = []
    for s in range(slow):
        along = range(1, fast) if s % 2 == 0 else range(fast - 1, 0, -1)
        ring += [s * fast + f for f in along]
    ring += [s * fast for s in range(slow - 1, -1, -1)]
    return ring


def encode(part):
    top = jnp.max(jnp.abs(part), axis=0, keepdims=True)
    code = jnp.ceil(STEPS * jnp.log2(jnp.maximum(top, 1e-30)))
    scaled = part * (jnp.exp2(code * (-1.0 / STEPS)) * CODE)
    whole = jnp.clip(jnp.round(scaled), -32767.0, 32767.0)
    return whole.astype(jnp.int32), code.astype(jnp.int32)


def wide_mask(mask, first, width):
    cols = mask.shape[1]
    of_column = first + lax.broadcasted_iota(jnp.int32, (cols, width), 1) // BLOCK
    spread = of_column == lax.broadcasted_iota(jnp.int32, (cols, width), 0)
    return jnp.dot(
        mask.astype(jnp.float32).astype(jnp.bfloat16),
        spread.astype(jnp.float32).astype(jnp.bfloat16),
        preferred_element_type=jnp.float32,
    )


def spread_kernel(place, mask, spread, mask_here, mask_sem):
    copy = pltpu.make_async_copy(mask, mask_here, mask_sem)
    copy.start()
    copy.wait()
    width = spread.shape[1]
    spread[...] = wide_mask(mask_here[...], place[0] * (width // BLOCK), width)


def row_copy(weight, first, here, sems, block):
    to = pl.multiple_of(block * BLOCK, BLOCK)
    at = pl.multiple_of((first + block) * BLOCK, BLOCK)
    return pltpu.make_async_copy(
        weight.at[pl.ds(at, BLOCK), :], here.at[pl.ds(to, BLOCK), :], sems.at[block]
    )


def fetch(weight, first, here, sems):
    blocks = here.shape[0] // BLOCK
    lax.fori_loop(0, blocks, lambda b, _: (row_copy(weight, first, here, sems, b).start(), 0)[1], 0)


def fetched(weight, first, here, sems):
    blocks = here.shape[0] // BLOCK
    lax.fori_loop(0, blocks, lambda b, _: (row_copy(weight, first, here, sems, b).wait(), 0)[1], 0)


def pack_kernel(*refs):
    shards, out = refs[:-1], refs[-1]
    rows = shards[0].shape[0]
    for n, shard in enumerate(shards):
        out[n * rows : (n + 1) * rows, :] = shard[...]


def turn_kernel(*refs):
    acts, out = refs[:-1], refs[-1]
    tokens, hidden = acts[0].shape
    for k, act in enumerate(acts):
        place = (len(acts) - k) % len(acts)
        for c in range(0, hidden, BLOCK):
            out[c : c + BLOCK, place * tokens : (place + 1) * tokens] = act[:, c : c + BLOCK].T


def store_terms(total, own, outs):
    rows, tokens = own.shape
    own[...] = total[:, :tokens]
    for k, out in enumerate(outs):
        of_code = lax.broadcasted_iota(jnp.int32, (out.shape[0] - rows, tokens), 0)
        codes = jnp.zeros(of_code.shape, jnp.int32)
        for b in range(rows // BLOCK):
            at = slice(b * BLOCK, (b + 1) * BLOCK)
            whole, code = encode(total[at, (k + 1) * tokens : (k + 2) * tokens])
            out[at, :] = whole.astype(jnp.int16)
            codes = jnp.where(of_code == b, code, codes)
        out[rows:, :] = codes.astype(jnp.int16)


def fetch_kernel(first, weight, out, sems):
    fetch(weight, first, out, sems)
    fetched(weight, first, out, sems)


def kept_blocks(pieces, spread, cols):
    kept = []
    for weight, first, end, row in pieces:
        factors = spread[row : row + end - first, cols].astype(jnp.bfloat16)
        for b in range(first, end):
            block = weight[b * BLOCK : (b + 1) * BLOCK, cols]
            kept.append(block * factors[b - first : b - first + 1, :])
    return jnp.concatenate(kept, axis=0)


def first_terms_kernel(n_shards, n_parts, shift, chunk, blocks, place, table, *refs):
    shards = refs[:n_shards]
    *weights, spread, full, turned, own = refs[n_shards : -n_parts - 1]
    outs, total = refs[-n_parts - 1 : -1], refs[-1]
    pieces, done = [], 0
    for weight in weights:
        end = min(weight.shape[0] // BLOCK, blocks - done)
        pieces.append((weight, 0, end, done))
        done += end
    rows = shards[0].shape[0]
    n_cols = table.shape[0]
    slots = [(shard, at) for shard in shards for at in range(0, shard.shape[0], rows)]
    for n, (shard, at) in enumerate(slots):
        to = lax.rem(table[place[1], n] + n_cols - place[0] * shift, n_cols)
        full[pl.ds(pl.multiple_of(to * rows, rows), rows), :] = shard[at : at + rows, :]
    for c in range(0, full.shape[1], chunk):
        cols = slice(c, c + chunk)
        turned[cols, :] = full[:, cols].T
        kept = kept_blocks(pieces, spread, cols)
        terms = jnp.dot(kept, turned[cols, :], preferred_element_type=jnp.float32)
        total[...] = terms if c == 0 else total[...] + terms
    store_terms(total, own, outs)


def more_terms_kernel(n_parts, first, chunk, turned, weight, spread, *refs):
    acts, (own, *outs, acts_turned, total) = refs[: n_parts + 1], refs[n_parts + 1 :]
    end = weight.shape[0] // BLOCK
    pieces = [(weight, end - own.shape[0] // BLOCK, end, first)]
    for c in range(0, weight.shape[1], chunk):
        cols = slice(c, c + chunk)
        kept = kept_blocks(pieces, spread, cols)
        terms = jnp.dot(kept, turned[cols, :], preferred_element_type=jnp.float32)
        total[...] = terms if c == 0 else total[...] + terms
    store_terms(total, own, outs)
    turn_kernel(*acts, acts_turned)


def weight_grad_kernel(chunk, acts, full, spread, out, held, sems):
    hidden, width = out.shape
    blocks = hidden // BLOCK
    pair = 2 if blocks % 2 == 0 else 1
    copies = []
    for first in range(0, blocks, pair):
        left = acts[first * BLOCK : (first + pair) * BLOCK, :]
        for c in range(0, width, chunk):
            cols = slice(c, c + chunk)
            product = jnp.dot(left, full[:, cols], preferred_element_type=jnp.float32)
            for b in range(pair):
                part = product[b * BLOCK : (b + 1) * BLOCK, :].astype(out.dtype)
                factor = spread[first + b : first + b + 1, cols].astype(out.dtype)
                held[(first + b) * BLOCK : (first + b + 1) * BLOCK, cols] = part * factor
        for b in range(first, first + pair):
            at = pl.ds(b * BLOCK, BLOCK)
            copies.append(pltpu.make_async_copy(held.at[at, :], out.at[at, :], sems.at[b]))
            copies[-1].start()
    for copy in copies:
        copy.wait()


def finish_kernel(n_parts, own, *refs):
    parts, out = refs[:n_parts], refs[-1]
    rows = own.shape[0]
    scales = []
    for part in parts:
        code = part[rows:, :].astype(jnp.int32).astype(jnp.float32)
        scales.append(jnp.exp2(code * (1.0 / STEPS)) * (1.0 / CODE))
    for b in range(rows // BLOCK):
        at = slice(b * BLOCK, (b + 1) * BLOCK)
        total = own[at, :]
        for part, scale in zip(parts, scales, strict=True):
            got = part[at, :].astype(jnp.int32).astype(jnp.float32)
            total = total + got * scale[b : b + 1, :]
        out[:, at] = total.T.astype(out.dtype)


def in_vmem():
    return pl.BlockSpec(memory_space=pltpu.VMEM)


def in_smem():
    return pl.BlockSpec(memory_space=pltpu.SMEM)


def in_hbm():
    return pl.BlockSpec(memory_space=pl.ANY)


def params():
    return pltpu.CompilerParams(vmem_limit_bytes=VMEM_LIMIT)


def cost(flops, nbytes):
    return pl.CostEstimate(flops=flops, bytes_accessed=nbytes, transcendentals=0)


def per_device(n_rows, n_cols, grad_output, inputs, weight, block_mask):
    row, col = lax.axis_index("row"), lax.axis_index("col")
    hidden, width = weight.shape
    blocks = hidden // BLOCK
    n_pieces = 2 if blocks % 2 == 0 else 1
    piece = hidden // n_pieces
    n_parts = n_rows - 1
    tokens = inputs.shape[0]
    shard_rows = grad_output.shape[0]
    all_tokens = tokens * n_rows
    chunk = min(512, width)
    bf16 = jnp.bfloat16

    ring = chip_ring(n_cols)
    n_chips = len(ring)

    def send_ring(x, by):
        perm = []
        for p in range(n_chips):
            for core in range(2):
                q = (p + (by if core == 0 else -by)) % n_chips
                perm.append((ring[p] * 2 + core, ring[q] * 2 + core))
        return lax.ppermute(x, "col", perm)

    def send_core(x):
        return lax.ppermute(x, "col", [(c, c ^ 1) for c in range(n_cols)])

    def send_row(x, by):
        return lax.ppermute(x, "row", [(r, (r + by) % n_rows) for r in range(n_rows)])

    reach = [0]
    for j in range(1, n_chips // 2 + 1):
        reach += [j] if 2 * j == n_chips else [j, -j]
    near = [j for j in reach if abs(j) < 3]
    last = [j for j in reach if abs(j) > 2]
    steps = [(j, other) for other in range(2) for j in near]
    steps += [(j, other) for j in last for other in range(2)]
    table = []
    for c in range(n_cols):
        p, core = ring.index(c // 2), c % 2
        line = []
        for j, other in steps:
            of_core = core ^ other
            q = (p - j if of_core == 0 else p + j) % n_chips
            line.append(ring[q] * 2 + of_core)
        table.append(line)
    place = jnp.stack([row, col]).astype(jnp.int32)

    weight = pltpu.with_memory_space_constraint(weight, pltpu.HBM)
    block_mask = pltpu.with_memory_space_constraint(block_mask, pltpu.HBM)
    piece_blocks = piece // BLOCK
    spread = pl.pallas_call(
        spread_kernel,
        in_specs=[in_smem(), in_hbm()],
        out_specs=in_vmem(),
        out_shape=pltpu.VMEM((blocks, width), jnp.float32),
        scratch_shapes=[pltpu.VMEM(block_mask.shape, jnp.int32), pltpu.SemaphoreType.DMA],
        compiler_params=params(),
        cost_estimate=cost(1 << 34, BLOCK),
        name="spread",
    )(place, block_mask)

    def fetch_rows(first, count, flops):
        return pl.pallas_call(
            functools.partial(fetch_kernel, first),
            in_specs=[in_hbm()],
            out_specs=in_vmem(),
            out_shape=pltpu.VMEM((count * BLOCK, width), bf16),
            scratch_shapes=[pltpu.SemaphoreType.DMA((count,))],
            compiler_params=params(),
            cost_estimate=cost(flops, BLOCK),
            name="fetch",
        )(weight)

    held = {0: grad_output}
    for j in (2, -2):
        if abs(j) < n_chips // 2 or j == n_chips // 2:
            held[j] = send_ring(grad_output, j)
    far = [j for j in held if j]
    spread, again = lax.optimization_barrier((spread, grad_output))
    held[1], held[-1] = send_ring(again, 1), send_ring(again, -1)
    n_soon = max(1, blocks * 5 // 14)
    weight, spread = lax.optimization_barrier((weight, spread))
    soon = fetch_rows(0, n_soon, BLOCK)
    soon, *ready = lax.optimization_barrier((soon, *(held[j] for j in far)))
    held.update(zip(far, ready, strict=True))
    acts = [inputs] + [send_row(inputs, k) for k in range(1, n_rows)]
    for j in range(3, n_chips // 2 + 1):
        by = 1 if j % 2 else 2
        held[j] = send_ring(held[j - by], by)
        if 2 * j < n_chips:
            held[-j] = send_ring(held[by - j], -by)

    weight, held[1], held[-1], *acts = lax.optimization_barrier(
        (weight, held[1], held[-1], *acts)
    )
    rest = fetch_rows(n_soon, blocks - n_soon, 1 << 34)
    rest, *ready = lax.optimization_barrier((rest, *(held[j] for j in last)))
    held.update(zip(last, ready, strict=True))
    packed = pl.pallas_call(
        pack_kernel,
        in_specs=[in_vmem()] * len(near),
        out_specs=in_vmem(),
        out_shape=jax.ShapeDtypeStruct((len(near) * shard_rows, width), bf16),
        compiler_params=params(),
        name="pack",
    )(*(held[j] for j in near))
    shards = [held[j] for j in near] + [send_core(packed)]
    for j in last:
        shards += [held[j], send_core(held[j])]
    n_shards = len(shards)
    code_rows = -(-(piece // BLOCK) // 16) * 16
    sent_shape = jax.ShapeDtypeStruct((piece + code_rows, tokens), jnp.int16)
    own_shape = jax.ShapeDtypeStruct((piece, tokens), jnp.float32)
    small_cost = cost(piece * width, piece * width // 8)
    full, turned, own, *coded = pl.pallas_call(
        functools.partial(
            first_terms_kernel, n_shards, n_parts, tokens // shard_rows, chunk, piece_blocks
        ),
        in_specs=[in_smem()] * 2 + [in_vmem()] * (n_shards + 3),
        out_specs=[in_vmem()] * (3 + n_parts),
        out_shape=[
            jax.ShapeDtypeStruct((all_tokens, width), bf16),
            jax.ShapeDtypeStruct((width, all_tokens), bf16),
            own_shape,
        ]
        + [sent_shape] * n_parts,
        scratch_shapes=[pltpu.VMEM((piece, all_tokens), jnp.float32)],
        compiler_params=params(),
        cost_estimate=small_cost,
        name="first_terms",
    )(place, jnp.array(table, jnp.int32), *shards, soon, rest, spread)
    owns = [own]
    parts = [send_row(coded[k], k + 1) for k in range(n_parts)]

    acts_shape = jax.ShapeDtypeStruct((hidden, all_tokens), bf16)
    if n_pieces > 1:
        own, *coded, acts_turned = pl.pallas_call(
            functools.partial(more_terms_kernel, n_parts, piece_blocks, chunk),
            in_specs=[in_vmem()] * (3 + n_rows),
            out_specs=[in_vmem()] * (2 + n_parts),
            out_shape=[own_shape] + [sent_shape] * n_parts + [acts_shape],
            scratch_shapes=[pltpu.VMEM((piece, all_tokens), jnp.float32)],
            compiler_params=params(),
            cost_estimate=small_cost,
            name="more_terms",
        )(turned, rest, spread, *acts)
        owns.append(own)
        parts += [send_row(coded[k], k + 1) for k in range(n_parts)]
    else:
        acts_turned = pl.pallas_call(
            turn_kernel,
            in_specs=[in_vmem()] * n_rows,
            out_specs=in_vmem(),
            out_shape=acts_shape,
            compiler_params=params(),
            name="turn",
        )(*acts)

    grad_weight = pl.pallas_call(
        functools.partial(weight_grad_kernel, chunk),
        in_specs=[in_vmem()] * 3,
        out_specs=in_hbm(),
        out_shape=jax.ShapeDtypeStruct((hidden, width), bf16),
        scratch_shapes=[
            pltpu.VMEM((hidden, width), bf16),
            pltpu.SemaphoreType.DMA((blocks,)),
        ],
        compiler_params=params(),
        cost_estimate=small_cost,
        name="weight_grad",
    )(acts_turned, full, spread)

    grad_input = None
    for p in range(n_pieces):
        operands = [owns[p], *parts[p * n_parts : (p + 1) * n_parts]]
        specs = [in_vmem()] * len(operands)
        if p:
            operands.append(grad_input)
            specs.append(in_hbm())
        grad_input = pl.pallas_call(
            functools.partial(finish_kernel, n_parts),
            grid=(1,),
            in_specs=specs,
            out_specs=pl.BlockSpec((tokens, piece), lambda i, p=p: (0, p)),
            out_shape=jax.ShapeDtypeStruct((tokens, hidden), bf16),
            input_output_aliases={len(operands) - 1: 0} if p else {},
            compiler_params=params(),
            name="add_terms",
        )(*operands)
    return (grad_input, grad_weight)


def solution(mesh):
    return jax.shard_map(
        functools.partial(per_device, mesh.shape["row"], mesh.shape["col"]),
        mesh=mesh,
        in_specs=(P("col", "row"), P("row", "col"), P("col", "row"), P("col", None)),
        out_specs=(P("row", "col"), P("col", "row")),
        check_vma=False,
    )
```

```python
import functools

import jax
import jax.numpy as jnp
from jax import lax
from jax.experimental import pallas as pl
from jax.experimental.pallas import tpu as pltpu
from jax.sharding import PartitionSpec as P

BLOCK = 128
CODE = 32700.0
STEPS = 64.0
VMEM_LIMIT = 24 * 1024 * 1024


def chip_ring(cols):
    half, fast = cols // 2, 1
    while half % (fast * 2) == 0 and fast * 2 * fast * 2 <= half:
        fast *= 2
    slow = half // fast
    ring = []
    for s in range(slow):
        along = range(1, fast) if s % 2 == 0 else range(fast - 1, 0, -1)
        ring += [s * fast + f for f in along]
    ring += [s * fast for s in range(slow - 1, -1, -1)]
    return ring


def encode(part):
    top = jnp.max(jnp.abs(part), axis=0, keepdims=True)
    code = jnp.ceil(STEPS * jnp.log2(jnp.maximum(top, 1e-30)))
    scaled = part * (jnp.exp2(code * (-1.0 / STEPS)) * CODE)
    whole = jnp.clip(jnp.round(scaled), -32767.0, 32767.0)
    return whole.astype(jnp.int32), code.astype(jnp.int32)


def wide_mask(mask, first, width):
    cols = mask.shape[1]
    of_column = first + lax.broadcasted_iota(jnp.int32, (cols, width), 1) // BLOCK
    spread = of_column == lax.broadcasted_iota(jnp.int32, (cols, width), 0)
    return jnp.dot(
        mask.astype(jnp.float32).astype(jnp.bfloat16),
        spread.astype(jnp.float32).astype(jnp.bfloat16),
        preferred_element_type=jnp.float32,
    )


def spread_kernel(place, mask, spread, mask_here, mask_sem):
    copy = pltpu.make_async_copy(mask, mask_here, mask_sem)
    copy.start()
    copy.wait()
    width = spread.shape[1]
    spread[...] = wide_mask(mask_here[...], place[0] * (width // BLOCK), width)


def row_copy(weight, first, here, sems, block):
    to = pl.multiple_of(block * BLOCK, BLOCK)
    at = pl.multiple_of((first + block) * BLOCK, BLOCK)
    return pltpu.make_async_copy(
        weight.at[pl.ds(at, BLOCK), :], here.at[pl.ds(to, BLOCK), :], sems.at[block]
    )


def fetch(weight, first, here, sems):
    blocks = here.shape[0] // BLOCK
    lax.fori_loop(0, blocks, lambda b, _: (row_copy(weight, first, here, sems, b).start(), 0)[1], 0)


def fetched(weight, first, here, sems):
    blocks = here.shape[0] // BLOCK
    lax.fori_loop(0, blocks, lambda b, _: (row_copy(weight, first, here, sems, b).wait(), 0)[1], 0)


def pack_kernel(*refs):
    shards, out = refs[:-1], refs[-1]
    rows = shards[0].shape[0]
    for n, shard in enumerate(shards):
        out[n * rows : (n + 1) * rows, :] = shard[...]


def turn_kernel(*refs):
    acts, out = refs[:-1], refs[-1]
    tokens, hidden = acts[0].shape
    for k, act in enumerate(acts):
        place = (len(acts) - k) % len(acts)
        for c in range(0, hidden, BLOCK):
            out[c : c + BLOCK, place * tokens : (place + 1) * tokens] = act[:, c : c + BLOCK].T


def store_terms(total, own, outs):
    rows, tokens = own.shape
    own[...] = total[:, :tokens]
    for k, out in enumerate(outs):
        of_code = lax.broadcasted_iota(jnp.int32, (out.shape[0] - rows, tokens), 0)
        codes = jnp.zeros(of_code.shape, jnp.int32)
        for b in range(rows // BLOCK):
            at = slice(b * BLOCK, (b + 1) * BLOCK)
            whole, code = encode(total[at, (k + 1) * tokens : (k + 2) * tokens])
            out[at, :] = whole.astype(jnp.int16)
            codes = jnp.where(of_code == b, code, codes)
        out[rows:, :] = codes.astype(jnp.int16)


def fetch_kernel(first, weight, out, sems):
    fetch(weight, first, out, sems)
    fetched(weight, first, out, sems)


def kept_blocks(pieces, spread, cols):
    kept = []
    for weight, first, end, row in pieces:
        factors = spread[row : row + end - first, cols].astype(jnp.bfloat16)
        for b in range(first, end):
            block = weight[b * BLOCK : (b + 1) * BLOCK, cols]
            kept.append(block * factors[b - first : b - first + 1, :])
    return jnp.concatenate(kept, axis=0)


def first_terms_kernel(n_shards, n_parts, shift, chunk, blocks, place, table, *refs):
    shards = refs[:n_shards]
    *weights, spread, full, turned, own = refs[n_shards : -n_parts - 1]
    outs, total = refs[-n_parts - 1 : -1], refs[-1]
    pieces, done = [], 0
    for weight in weights:
        end = min(weight.shape[0] // BLOCK, blocks - done)
        if end:
            pieces.append((weight, 0, end, done))
        done += end
    rows = shards[0].shape[0]
    n_cols = table.shape[0]
    slots = [(shard, at) for shard in shards for at in range(0, shard.shape[0], rows)]
    for n, (shard, at) in enumerate(slots):
        to = lax.rem(table[place[1], n] + n_cols - place[0] * shift, n_cols)
        full[pl.ds(pl.multiple_of(to * rows, rows), rows), :] = shard[at : at + rows, :]
    for c in range(0, full.shape[1], chunk):
        cols = slice(c, c + chunk)
        turned[cols, :] = full[:, cols].T
        kept = kept_blocks(pieces, spread, cols)
        terms = jnp.dot(kept, turned[cols, :], preferred_element_type=jnp.float32)
        total[...] = terms if c == 0 else total[...] + terms
    store_terms(total, own, outs)


def more_terms_kernel(n_parts, first, chunk, turned, weight, spread, *refs):
    acts, (own, *outs, acts_turned, total) = refs[: n_parts + 1], refs[n_parts + 1 :]
    end = weight.shape[0] // BLOCK
    pieces = [(weight, end - own.shape[0] // BLOCK, end, first)]
    for c in range(0, weight.shape[1], chunk):
        cols = slice(c, c + chunk)
        kept = kept_blocks(pieces, spread, cols)
        terms = jnp.dot(kept, turned[cols, :], preferred_element_type=jnp.float32)
        total[...] = terms if c == 0 else total[...] + terms
    store_terms(total, own, outs)
    turn_kernel(*acts, acts_turned)


def weight_grad_kernel(chunk, acts, full, spread, out, held, sems):
    hidden, width = out.shape
    blocks = hidden // BLOCK
    pair = 2 if blocks % 2 == 0 else 1
    copies = []
    for first in range(0, blocks, pair):
        left = acts[first * BLOCK : (first + pair) * BLOCK, :]
        for c in range(0, width, chunk):
            cols = slice(c, c + chunk)
            product = jnp.dot(left, full[:, cols], preferred_element_type=jnp.float32)
            for b in range(pair):
                part = product[b * BLOCK : (b + 1) * BLOCK, :].astype(out.dtype)
                factor = spread[first + b : first + b + 1, cols].astype(out.dtype)
                held[(first + b) * BLOCK : (first + b + 1) * BLOCK, cols] = part * factor
        for b in range(first, first + pair):
            at = pl.ds(b * BLOCK, BLOCK)
            copies.append(pltpu.make_async_copy(held.at[at, :], out.at[at, :], sems.at[b]))
            copies[-1].start()
    for copy in copies:
        copy.wait()


def finish_kernel(n_parts, own, *refs):
    parts, out = refs[:n_parts], refs[-1]
    rows = own.shape[0]
    scales = []
    for part in parts:
        code = part[rows:, :].astype(jnp.int32).astype(jnp.float32)
        scales.append(jnp.exp2(code * (1.0 / STEPS)) * (1.0 / CODE))
    for b in range(rows // BLOCK):
        at = slice(b * BLOCK, (b + 1) * BLOCK)
        total = own[at, :]
        for part, scale in zip(parts, scales, strict=True):
            got = part[at, :].astype(jnp.int32).astype(jnp.float32)
            total = total + got * scale[b : b + 1, :]
        out[:, at] = total.T.astype(out.dtype)


def in_vmem():
    return pl.BlockSpec(memory_space=pltpu.VMEM)


def in_smem():
    return pl.BlockSpec(memory_space=pltpu.SMEM)


def in_hbm():
    return pl.BlockSpec(memory_space=pl.ANY)


def params():
    return pltpu.CompilerParams(vmem_limit_bytes=VMEM_LIMIT)


def cost(flops, nbytes):
    return pl.CostEstimate(flops=flops, bytes_accessed=nbytes, transcendentals=0)


def per_device(n_rows, n_cols, grad_output, inputs, weight, block_mask):
    row, col = lax.axis_index("row"), lax.axis_index("col")
    hidden, width = weight.shape
    blocks = hidden // BLOCK
    n_pieces = 2 if blocks % 2 == 0 else 1
    piece = hidden // n_pieces
    n_parts = n_rows - 1
    tokens = inputs.shape[0]
    shard_rows = grad_output.shape[0]
    all_tokens = tokens * n_rows
    chunk = min(512, width)
    bf16 = jnp.bfloat16

    ring = chip_ring(n_cols)
    n_chips = len(ring)

    def send_ring(x, by):
        perm = []
        for p in range(n_chips):
            for core in range(2):
                q = (p + (by if core == 0 else -by)) % n_chips
                perm.append((ring[p] * 2 + core, ring[q] * 2 + core))
        return lax.ppermute(x, "col", perm)

    def send_core(x):
        return lax.ppermute(x, "col", [(c, c ^ 1) for c in range(n_cols)])

    def send_row(x, by):
        return lax.ppermute(x, "row", [(r, (r + by) % n_rows) for r in range(n_rows)])

    reach = [0]
    for j in range(1, n_chips // 2 + 1):
        reach += [j] if 2 * j == n_chips else [j, -j]
    near = [j for j in reach if abs(j) < 3]
    last = [j for j in reach if abs(j) > 2]
    steps = [(j, other) for other in range(2) for j in near]
    steps += [(j, other) for j in last for other in range(2)]
    table = []
    for c in range(n_cols):
        p, core = ring.index(c // 2), c % 2
        line = []
        for j, other in steps:
            of_core = core ^ other
            q = (p - j if of_core == 0 else p + j) % n_chips
            line.append(ring[q] * 2 + of_core)
        table.append(line)
    place = jnp.stack([row, col]).astype(jnp.int32)

    weight = pltpu.with_memory_space_constraint(weight, pltpu.HBM)
    block_mask = pltpu.with_memory_space_constraint(block_mask, pltpu.HBM)
    piece_blocks = piece // BLOCK
    spread = pl.pallas_call(
        spread_kernel,
        in_specs=[in_smem(), in_hbm()],
        out_specs=in_vmem(),
        out_shape=pltpu.VMEM((blocks, width), jnp.float32),
        scratch_shapes=[pltpu.VMEM(block_mask.shape, jnp.int32), pltpu.SemaphoreType.DMA],
        compiler_params=params(),
        cost_estimate=cost(BLOCK, BLOCK),
        name="spread",
    )(place, block_mask)

    def fetch_rows(first, count, flops):
        return pl.pallas_call(
            functools.partial(fetch_kernel, first),
            in_specs=[in_hbm()],
            out_specs=in_vmem(),
            out_shape=pltpu.VMEM((count * BLOCK, width), bf16),
            scratch_shapes=[pltpu.SemaphoreType.DMA((count,))],
            compiler_params=params(),
            cost_estimate=cost(flops, BLOCK),
            name="fetch",
        )(weight)

    held = {0: grad_output}
    for j in (2, -2):
        if abs(j) < n_chips // 2 or j == n_chips // 2:
            held[j] = send_ring(grad_output, j)
    far = [j for j in held if j]
    spread, again = lax.optimization_barrier((spread, grad_output))
    held[1], held[-1] = send_ring(again, 1), send_ring(again, -1)
    n_soon = piece_blocks if n_pieces > 1 else max(1, blocks * 5 // 14)
    weight, spread = lax.optimization_barrier((weight, spread))
    soon = fetch_rows(0, n_soon, BLOCK)
    soon, inputs, *ready = lax.optimization_barrier((soon, inputs, *(held[j] for j in far)))
    held.update(zip(far, ready, strict=True))
    acts = [inputs] + [send_row(inputs, k) for k in range(1, n_rows)]
    for j in range(3, n_chips // 2 + 1):
        by = 1 if j % 2 else 2
        held[j] = send_ring(held[j - by], by)
        if 2 * j < n_chips:
            held[-j] = send_ring(held[by - j], -by)

    weight, held[1], held[-1] = lax.optimization_barrier((weight, held[1], held[-1]))
    rest = fetch_rows(n_soon, blocks - n_soon, 1 << 34)
    rest, *ready = lax.optimization_barrier((rest, *(held[j] for j in last)))
    held.update(zip(last, ready, strict=True))
    packed = pl.pallas_call(
        pack_kernel,
        in_specs=[in_vmem()] * len(near),
        out_specs=in_vmem(),
        out_shape=jax.ShapeDtypeStruct((len(near) * shard_rows, width), bf16),
        compiler_params=params(),
        name="pack",
    )(*(held[j] for j in near))
    shards = [held[j] for j in near] + [send_core(packed)]
    for j in last:
        shards += [held[j], send_core(held[j])]
    n_shards = len(shards)
    code_rows = -(-(piece // BLOCK) // 16) * 16
    sent_shape = jax.ShapeDtypeStruct((piece + code_rows, tokens), jnp.int16)
    own_shape = jax.ShapeDtypeStruct((piece, tokens), jnp.float32)
    small_cost = cost(piece * width, piece * width // 8)
    full, turned, own, *coded = pl.pallas_call(
        functools.partial(
            first_terms_kernel, n_shards, n_parts, tokens // shard_rows, chunk, piece_blocks
        ),
        in_specs=[in_smem()] * 2 + [in_vmem()] * (n_shards + 3),
        out_specs=[in_vmem()] * (3 + n_parts),
        out_shape=[
            jax.ShapeDtypeStruct((all_tokens, width), bf16),
            jax.ShapeDtypeStruct((width, all_tokens), bf16),
            own_shape,
        ]
        + [sent_shape] * n_parts,
        scratch_shapes=[pltpu.VMEM((piece, all_tokens), jnp.float32)],
        compiler_params=params(),
        cost_estimate=small_cost,
        name="first_terms",
    )(place, jnp.array(table, jnp.int32), *shards, soon, rest, spread)
    owns = [own]
    parts = [send_row(coded[k], k + 1) for k in range(n_parts)]

    acts_shape = jax.ShapeDtypeStruct((hidden, all_tokens), bf16)
    if n_pieces > 1:
        own, *coded, acts_turned = pl.pallas_call(
            functools.partial(more_terms_kernel, n_parts, piece_blocks, chunk),
            in_specs=[in_vmem()] * (3 + n_rows),
            out_specs=[in_vmem()] * (2 + n_parts),
            out_shape=[own_shape] + [sent_shape] * n_parts + [acts_shape],
            scratch_shapes=[pltpu.VMEM((piece, all_tokens), jnp.float32)],
            compiler_params=params(),
            cost_estimate=small_cost,
            name="more_terms",
        )(turned, rest, spread, *acts)
        owns.append(own)
        parts += [send_row(coded[k], k + 1) for k in range(n_parts)]
    else:
        acts_turned = pl.pallas_call(
            turn_kernel,
            in_specs=[in_vmem()] * n_rows,
            out_specs=in_vmem(),
            out_shape=acts_shape,
            compiler_params=params(),
            name="turn",
        )(*acts)

    grad_weight = pl.pallas_call(
        functools.partial(weight_grad_kernel, chunk),
        in_specs=[in_vmem()] * 3,
        out_specs=in_hbm(),
        out_shape=jax.ShapeDtypeStruct((hidden, width), bf16),
        scratch_shapes=[
            pltpu.VMEM((hidden, width), bf16),
            pltpu.SemaphoreType.DMA((blocks,)),
        ],
        compiler_params=params(),
        cost_estimate=small_cost,
        name="weight_grad",
    )(acts_turned, full, spread)

    grad_input = None
    for p in range(n_pieces):
        operands = [owns[p], *parts[p * n_parts : (p + 1) * n_parts]]
        specs = [in_vmem()] * len(operands)
        if p:
            operands.append(grad_input)
            specs.append(in_hbm())
        grad_input = pl.pallas_call(
            functools.partial(finish_kernel, n_parts),
            grid=(1,),
            in_specs=specs,
            out_specs=pl.BlockSpec((tokens, piece), lambda i, p=p: (0, p)),
            out_shape=jax.ShapeDtypeStruct((tokens, hidden), bf16),
            input_output_aliases={len(operands) - 1: 0} if p else {},
            compiler_params=params(),
            name="add_terms",
        )(*operands)
    return (grad_input, grad_weight)


def solution(mesh):
    return jax.shard_map(
        functools.partial(per_device, mesh.shape["row"], mesh.shape["col"]),
        mesh=mesh,
        in_specs=(P("col", "row"), P("row", "col"), P("col", "row"), P("col", None)),
        out_specs=(P("row", "col"), P("col", "row")),
        check_vma=False,
    )
```

```python
import functools

import jax
import jax.numpy as jnp
from jax import lax
from jax.experimental import pallas as pl
from jax.experimental.pallas import tpu as pltpu
from jax.sharding import PartitionSpec as P

BLOCK = 128
CODE = 32700.0
STEPS = 64.0
VMEM_LIMIT = 24 * 1024 * 1024


def chip_ring(cols):
    half, fast = cols // 2, 1
    while half % (fast * 2) == 0 and fast * 2 * fast * 2 <= half:
        fast *= 2
    slow = half // fast
    ring = []
    for s in range(slow):
        along = range(1, fast) if s % 2 == 0 else range(fast - 1, 0, -1)
        ring += [s * fast + f for f in along]
    ring += [s * fast for s in range(slow - 1, -1, -1)]
    return ring


def encode(part):
    top = jnp.max(jnp.abs(part), axis=0, keepdims=True)
    code = jnp.ceil(STEPS * jnp.log2(jnp.maximum(top, 1e-30)))
    scaled = part * (jnp.exp2(code * (-1.0 / STEPS)) * CODE)
    whole = jnp.clip(jnp.round(scaled), -32767.0, 32767.0)
    return whole.astype(jnp.int32), code.astype(jnp.int32)


def wide_mask(mask, first, width):
    cols = mask.shape[1]
    of_column = first + lax.broadcasted_iota(jnp.int32, (cols, width), 1) // BLOCK
    spread = of_column == lax.broadcasted_iota(jnp.int32, (cols, width), 0)
    return jnp.dot(
        mask.astype(jnp.float32).astype(jnp.bfloat16),
        spread.astype(jnp.float32).astype(jnp.bfloat16),
        preferred_element_type=jnp.float32,
    )


def spread_kernel(place, mask, spread, mask_here, mask_sem):
    copy = pltpu.make_async_copy(mask, mask_here, mask_sem)
    copy.start()
    copy.wait()
    width = spread.shape[1]
    spread[...] = wide_mask(mask_here[...], place[0] * (width // BLOCK), width)


def row_copy(weight, first, here, sems, block):
    to = pl.multiple_of(block * BLOCK, BLOCK)
    at = pl.multiple_of((first + block) * BLOCK, BLOCK)
    return pltpu.make_async_copy(
        weight.at[pl.ds(at, BLOCK), :], here.at[pl.ds(to, BLOCK), :], sems.at[block]
    )


def fetch(weight, first, here, sems):
    blocks = here.shape[0] // BLOCK
    lax.fori_loop(0, blocks, lambda b, _: (row_copy(weight, first, here, sems, b).start(), 0)[1], 0)


def fetched(weight, first, here, sems):
    blocks = here.shape[0] // BLOCK
    lax.fori_loop(0, blocks, lambda b, _: (row_copy(weight, first, here, sems, b).wait(), 0)[1], 0)


def pack_kernel(*refs):
    shards, out = refs[:-1], refs[-1]
    rows = shards[0].shape[0]
    for n, shard in enumerate(shards):
        out[n * rows : (n + 1) * rows, :] = shard[...]


def turn_kernel(*refs):
    acts, out = refs[:-1], refs[-1]
    tokens, hidden = acts[0].shape
    for k, act in enumerate(acts):
        place = (len(acts) - k) % len(acts)
        for c in range(0, hidden, BLOCK):
            out[c : c + BLOCK, place * tokens : (place + 1) * tokens] = act[:, c : c + BLOCK].T


def store_terms(total, own, outs):
    rows, tokens = own.shape
    own[...] = total[:, :tokens]
    for k, out in enumerate(outs):
        of_code = lax.broadcasted_iota(jnp.int32, (out.shape[0] - rows, tokens), 0)
        codes = jnp.zeros(of_code.shape, jnp.int32)
        for b in range(rows // BLOCK):
            at = slice(b * BLOCK, (b + 1) * BLOCK)
            whole, code = encode(total[at, (k + 1) * tokens : (k + 2) * tokens])
            out[at, :] = whole.astype(jnp.int16)
            codes = jnp.where(of_code == b, code, codes)
        out[rows:, :] = codes.astype(jnp.int16)


def fetch_kernel(first, weight, out, sems):
    fetch(weight, first, out, sems)
    fetched(weight, first, out, sems)


def kept_blocks(pieces, spread, cols):
    kept = []
    for weight, first, end, row in pieces:
        factors = spread[row : row + end - first, cols].astype(jnp.bfloat16)
        for b in range(first, end):
            block = weight[b * BLOCK : (b + 1) * BLOCK, cols]
            kept.append(block * factors[b - first : b - first + 1, :])
    return jnp.concatenate(kept, axis=0)


def first_terms_kernel(n_shards, n_parts, shift, chunk, blocks, place, table, *refs):
    shards = refs[:n_shards]
    *weights, spread, full, turned, own = refs[n_shards : -n_parts - 1]
    outs, total = refs[-n_parts - 1 : -1], refs[-1]
    pieces, done = [], 0
    for weight in weights:
        end = min(weight.shape[0] // BLOCK, blocks - done)
        pieces.append((weight, 0, end, done))
        done += end
    rows = shards[0].shape[0]
    n_cols = table.shape[0]
    slots = [(shard, at) for shard in shards for at in range(0, shard.shape[0], rows)]
    for n, (shard, at) in enumerate(slots):
        to = lax.rem(table[place[1], n] + n_cols - place[0] * shift, n_cols)
        full[pl.ds(pl.multiple_of(to * rows, rows), rows), :] = shard[at : at + rows, :]
    for c in range(0, full.shape[1], chunk):
        cols = slice(c, c + chunk)
        turned[cols, :] = full[:, cols].T
        kept = kept_blocks(pieces, spread, cols)
        terms = jnp.dot(kept, turned[cols, :], preferred_element_type=jnp.float32)
        total[...] = terms if c == 0 else total[...] + terms
    store_terms(total, own, outs)


def more_terms_kernel(n_parts, first, chunk, turned, weight, spread, *refs):
    acts, (own, *outs, acts_turned, total) = refs[: n_parts + 1], refs[n_parts + 1 :]
    end = weight.shape[0] // BLOCK
    pieces = [(weight, end - own.shape[0] // BLOCK, end, first)]
    for c in range(0, weight.shape[1], chunk):
        cols = slice(c, c + chunk)
        kept = kept_blocks(pieces, spread, cols)
        terms = jnp.dot(kept, turned[cols, :], preferred_element_type=jnp.float32)
        total[...] = terms if c == 0 else total[...] + terms
    store_terms(total, own, outs)
    turn_kernel(*acts, acts_turned)


def weight_grad_kernel(chunk, acts, full, spread, out, held, sems):
    hidden, width = out.shape
    blocks = hidden // BLOCK
    pair = 2 if blocks % 2 == 0 else 1
    copies = []
    for first in range(0, blocks, pair):
        left = acts[first * BLOCK : (first + pair) * BLOCK, :]
        for c in range(0, width, chunk):
            cols = slice(c, c + chunk)
            product = jnp.dot(left, full[:, cols], preferred_element_type=jnp.float32)
            for b in range(pair):
                part = product[b * BLOCK : (b + 1) * BLOCK, :].astype(out.dtype)
                factor = spread[first + b : first + b + 1, cols].astype(out.dtype)
                held[(first + b) * BLOCK : (first + b + 1) * BLOCK, cols] = part * factor
        for b in range(first, first + pair):
            at = pl.ds(b * BLOCK, BLOCK)
            copies.append(pltpu.make_async_copy(held.at[at, :], out.at[at, :], sems.at[b]))
            copies[-1].start()
    for copy in copies:
        copy.wait()


def finish_kernel(first, n_parts, own, *refs):
    parts, (*_, out, held, sem) = refs[:n_parts], refs[n_parts:]
    rows = own.shape[0]
    scales = []
    for part in parts:
        code = part[rows:, :].astype(jnp.int32).astype(jnp.float32)
        scales.append(jnp.exp2(code * (1.0 / STEPS)) * (1.0 / CODE))
    for b in range(rows // BLOCK):
        at = slice(b * BLOCK, (b + 1) * BLOCK)
        total = own[at, :]
        for part, scale in zip(parts, scales, strict=True):
            got = part[at, :].astype(jnp.int32).astype(jnp.float32)
            total = total + got * scale[b : b + 1, :]
        held[:, at] = total.T.astype(out.dtype)
    copy = pltpu.make_async_copy(held, out.at[:, pl.ds(first, rows)], sem)
    copy.start()
    copy.wait()


def in_vmem():
    return pl.BlockSpec(memory_space=pltpu.VMEM)


def in_smem():
    return pl.BlockSpec(memory_space=pltpu.SMEM)


def in_hbm():
    return pl.BlockSpec(memory_space=pl.ANY)


def params():
    return pltpu.CompilerParams(vmem_limit_bytes=VMEM_LIMIT)


def cost(flops, nbytes):
    return pl.CostEstimate(flops=flops, bytes_accessed=nbytes, transcendentals=0)


def per_device(n_rows, n_cols, grad_output, inputs, weight, block_mask):
    row, col = lax.axis_index("row"), lax.axis_index("col")
    hidden, width = weight.shape
    blocks = hidden // BLOCK
    n_pieces = 2 if blocks > 7 else 1
    piece = blocks * 5 // 14 * BLOCK if n_pieces > 1 else hidden
    sizes = [piece, hidden - piece][:n_pieces]
    n_parts = n_rows - 1
    tokens = inputs.shape[0]
    shard_rows = grad_output.shape[0]
    all_tokens = tokens * n_rows
    chunk = min(512, width)
    bf16 = jnp.bfloat16

    ring = chip_ring(n_cols)
    n_chips = len(ring)

    def send_ring(x, by):
        perm = []
        for p in range(n_chips):
            for core in range(2):
                q = (p + (by if core == 0 else -by)) % n_chips
                perm.append((ring[p] * 2 + core, ring[q] * 2 + core))
        return lax.ppermute(x, "col", perm)

    def send_core(x):
        return lax.ppermute(x, "col", [(c, c ^ 1) for c in range(n_cols)])

    def send_row(x, by):
        return lax.ppermute(x, "row", [(r, (r + by) % n_rows) for r in range(n_rows)])

    reach = [0]
    for j in range(1, n_chips // 2 + 1):
        reach += [j] if 2 * j == n_chips else [j, -j]
    near = [j for j in reach if abs(j) < 3]
    last = [j for j in reach if abs(j) > 2]
    steps = [(j, other) for other in range(2) for j in near]
    steps += [(j, other) for j in last for other in range(2)]
    table = []
    for c in range(n_cols):
        p, core = ring.index(c // 2), c % 2
        line = []
        for j, other in steps:
            of_core = core ^ other
            q = (p - j if of_core == 0 else p + j) % n_chips
            line.append(ring[q] * 2 + of_core)
        table.append(line)
    place = jnp.stack([row, col]).astype(jnp.int32)

    weight = pltpu.with_memory_space_constraint(weight, pltpu.HBM)
    block_mask = pltpu.with_memory_space_constraint(block_mask, pltpu.HBM)
    piece_blocks = piece // BLOCK
    spread = pl.pallas_call(
        spread_kernel,
        in_specs=[in_smem(), in_hbm()],
        out_specs=in_vmem(),
        out_shape=pltpu.VMEM((blocks, width), jnp.float32),
        scratch_shapes=[pltpu.VMEM(block_mask.shape, jnp.int32), pltpu.SemaphoreType.DMA],
        compiler_params=params(),
        cost_estimate=cost(1 << 34, BLOCK),
        name="spread",
    )(place, block_mask)

    def fetch_rows(first, count, flops):
        return pl.pallas_call(
            functools.partial(fetch_kernel, first),
            in_specs=[in_hbm()],
            out_specs=in_vmem(),
            out_shape=pltpu.VMEM((count * BLOCK, width), bf16),
            scratch_shapes=[pltpu.SemaphoreType.DMA((count,))],
            compiler_params=params(),
            cost_estimate=cost(flops, BLOCK),
            name="fetch",
        )(weight)

    held = {0: grad_output}
    for j in (2, -2):
        if abs(j) < n_chips // 2 or j == n_chips // 2:
            held[j] = send_ring(grad_output, j)
    far = [j for j in held if j]
    spread, again = lax.optimization_barrier((spread, grad_output))
    held[1], held[-1] = send_ring(again, 1), send_ring(again, -1)
    n_soon = max(1, blocks // 7)
    weight, spread = lax.optimization_barrier((weight, spread))
    soon = fetch_rows(0, n_soon, BLOCK)
    soon, *ready = lax.optimization_barrier((soon, *(held[j] for j in far)))
    held.update(zip(far, ready, strict=True))
    acts = [inputs] + [send_row(inputs, k) for k in range(1, n_rows)]
    for j in range(3, n_chips // 2 + 1):
        by = 1 if j % 2 else 2
        held[j] = send_ring(held[j - by], by)
        if 2 * j < n_chips:
            held[-j] = send_ring(held[by - j], -by)

    weight, held[1], held[-1], *acts = lax.optimization_barrier(
        (weight, held[1], held[-1], *acts)
    )
    rest = fetch_rows(n_soon, blocks - n_soon, 1 << 34)
    rest, *ready = lax.optimization_barrier((rest, *(held[j] for j in last)))
    held.update(zip(last, ready, strict=True))
    packed = pl.pallas_call(
        pack_kernel,
        in_specs=[in_vmem()] * len(near),
        out_specs=in_vmem(),
        out_shape=jax.ShapeDtypeStruct((len(near) * shard_rows, width), bf16),
        compiler_params=params(),
        name="pack",
    )(*(held[j] for j in near))
    shards = [held[j] for j in near] + [send_core(packed)]
    for j in last:
        shards += [held[j], send_core(held[j])]
    n_shards = len(shards)
    def out_shapes(rows):
        code_rows = -(-(rows // BLOCK) // 16) * 16
        sent_shape = jax.ShapeDtypeStruct((rows + code_rows, tokens), jnp.int16)
        return [jax.ShapeDtypeStruct((rows, tokens), jnp.float32)] + [sent_shape] * n_parts

    small_cost = cost(piece * width, piece * width // 8)
    full, turned, own, *coded = pl.pallas_call(
        functools.partial(
            first_terms_kernel, n_shards, n_parts, tokens // shard_rows, chunk, piece_blocks
        ),
        in_specs=[in_smem()] * 2 + [in_vmem()] * (n_shards + 3),
        out_specs=[in_vmem()] * (3 + n_parts),
        out_shape=[
            jax.ShapeDtypeStruct((all_tokens, width), bf16),
            jax.ShapeDtypeStruct((width, all_tokens), bf16),
        ]
        + out_shapes(piece),
        scratch_shapes=[pltpu.VMEM((piece, all_tokens), jnp.float32)],
        compiler_params=params(),
        cost_estimate=small_cost,
        name="first_terms",
    )(place, jnp.array(table, jnp.int32), *shards, soon, rest, spread)
    owns = [own]
    parts = [send_row(coded[k], k + 1) for k in range(n_parts)]

    acts_shape = jax.ShapeDtypeStruct((hidden, all_tokens), bf16)
    if n_pieces > 1:
        own, *coded, acts_turned = pl.pallas_call(
            functools.partial(more_terms_kernel, n_parts, piece_blocks, chunk),
            in_specs=[in_vmem()] * (3 + n_rows),
            out_specs=[in_vmem()] * (2 + n_parts),
            out_shape=out_shapes(sizes[1]) + [acts_shape],
            scratch_shapes=[pltpu.VMEM((sizes[1], all_tokens), jnp.float32)],
            compiler_params=params(),
            cost_estimate=small_cost,
            name="more_terms",
        )(turned, rest, spread, *acts)
        owns.append(own)
        parts += [send_row(coded[k], k + 1) for k in range(n_parts)]
    else:
        acts_turned = pl.pallas_call(
            turn_kernel,
            in_specs=[in_vmem()] * n_rows,
            out_specs=in_vmem(),
            out_shape=acts_shape,
            compiler_params=params(),
            name="turn",
        )(*acts)

    grad_weight = pl.pallas_call(
        functools.partial(weight_grad_kernel, chunk),
        in_specs=[in_vmem()] * 3,
        out_specs=in_hbm(),
        out_shape=jax.ShapeDtypeStruct((hidden, width), bf16),
        scratch_shapes=[
            pltpu.VMEM((hidden, width), bf16),
            pltpu.SemaphoreType.DMA((blocks,)),
        ],
        compiler_params=params(),
        cost_estimate=small_cost,
        name="weight_grad",
    )(acts_turned, full, spread)

    grad_input = None
    for p, rows in enumerate(sizes):
        operands = [owns[p], *parts[p * n_parts : (p + 1) * n_parts]]
        specs = [in_vmem()] * len(operands)
        if p:
            operands.append(grad_input)
            specs.append(in_hbm())
        grad_input = pl.pallas_call(
            functools.partial(finish_kernel, sum(sizes[:p]), n_parts),
            in_specs=specs,
            out_specs=in_hbm(),
            out_shape=jax.ShapeDtypeStruct((tokens, hidden), bf16),
            scratch_shapes=[pltpu.VMEM((tokens, rows), bf16), pltpu.SemaphoreType.DMA],
            input_output_aliases={len(operands) - 1: 0} if p else {},
            compiler_params=params(),
            cost_estimate=cost(BLOCK if p else 1 << 34, BLOCK),
            name="add_terms",
        )(*operands)
    return (grad_input, grad_weight)


def solution(mesh):
    return jax.shard_map(
        functools.partial(per_device, mesh.shape["row"], mesh.shape["col"]),
        mesh=mesh,
        in_specs=(P("col", "row"), P("row", "col"), P("col", "row"), P("col", None)),
        out_specs=(P("row", "col"), P("col", "row")),
        check_vma=False,
    )
```

```python
import functools

import jax
import jax.numpy as jnp
from jax import lax
from jax.experimental import pallas as pl
from jax.experimental.pallas import tpu as pltpu
from jax.sharding import PartitionSpec as P

BLOCK = 128
CODE = 32700.0
STEPS = 64.0
VMEM_LIMIT = 24 * 1024 * 1024


def chip_ring(cols):
    half, fast = cols // 2, 1
    while half % (fast * 2) == 0 and fast * 2 * fast * 2 <= half:
        fast *= 2
    slow = half // fast
    ring = []
    for s in range(slow):
        along = range(1, fast) if s % 2 == 0 else range(fast - 1, 0, -1)
        ring += [s * fast + f for f in along]
    ring += [s * fast for s in range(slow - 1, -1, -1)]
    return ring


def encode(part):
    top = jnp.max(jnp.abs(part), axis=0, keepdims=True)
    code = jnp.ceil(STEPS * jnp.log2(jnp.maximum(top, 1e-30)))
    scaled = part * (jnp.exp2(code * (-1.0 / STEPS)) * CODE)
    whole = jnp.clip(jnp.round(scaled), -32767.0, 32767.0)
    return whole.astype(jnp.int32), code.astype(jnp.int32)


def wide_mask(mask, first, width):
    cols = mask.shape[1]
    of_column = first + lax.broadcasted_iota(jnp.int32, (cols, width), 1) // BLOCK
    spread = of_column == lax.broadcasted_iota(jnp.int32, (cols, width), 0)
    return jnp.dot(
        mask.astype(jnp.float32).astype(jnp.bfloat16),
        spread.astype(jnp.float32).astype(jnp.bfloat16),
        preferred_element_type=jnp.float32,
    )


def spread_kernel(place, mask, spread, mask_here, mask_sem):
    copy = pltpu.make_async_copy(mask, mask_here, mask_sem)
    copy.start()
    copy.wait()
    width = spread.shape[1]
    spread[...] = wide_mask(mask_here[...], place[0] * (width // BLOCK), width)


def row_copy(weight, first, here, sems, block):
    to = pl.multiple_of(block * BLOCK, BLOCK)
    at = pl.multiple_of((first + block) * BLOCK, BLOCK)
    return pltpu.make_async_copy(
        weight.at[pl.ds(at, BLOCK), :], here.at[pl.ds(to, BLOCK), :], sems.at[block]
    )


def fetch(weight, first, here, sems):
    blocks = here.shape[0] // BLOCK
    lax.fori_loop(0, blocks, lambda b, _: (row_copy(weight, first, here, sems, b).start(), 0)[1], 0)


def fetched(weight, first, here, sems):
    blocks = here.shape[0] // BLOCK
    lax.fori_loop(0, blocks, lambda b, _: (row_copy(weight, first, here, sems, b).wait(), 0)[1], 0)


def pack_kernel(*refs):
    shards, out = refs[:-1], refs[-1]
    rows = shards[0].shape[0]
    for n, shard in enumerate(shards):
        out[n * rows : (n + 1) * rows, :] = shard[...]


def turn_kernel(*refs):
    acts, out = refs[:-1], refs[-1]
    tokens, hidden = acts[0].shape
    for k, act in enumerate(acts):
        place = (len(acts) - k) % len(acts)
        for c in range(0, hidden, BLOCK):
            out[c : c + BLOCK, place * tokens : (place + 1) * tokens] = act[:, c : c + BLOCK].T


def store_terms(total, own, outs):
    rows, tokens = own.shape
    own[...] = total[:, :tokens]
    for k, out in enumerate(outs):
        of_code = lax.broadcasted_iota(jnp.int32, (out.shape[0] - rows, tokens), 0)
        codes = jnp.zeros(of_code.shape, jnp.int32)
        for b in range(rows // BLOCK):
            at = slice(b * BLOCK, (b + 1) * BLOCK)
            whole, code = encode(total[at, (k + 1) * tokens : (k + 2) * tokens])
            out[at, :] = whole.astype(jnp.int16)
            codes = jnp.where(of_code == b, code, codes)
        out[rows:, :] = codes.astype(jnp.int16)


def fetch_kernel(first, weight, out, sems):
    fetch(weight, first, out, sems)
    fetched(weight, first, out, sems)


def kept_blocks(pieces, spread, cols):
    kept = []
    for weight, first, end, row in pieces:
        factors = spread[row : row + end - first, cols].astype(jnp.bfloat16)
        for b in range(first, end):
            block = weight[b * BLOCK : (b + 1) * BLOCK, cols]
            kept.append(block * factors[b - first : b - first + 1, :])
    return jnp.concatenate(kept, axis=0)


def first_terms_kernel(n_shards, n_parts, shift, chunk, blocks, place, table, *refs):
    shards = refs[:n_shards]
    *weights, spread, full, turned, own = refs[n_shards : -n_parts - 1]
    outs, total = refs[-n_parts - 1 : -1], refs[-1]
    pieces, done = [], 0
    for weight in weights:
        end = min(weight.shape[0] // BLOCK, blocks - done)
        pieces.append((weight, 0, end, done))
        done += end
    rows = shards[0].shape[0]
    n_cols = table.shape[0]
    slots = [(shard, at) for shard in shards for at in range(0, shard.shape[0], rows)]
    for n, (shard, at) in enumerate(slots):
        to = lax.rem(table[place[1], n] + n_cols - place[0] * shift, n_cols)
        full[pl.ds(pl.multiple_of(to * rows, rows), rows), :] = shard[at : at + rows, :]
    for c in range(0, full.shape[1], chunk):
        cols = slice(c, c + chunk)
        turned[cols, :] = full[:, cols].T
        kept = kept_blocks(pieces, spread, cols)
        terms = jnp.dot(kept, turned[cols, :], preferred_element_type=jnp.float32)
        total[...] = terms if c == 0 else total[...] + terms
    store_terms(total, own, outs)


def more_terms_kernel(n_parts, first, chunk, turned, weight, spread, *refs):
    acts, (own, *outs, acts_turned, total) = refs[: n_parts + 1], refs[n_parts + 1 :]
    end = weight.shape[0] // BLOCK
    pieces = [(weight, end - own.shape[0] // BLOCK, end, first)]
    for c in range(0, weight.shape[1], chunk):
        cols = slice(c, c + chunk)
        kept = kept_blocks(pieces, spread, cols)
        terms = jnp.dot(kept, turned[cols, :], preferred_element_type=jnp.float32)
        total[...] = terms if c == 0 else total[...] + terms
    store_terms(total, own, outs)
    turn_kernel(*acts, acts_turned)


def weight_grad_kernel(chunk, acts, full, spread, out, held, sems):
    hidden, width = out.shape
    blocks = hidden // BLOCK
    pair = 2 if blocks % 2 == 0 else 1
    copies = []
    for first in range(0, blocks, pair):
        left = acts[first * BLOCK : (first + pair) * BLOCK, :]
        for c in range(0, width, chunk):
            cols = slice(c, c + chunk)
            product = jnp.dot(left, full[:, cols], preferred_element_type=jnp.float32)
            for b in range(pair):
                part = product[b * BLOCK : (b + 1) * BLOCK, :].astype(out.dtype)
                factor = spread[first + b : first + b + 1, cols].astype(out.dtype)
                held[(first + b) * BLOCK : (first + b + 1) * BLOCK, cols] = part * factor
        for b in range(first, first + pair):
            at = pl.ds(b * BLOCK, BLOCK)
            copies.append(pltpu.make_async_copy(held.at[at, :], out.at[at, :], sems.at[b]))
            copies[-1].start()
    for copy in copies:
        copy.wait()


def finish_kernel(first, n_parts, own, *refs):
    parts, (*_, out, held, sem) = refs[:n_parts], refs[n_parts:]
    rows = own.shape[0]
    scales = []
    for part in parts:
        code = part[rows:, :].astype(jnp.int32).astype(jnp.float32)
        scales.append(jnp.exp2(code * (1.0 / STEPS)) * (1.0 / CODE))
    for b in range(rows // BLOCK):
        at = slice(b * BLOCK, (b + 1) * BLOCK)
        total = own[at, :]
        for part, scale in zip(parts, scales, strict=True):
            got = part[at, :].astype(jnp.int32).astype(jnp.float32)
            total = total + got * scale[b : b + 1, :]
        held[:, at] = total.T.astype(out.dtype)
    copy = pltpu.make_async_copy(held, out.at[:, pl.ds(first, rows)], sem)
    copy.start()
    copy.wait()


def in_vmem():
    return pl.BlockSpec(memory_space=pltpu.VMEM)


def in_smem():
    return pl.BlockSpec(memory_space=pltpu.SMEM)


def in_hbm():
    return pl.BlockSpec(memory_space=pl.ANY)


def params():
    return pltpu.CompilerParams(vmem_limit_bytes=VMEM_LIMIT)


def cost(flops, nbytes):
    return pl.CostEstimate(flops=flops, bytes_accessed=nbytes, transcendentals=0)


def per_device(n_rows, n_cols, grad_output, inputs, weight, block_mask):
    row, col = lax.axis_index("row"), lax.axis_index("col")
    hidden, width = weight.shape
    blocks = hidden // BLOCK
    n_pieces = 2 if blocks > 7 else 1
    piece = blocks * 5 // 14 * BLOCK if n_pieces > 1 else hidden
    sizes = [piece, hidden - piece][:n_pieces]
    n_parts = n_rows - 1
    tokens = inputs.shape[0]
    shard_rows = grad_output.shape[0]
    all_tokens = tokens * n_rows
    chunk = min(512, width)
    bf16 = jnp.bfloat16

    ring = chip_ring(n_cols)
    n_chips = len(ring)

    def send_ring(x, by):
        perm = []
        for p in range(n_chips):
            for core in range(2):
                q = (p + (by if core == 0 else -by)) % n_chips
                perm.append((ring[p] * 2 + core, ring[q] * 2 + core))
        return lax.ppermute(x, "col", perm)

    def send_core(x):
        return lax.ppermute(x, "col", [(c, c ^ 1) for c in range(n_cols)])

    def send_row(x, by):
        return lax.ppermute(x, "row", [(r, (r + by) % n_rows) for r in range(n_rows)])

    reach = [0]
    for j in range(1, n_chips // 2 + 1):
        reach += [j] if 2 * j == n_chips else [j, -j]
    near = [j for j in reach if abs(j) < 3]
    last = [j for j in reach if abs(j) > 2]
    steps = [(j, other) for other in range(2) for j in near]
    steps += [(j, other) for j in last for other in range(2)]
    table = []
    for c in range(n_cols):
        p, core = ring.index(c // 2), c % 2
        line = []
        for j, other in steps:
            of_core = core ^ other
            q = (p - j if of_core == 0 else p + j) % n_chips
            line.append(ring[q] * 2 + of_core)
        table.append(line)
    place = jnp.stack([row, col]).astype(jnp.int32)

    weight = pltpu.with_memory_space_constraint(weight, pltpu.HBM)
    block_mask = pltpu.with_memory_space_constraint(block_mask, pltpu.HBM)
    piece_blocks = piece // BLOCK
    spread = pl.pallas_call(
        spread_kernel,
        in_specs=[in_smem(), in_hbm()],
        out_specs=in_vmem(),
        out_shape=pltpu.VMEM((blocks, width), jnp.float32),
        scratch_shapes=[pltpu.VMEM(block_mask.shape, jnp.int32), pltpu.SemaphoreType.DMA],
        compiler_params=params(),
        cost_estimate=cost(1 << 34, BLOCK),
        name="spread",
    )(place, block_mask)

    def fetch_rows(first, count, flops):
        return pl.pallas_call(
            functools.partial(fetch_kernel, first),
            in_specs=[in_hbm()],
            out_specs=in_vmem(),
            out_shape=pltpu.VMEM((count * BLOCK, width), bf16),
            scratch_shapes=[pltpu.SemaphoreType.DMA((count,))],
            compiler_params=params(),
            cost_estimate=cost(flops, BLOCK),
            name="fetch",
        )(weight)

    held = {0: grad_output}
    for j in (2, -2):
        if abs(j) < n_chips // 2 or j == n_chips // 2:
            held[j] = send_ring(grad_output, j)
    far = [j for j in held if j]
    spread, again = lax.optimization_barrier((spread, grad_output))
    held[1], held[-1] = send_ring(again, 1), send_ring(again, -1)
    n_soon = max(1, blocks * 2 // 7)
    weight, spread = lax.optimization_barrier((weight, spread))
    soon = fetch_rows(0, n_soon, BLOCK)
    soon, *ready = lax.optimization_barrier((soon, *(held[j] for j in far)))
    held.update(zip(far, ready, strict=True))
    acts = [inputs] + [send_row(inputs, k) for k in range(1, n_rows)]
    for j in range(3, n_chips // 2 + 1):
        by = 1 if j % 2 else 2
        held[j] = send_ring(held[j - by], by)
        if 2 * j < n_chips:
            held[-j] = send_ring(held[by - j], -by)

    weight, held[1], held[-1], *acts = lax.optimization_barrier(
        (weight, held[1], held[-1], *acts)
    )
    rest = fetch_rows(n_soon, blocks - n_soon, 1 << 34)
    rest, *ready = lax.optimization_barrier((rest, *(held[j] for j in last)))
    held.update(zip(last, ready, strict=True))
    packed = pl.pallas_call(
        pack_kernel,
        in_specs=[in_vmem()] * len(near),
        out_specs=in_vmem(),
        out_shape=jax.ShapeDtypeStruct((len(near) * shard_rows, width), bf16),
        compiler_params=params(),
        name="pack",
    )(*(held[j] for j in near))
    shards = [held[j] for j in near] + [send_core(packed)]
    for j in last:
        shards += [held[j], send_core(held[j])]
    n_shards = len(shards)
    def out_shapes(rows):
        code_rows = -(-(rows // BLOCK) // 16) * 16
        sent_shape = jax.ShapeDtypeStruct((rows + code_rows, tokens), jnp.int16)
        return [jax.ShapeDtypeStruct((rows, tokens), jnp.float32)] + [sent_shape] * n_parts

    small_cost = cost(piece * width, piece * width // 8)
    full, turned, own, *coded = pl.pallas_call(
        functools.partial(
            first_terms_kernel, n_shards, n_parts, tokens // shard_rows, chunk, piece_blocks
        ),
        in_specs=[in_smem()] * 2 + [in_vmem()] * (n_shards + 3),
        out_specs=[in_vmem()] * (3 + n_parts),
        out_shape=[
            jax.ShapeDtypeStruct((all_tokens, width), bf16),
            jax.ShapeDtypeStruct((width, all_tokens), bf16),
        ]
        + out_shapes(piece),
        scratch_shapes=[pltpu.VMEM((piece, all_tokens), jnp.float32)],
        compiler_params=params(),
        cost_estimate=small_cost,
        name="first_terms",
    )(place, jnp.array(table, jnp.int32), *shards, soon, rest, spread)
    owns = [own]
    parts = [send_row(coded[k], k + 1) for k in range(n_parts)]

    acts_shape = jax.ShapeDtypeStruct((hidden, all_tokens), bf16)
    if n_pieces > 1:
        own, *coded, acts_turned = pl.pallas_call(
            functools.partial(more_terms_kernel, n_parts, piece_blocks, chunk),
            in_specs=[in_vmem()] * (3 + n_rows),
            out_specs=[in_vmem()] * (2 + n_parts),
            out_shape=out_shapes(sizes[1]) + [acts_shape],
            scratch_shapes=[pltpu.VMEM((sizes[1], all_tokens), jnp.float32)],
            compiler_params=params(),
            cost_estimate=small_cost,
            name="more_terms",
        )(turned, rest, spread, *acts)
        owns.append(own)
        parts += [send_row(coded[k], k + 1) for k in range(n_parts)]
    else:
        acts_turned = pl.pallas_call(
            turn_kernel,
            in_specs=[in_vmem()] * n_rows,
            out_specs=in_vmem(),
            out_shape=acts_shape,
            compiler_params=params(),
            name="turn",
        )(*acts)

    grad_weight = pl.pallas_call(
        functools.partial(weight_grad_kernel, chunk),
        in_specs=[in_vmem()] * 3,
        out_specs=in_hbm(),
        out_shape=jax.ShapeDtypeStruct((hidden, width), bf16),
        scratch_shapes=[
            pltpu.VMEM((hidden, width), bf16),
            pltpu.SemaphoreType.DMA((blocks,)),
        ],
        compiler_params=params(),
        cost_estimate=small_cost,
        name="weight_grad",
    )(acts_turned, full, spread)

    grad_input = None
    for p, rows in enumerate(sizes):
        operands = [owns[p], *parts[p * n_parts : (p + 1) * n_parts]]
        specs = [in_vmem()] * len(operands)
        if p:
            operands.append(grad_input)
            specs.append(in_hbm())
        grad_input = pl.pallas_call(
            functools.partial(finish_kernel, sum(sizes[:p]), n_parts),
            in_specs=specs,
            out_specs=in_hbm(),
            out_shape=jax.ShapeDtypeStruct((tokens, hidden), bf16),
            scratch_shapes=[pltpu.VMEM((tokens, rows), bf16), pltpu.SemaphoreType.DMA],
            input_output_aliases={len(operands) - 1: 0} if p else {},
            compiler_params=params(),
            cost_estimate=cost(BLOCK if p else 1 << 34, BLOCK),
            name="add_terms",
        )(*operands)
    return (grad_input, grad_weight)


def solution(mesh):
    return jax.shard_map(
        functools.partial(per_device, mesh.shape["row"], mesh.shape["col"]),
        mesh=mesh,
        in_specs=(P("col", "row"), P("row", "col"), P("col", "row"), P("col", None)),
        out_specs=(P("row", "col"), P("col", "row")),
        check_vma=False,
    )
```

```python
import functools

import jax
import jax.numpy as jnp
from jax import lax
from jax.experimental import pallas as pl
from jax.experimental.pallas import tpu as pltpu
from jax.sharding import PartitionSpec as P

BLOCK = 128
CODE = 32700.0
STEPS = 64.0
VMEM_LIMIT = 24 * 1024 * 1024


def chip_ring(cols):
    half, fast = cols // 2, 1
    while half % (fast * 2) == 0 and fast * 2 * fast * 2 <= half:
        fast *= 2
    slow = half // fast
    ring = []
    for s in range(slow):
        along = range(1, fast) if s % 2 == 0 else range(fast - 1, 0, -1)
        ring += [s * fast + f for f in along]
    ring += [s * fast for s in range(slow - 1, -1, -1)]
    return ring


def encode(part):
    top = jnp.max(jnp.abs(part), axis=0, keepdims=True)
    code = jnp.ceil(STEPS * jnp.log2(jnp.maximum(top, 1e-30)))
    scaled = part * (jnp.exp2(code * (-1.0 / STEPS)) * CODE)
    whole = jnp.clip(jnp.round(scaled), -32767.0, 32767.0)
    return whole.astype(jnp.int32), code.astype(jnp.int32)


def wide_mask(mask, first, width):
    cols = mask.shape[1]
    of_column = first + lax.broadcasted_iota(jnp.int32, (cols, width), 1) // BLOCK
    spread = of_column == lax.broadcasted_iota(jnp.int32, (cols, width), 0)
    return jnp.dot(
        mask.astype(jnp.float32).astype(jnp.bfloat16),
        spread.astype(jnp.float32).astype(jnp.bfloat16),
        preferred_element_type=jnp.float32,
    )


def spread_kernel(place, mask, spread, mask_here, mask_sem):
    copy = pltpu.make_async_copy(mask, mask_here, mask_sem)
    copy.start()
    copy.wait()
    width = spread.shape[1]
    spread[...] = wide_mask(mask_here[...], place[0] * (width // BLOCK), width)


def row_copy(weight, first, here, sems, block):
    to = pl.multiple_of(block * BLOCK, BLOCK)
    at = pl.multiple_of((first + block) * BLOCK, BLOCK)
    return pltpu.make_async_copy(
        weight.at[pl.ds(at, BLOCK), :], here.at[pl.ds(to, BLOCK), :], sems.at[block]
    )


def fetch(weight, first, here, sems):
    blocks = here.shape[0] // BLOCK
    lax.fori_loop(0, blocks, lambda b, _: (row_copy(weight, first, here, sems, b).start(), 0)[1], 0)


def fetched(weight, first, here, sems):
    blocks = here.shape[0] // BLOCK
    lax.fori_loop(0, blocks, lambda b, _: (row_copy(weight, first, here, sems, b).wait(), 0)[1], 0)


def pack_kernel(*refs):
    shards, out = refs[:-1], refs[-1]
    rows = shards[0].shape[0]
    for n, shard in enumerate(shards):
        out[n * rows : (n + 1) * rows, :] = shard[...]


def turn_kernel(*refs):
    acts, out = refs[:-1], refs[-1]
    tokens, hidden = acts[0].shape
    for k, act in enumerate(acts):
        place = (len(acts) - k) % len(acts)
        for c in range(0, hidden, BLOCK):
            out[c : c + BLOCK, place * tokens : (place + 1) * tokens] = act[:, c : c + BLOCK].T


def store_terms(total, own, outs):
    rows, tokens = own.shape
    own[...] = total[:, :tokens]
    for k, out in enumerate(outs):
        of_code = lax.broadcasted_iota(jnp.int32, (out.shape[0] - rows, tokens), 0)
        codes = jnp.zeros(of_code.shape, jnp.int32)
        for b in range(rows // BLOCK):
            at = slice(b * BLOCK, (b + 1) * BLOCK)
            whole, code = encode(total[at, (k + 1) * tokens : (k + 2) * tokens])
            out[at, :] = whole.astype(jnp.int16)
            codes = jnp.where(of_code == b, code, codes)
        out[rows:, :] = codes.astype(jnp.int16)


def fetch_kernel(first, weight, out, sems):
    fetch(weight, first, out, sems)
    fetched(weight, first, out, sems)


def kept_blocks(pieces, spread, cols):
    kept = []
    for weight, first, end, row in pieces:
        factors = spread[row : row + end - first, cols].astype(jnp.bfloat16)
        for b in range(first, end):
            block = weight[b * BLOCK : (b + 1) * BLOCK, cols]
            kept.append(block * factors[b - first : b - first + 1, :])
    return jnp.concatenate(kept, axis=0)


def first_terms_kernel(n_shards, n_parts, shift, chunk, blocks, place, table, *refs):
    shards = refs[:n_shards]
    *weights, spread, full, turned, own = refs[n_shards : -n_parts - 1]
    outs, total = refs[-n_parts - 1 : -1], refs[-1]
    pieces, done = [], 0
    for weight in weights:
        end = min(weight.shape[0] // BLOCK, blocks - done)
        pieces.append((weight, 0, end, done))
        done += end
    rows = shards[0].shape[0]
    n_cols = table.shape[0]
    slots = [(shard, at) for shard in shards for at in range(0, shard.shape[0], rows)]
    for n, (shard, at) in enumerate(slots):
        to = lax.rem(table[place[1], n] + n_cols - place[0] * shift, n_cols)
        full[pl.ds(pl.multiple_of(to * rows, rows), rows), :] = shard[at : at + rows, :]
    for c in range(0, full.shape[1], chunk):
        cols = slice(c, c + chunk)
        turned[cols, :] = full[:, cols].T
        kept = kept_blocks(pieces, spread, cols)
        terms = jnp.dot(kept, turned[cols, :], preferred_element_type=jnp.float32)
        total[...] = terms if c == 0 else total[...] + terms
    store_terms(total, own, outs)


def more_terms_kernel(n_parts, first, chunk, turned, weight, spread, *refs):
    acts, (own, *outs, acts_turned, total) = refs[: n_parts + 1], refs[n_parts + 1 :]
    end = weight.shape[0] // BLOCK
    pieces = [(weight, end - own.shape[0] // BLOCK, end, first)]
    for c in range(0, weight.shape[1], chunk):
        cols = slice(c, c + chunk)
        kept = kept_blocks(pieces, spread, cols)
        terms = jnp.dot(kept, turned[cols, :], preferred_element_type=jnp.float32)
        total[...] = terms if c == 0 else total[...] + terms
    store_terms(total, own, outs)
    turn_kernel(*acts, acts_turned)


def weight_grad_kernel(chunk, acts, full, spread, out, held, sems):
    hidden, width = out.shape
    blocks = hidden // BLOCK
    pair = 2 if blocks % 2 == 0 else 1
    copies = []
    for first in range(0, blocks, pair):
        left = acts[first * BLOCK : (first + pair) * BLOCK, :]
        for c in range(0, width, chunk):
            cols = slice(c, c + chunk)
            product = jnp.dot(left, full[:, cols], preferred_element_type=jnp.float32)
            for b in range(pair):
                part = product[b * BLOCK : (b + 1) * BLOCK, :].astype(out.dtype)
                factor = spread[first + b : first + b + 1, cols].astype(out.dtype)
                held[(first + b) * BLOCK : (first + b + 1) * BLOCK, cols] = part * factor
        for b in range(first, first + pair):
            at = pl.ds(b * BLOCK, BLOCK)
            copies.append(pltpu.make_async_copy(held.at[at, :], out.at[at, :], sems.at[b]))
            copies[-1].start()
    for copy in copies:
        copy.wait()


def finish_kernel(first, n_parts, own, *refs):
    parts, (*_, out, held, sem) = refs[:n_parts], refs[n_parts:]
    rows = own.shape[0]
    scales = []
    for part in parts:
        code = part[rows:, :].astype(jnp.int32).astype(jnp.float32)
        scales.append(jnp.exp2(code * (1.0 / STEPS)) * (1.0 / CODE))
    for b in range(rows // BLOCK):
        at = slice(b * BLOCK, (b + 1) * BLOCK)
        total = own[at, :]
        for part, scale in zip(parts, scales, strict=True):
            got = part[at, :].astype(jnp.int32).astype(jnp.float32)
            total = total + got * scale[b : b + 1, :]
        held[:, at] = total.T.astype(out.dtype)
    copy = pltpu.make_async_copy(held, out.at[:, pl.ds(first, rows)], sem)
    copy.start()
    copy.wait()


def in_vmem():
    return pl.BlockSpec(memory_space=pltpu.VMEM)


def in_smem():
    return pl.BlockSpec(memory_space=pltpu.SMEM)


def in_hbm():
    return pl.BlockSpec(memory_space=pl.ANY)


def params():
    return pltpu.CompilerParams(vmem_limit_bytes=VMEM_LIMIT)


def cost(flops, nbytes):
    return pl.CostEstimate(flops=flops, bytes_accessed=nbytes, transcendentals=0)


def per_device(n_rows, n_cols, grad_output, inputs, weight, block_mask):
    row, col = lax.axis_index("row"), lax.axis_index("col")
    hidden, width = weight.shape
    blocks = hidden // BLOCK
    n_pieces = 2 if blocks > 7 else 1
    piece = blocks * 5 // 14 * BLOCK if n_pieces > 1 else hidden
    sizes = [piece, hidden - piece][:n_pieces]
    n_parts = n_rows - 1
    tokens = inputs.shape[0]
    shard_rows = grad_output.shape[0]
    all_tokens = tokens * n_rows
    chunk = min(512, width)
    bf16 = jnp.bfloat16

    ring = chip_ring(n_cols)
    n_chips = len(ring)

    def send_ring(x, by):
        perm = []
        for p in range(n_chips):
            for core in range(2):
                q = (p + (by if core == 0 else -by)) % n_chips
                perm.append((ring[p] * 2 + core, ring[q] * 2 + core))
        return lax.ppermute(x, "col", perm)

    def send_core(x):
        return lax.ppermute(x, "col", [(c, c ^ 1) for c in range(n_cols)])

    def send_row(x, by):
        return lax.ppermute(x, "row", [(r, (r + by) % n_rows) for r in range(n_rows)])

    reach = [0]
    for j in range(1, n_chips // 2 + 1):
        reach += [j] if 2 * j == n_chips else [j, -j]
    near = [j for j in reach if abs(j) < 3]
    last = [j for j in reach if abs(j) > 2]
    steps = [(j, other) for other in range(2) for j in near]
    steps += [(j, other) for j in last for other in range(2)]
    table = []
    for c in range(n_cols):
        p, core = ring.index(c // 2), c % 2
        line = []
        for j, other in steps:
            of_core = core ^ other
            q = (p - j if of_core == 0 else p + j) % n_chips
            line.append(ring[q] * 2 + of_core)
        table.append(line)
    place = jnp.stack([row, col]).astype(jnp.int32)

    weight = pltpu.with_memory_space_constraint(weight, pltpu.HBM)
    block_mask = pltpu.with_memory_space_constraint(block_mask, pltpu.HBM)
    piece_blocks = piece // BLOCK
    spread = pl.pallas_call(
        spread_kernel,
        in_specs=[in_smem(), in_hbm()],
        out_specs=in_vmem(),
        out_shape=pltpu.VMEM((blocks, width), jnp.float32),
        scratch_shapes=[pltpu.VMEM(block_mask.shape, jnp.int32), pltpu.SemaphoreType.DMA],
        compiler_params=params(),
        cost_estimate=cost(1 << 34, BLOCK),
        name="spread",
    )(place, block_mask)

    def fetch_rows(first, count, flops):
        return pl.pallas_call(
            functools.partial(fetch_kernel, first),
            in_specs=[in_hbm()],
            out_specs=in_vmem(),
            out_shape=pltpu.VMEM((count * BLOCK, width), bf16),
            scratch_shapes=[pltpu.SemaphoreType.DMA((count,))],
            compiler_params=params(),
            cost_estimate=cost(flops, BLOCK),
            name="fetch",
        )(weight)

    held = {0: grad_output}
    for j in (2, -2):
        if abs(j) < n_chips // 2 or j == n_chips // 2:
            held[j] = send_ring(grad_output, j)
    far = [j for j in held if j]
    spread, again = lax.optimization_barrier((spread, grad_output))
    held[1], held[-1] = send_ring(again, 1), send_ring(again, -1)
    n_soon = max(1, blocks * 2 // 7)
    weight, spread = lax.optimization_barrier((weight, spread))
    soon = fetch_rows(0, n_soon, BLOCK)
    soon, *ready = lax.optimization_barrier((soon, *(held[j] for j in far)))
    held.update(zip(far, ready, strict=True))
    acts = [inputs] + [send_row(inputs, k) for k in range(1, n_rows)]
    for j in range(3, n_chips // 2 + 1):
        by = 1 if j % 2 else 2
        held[j] = send_ring(held[j - by], by)
        if 2 * j < n_chips:
            held[-j] = send_ring(held[by - j], -by)

    weight, held[1], held[-1], *acts = lax.optimization_barrier(
        (weight, held[1], held[-1], *acts)
    )
    rest = fetch_rows(n_soon, blocks - n_soon, 1 << 34)
    order = sorted(last, reverse=True)
    rest, *ready = lax.optimization_barrier((rest, *(held[j] for j in order)))
    held.update(zip(order, ready, strict=True))
    packed = pl.pallas_call(
        pack_kernel,
        in_specs=[in_vmem()] * len(near),
        out_specs=in_vmem(),
        out_shape=jax.ShapeDtypeStruct((len(near) * shard_rows, width), bf16),
        compiler_params=params(),
        name="pack",
    )(*(held[j] for j in near))
    shards = [held[j] for j in near] + [send_core(packed)]
    for j in last:
        shards += [held[j], send_core(held[j])]
    n_shards = len(shards)
    def out_shapes(rows):
        code_rows = -(-(rows // BLOCK) // 16) * 16
        sent_shape = jax.ShapeDtypeStruct((rows + code_rows, tokens), jnp.int16)
        return [jax.ShapeDtypeStruct((rows, tokens), jnp.float32)] + [sent_shape] * n_parts

    small_cost = cost(piece * width, piece * width // 8)
    full, turned, own, *coded = pl.pallas_call(
        functools.partial(
            first_terms_kernel, n_shards, n_parts, tokens // shard_rows, chunk, piece_blocks
        ),
        in_specs=[in_smem()] * 2 + [in_vmem()] * (n_shards + 3),
        out_specs=[in_vmem()] * (3 + n_parts),
        out_shape=[
            jax.ShapeDtypeStruct((all_tokens, width), bf16),
            jax.ShapeDtypeStruct((width, all_tokens), bf16),
        ]
        + out_shapes(piece),
        scratch_shapes=[pltpu.VMEM((piece, all_tokens), jnp.float32)],
        compiler_params=params(),
        cost_estimate=small_cost,
        name="first_terms",
    )(place, jnp.array(table, jnp.int32), *shards, soon, rest, spread)
    owns = [own]
    parts = [send_row(coded[k], k + 1) for k in range(n_parts)]

    acts_shape = jax.ShapeDtypeStruct((hidden, all_tokens), bf16)
    if n_pieces > 1:
        own, *coded, acts_turned = pl.pallas_call(
            functools.partial(more_terms_kernel, n_parts, piece_blocks, chunk),
            in_specs=[in_vmem()] * (3 + n_rows),
            out_specs=[in_vmem()] * (2 + n_parts),
            out_shape=out_shapes(sizes[1]) + [acts_shape],
            scratch_shapes=[pltpu.VMEM((sizes[1], all_tokens), jnp.float32)],
            compiler_params=params(),
            cost_estimate=small_cost,
            name="more_terms",
        )(turned, rest, spread, *acts)
        owns.append(own)
        parts += [send_row(coded[k], k + 1) for k in range(n_parts)]
    else:
        acts_turned = pl.pallas_call(
            turn_kernel,
            in_specs=[in_vmem()] * n_rows,
            out_specs=in_vmem(),
            out_shape=acts_shape,
            compiler_params=params(),
            name="turn",
        )(*acts)

    grad_weight = pl.pallas_call(
        functools.partial(weight_grad_kernel, chunk),
        in_specs=[in_vmem()] * 3,
        out_specs=in_hbm(),
        out_shape=jax.ShapeDtypeStruct((hidden, width), bf16),
        scratch_shapes=[
            pltpu.VMEM((hidden, width), bf16),
            pltpu.SemaphoreType.DMA((blocks,)),
        ],
        compiler_params=params(),
        cost_estimate=small_cost,
        name="weight_grad",
    )(acts_turned, full, spread)

    grad_input = None
    for p, rows in enumerate(sizes):
        operands = [owns[p], *parts[p * n_parts : (p + 1) * n_parts]]
        specs = [in_vmem()] * len(operands)
        if p:
            operands.append(grad_input)
            specs.append(in_hbm())
        grad_input = pl.pallas_call(
            functools.partial(finish_kernel, sum(sizes[:p]), n_parts),
            in_specs=specs,
            out_specs=in_hbm(),
            out_shape=jax.ShapeDtypeStruct((tokens, hidden), bf16),
            scratch_shapes=[pltpu.VMEM((tokens, rows), bf16), pltpu.SemaphoreType.DMA],
            input_output_aliases={len(operands) - 1: 0} if p else {},
            compiler_params=params(),
            cost_estimate=cost(BLOCK if p else 1 << 34, BLOCK),
            name="add_terms",
        )(*operands)
    return (grad_input, grad_weight)


def solution(mesh):
    return jax.shard_map(
        functools.partial(per_device, mesh.shape["row"], mesh.shape["col"]),
        mesh=mesh,
        in_specs=(P("col", "row"), P("row", "col"), P("col", "row"), P("col", None)),
        out_specs=(P("row", "col"), P("col", "row")),
        check_vma=False,
    )
```

```python
import functools

import jax
import jax.numpy as jnp
from jax import lax
from jax.experimental import pallas as pl
from jax.experimental.pallas import tpu as pltpu
from jax.sharding import PartitionSpec as P

BLOCK = 128
CODE = 32700.0
STEPS = 64.0
VMEM_LIMIT = 24 * 1024 * 1024


def chip_ring(cols):
    half, fast = cols // 2, 1
    while half % (fast * 2) == 0 and fast * 2 * fast * 2 <= half:
        fast *= 2
    slow = half // fast
    ring = []
    for s in range(slow):
        along = range(1, fast) if s % 2 == 0 else range(fast - 1, 0, -1)
        ring += [s * fast + f for f in along]
    ring += [s * fast for s in range(slow - 1, -1, -1)]
    return ring


def encode(part):
    top = jnp.max(jnp.abs(part), axis=0, keepdims=True)
    code = jnp.ceil(STEPS * jnp.log2(jnp.maximum(top, 1e-30)))
    scaled = part * (jnp.exp2(code * (-1.0 / STEPS)) * CODE)
    whole = jnp.clip(jnp.round(scaled), -32767.0, 32767.0)
    return whole.astype(jnp.int32), code.astype(jnp.int32)


def wide_mask(mask, first, width):
    cols = mask.shape[1]
    of_column = first + lax.broadcasted_iota(jnp.int32, (cols, width), 1) // BLOCK
    spread = of_column == lax.broadcasted_iota(jnp.int32, (cols, width), 0)
    return jnp.dot(
        mask.astype(jnp.float32).astype(jnp.bfloat16),
        spread.astype(jnp.float32).astype(jnp.bfloat16),
        preferred_element_type=jnp.float32,
    )


def spread_kernel(place, mask, spread, mask_here, mask_sem):
    copy = pltpu.make_async_copy(mask, mask_here, mask_sem)
    copy.start()
    copy.wait()
    width = spread.shape[1]
    spread[...] = wide_mask(mask_here[...], place[0] * (width // BLOCK), width)


def row_copy(weight, first, here, sems, block):
    to = pl.multiple_of(block * BLOCK, BLOCK)
    at = pl.multiple_of((first + block) * BLOCK, BLOCK)
    return pltpu.make_async_copy(
        weight.at[pl.ds(at, BLOCK), :], here.at[pl.ds(to, BLOCK), :], sems.at[block]
    )


def fetch(weight, first, here, sems):
    blocks = here.shape[0] // BLOCK
    lax.fori_loop(0, blocks, lambda b, _: (row_copy(weight, first, here, sems, b).start(), 0)[1], 0)


def fetched(weight, first, here, sems):
    blocks = here.shape[0] // BLOCK
    lax.fori_loop(0, blocks, lambda b, _: (row_copy(weight, first, here, sems, b).wait(), 0)[1], 0)


def pack_kernel(*refs):
    shards, out = refs[:-1], refs[-1]
    rows = shards[0].shape[0]
    for n, shard in enumerate(shards):
        out[n * rows : (n + 1) * rows, :] = shard[...]


def turn_kernel(*refs):
    acts, out = refs[:-1], refs[-1]
    tokens, hidden = acts[0].shape
    for k, act in enumerate(acts):
        place = (len(acts) - k) % len(acts)
        for c in range(0, hidden, BLOCK):
            out[c : c + BLOCK, place * tokens : (place + 1) * tokens] = act[:, c : c + BLOCK].T


def store_terms(total, own, outs):
    rows, tokens = own.shape
    own[...] = total[:, :tokens]
    for k, out in enumerate(outs):
        of_code = lax.broadcasted_iota(jnp.int32, (out.shape[0] - rows, tokens), 0)
        codes = jnp.zeros(of_code.shape, jnp.int32)
        for b in range(rows // BLOCK):
            at = slice(b * BLOCK, (b + 1) * BLOCK)
            whole, code = encode(total[at, (k + 1) * tokens : (k + 2) * tokens])
            out[at, :] = whole.astype(jnp.int16)
            codes = jnp.where(of_code == b, code, codes)
        out[rows:, :] = codes.astype(jnp.int16)


def fetch_kernel(first, weight, out, sems):
    fetch(weight, first, out, sems)
    fetched(weight, first, out, sems)


def kept_blocks(pieces, spread, cols):
    kept = []
    for weight, first, end, row in pieces:
        factors = spread[row : row + end - first, cols].astype(jnp.bfloat16)
        for b in range(first, end):
            block = weight[b * BLOCK : (b + 1) * BLOCK, cols]
            kept.append(block * factors[b - first : b - first + 1, :])
    return jnp.concatenate(kept, axis=0)


def first_terms_kernel(n_shards, n_parts, shift, chunk, blocks, place, table, *refs):
    shards = refs[:n_shards]
    *weights, spread, full, turned, own = refs[n_shards : -n_parts - 1]
    outs, total = refs[-n_parts - 1 : -1], refs[-1]
    pieces, done = [], 0
    for weight in weights:
        end = min(weight.shape[0] // BLOCK, blocks - done)
        pieces.append((weight, 0, end, done))
        done += end
    rows = shards[0].shape[0]
    n_cols = table.shape[0]
    slots = [(shard, at) for shard in shards for at in range(0, shard.shape[0], rows)]
    for n, (shard, at) in enumerate(slots):
        to = lax.rem(table[place[1], n] + n_cols - place[0] * shift, n_cols)
        full[pl.ds(pl.multiple_of(to * rows, rows), rows), :] = shard[at : at + rows, :]
    for c in range(0, full.shape[1], chunk):
        cols = slice(c, c + chunk)
        turned[cols, :] = full[:, cols].T
        kept = kept_blocks(pieces, spread, cols)
        terms = jnp.dot(kept, turned[cols, :], preferred_element_type=jnp.float32)
        total[...] = terms if c == 0 else total[...] + terms
    store_terms(total, own, outs)


def more_terms_kernel(n_parts, first, chunk, turned, weight, spread, *refs):
    acts, (own, *outs, acts_turned, total) = refs[: n_parts + 1], refs[n_parts + 1 :]
    end = weight.shape[0] // BLOCK
    pieces = [(weight, end - own.shape[0] // BLOCK, end, first)]
    for c in range(0, weight.shape[1], chunk):
        cols = slice(c, c + chunk)
        kept = kept_blocks(pieces, spread, cols)
        terms = jnp.dot(kept, turned[cols, :], preferred_element_type=jnp.float32)
        total[...] = terms if c == 0 else total[...] + terms
    store_terms(total, own, outs)
    turn_kernel(*acts, acts_turned)


def weight_grad_kernel(chunk, acts, full, spread, out, held, sems):
    hidden, width = out.shape
    blocks = hidden // BLOCK
    pair = 2 if blocks % 2 == 0 else 1
    copies = []
    for first in range(0, blocks, pair):
        left = acts[first * BLOCK : (first + pair) * BLOCK, :]
        for c in range(0, width, chunk):
            cols = slice(c, c + chunk)
            product = jnp.dot(left, full[:, cols], preferred_element_type=jnp.float32)
            for b in range(pair):
                part = product[b * BLOCK : (b + 1) * BLOCK, :].astype(out.dtype)
                factor = spread[first + b : first + b + 1, cols].astype(out.dtype)
                held[(first + b) * BLOCK : (first + b + 1) * BLOCK, cols] = part * factor
        for b in range(first, first + pair):
            at = pl.ds(b * BLOCK, BLOCK)
            copies.append(pltpu.make_async_copy(held.at[at, :], out.at[at, :], sems.at[b]))
            copies[-1].start()
    for copy in copies:
        copy.wait()


def finish_kernel(first, n_parts, own, *refs):
    parts, (*_, out, held, sem) = refs[:n_parts], refs[n_parts:]
    rows = own.shape[0]
    scales = []
    for part in parts:
        code = part[rows:, :].astype(jnp.int32).astype(jnp.float32)
        scales.append(jnp.exp2(code * (1.0 / STEPS)) * (1.0 / CODE))
    for b in range(rows // BLOCK):
        at = slice(b * BLOCK, (b + 1) * BLOCK)
        total = own[at, :]
        for part, scale in zip(parts, scales, strict=True):
            got = part[at, :].astype(jnp.int32).astype(jnp.float32)
            total = total + got * scale[b : b + 1, :]
        held[:, at] = total.T.astype(out.dtype)
    copy = pltpu.make_async_copy(held, out.at[:, pl.ds(first, rows)], sem)
    copy.start()
    copy.wait()


def in_vmem():
    return pl.BlockSpec(memory_space=pltpu.VMEM)


def in_smem():
    return pl.BlockSpec(memory_space=pltpu.SMEM)


def in_hbm():
    return pl.BlockSpec(memory_space=pl.ANY)


def params():
    return pltpu.CompilerParams(vmem_limit_bytes=VMEM_LIMIT)


def cost(flops, nbytes):
    return pl.CostEstimate(flops=flops, bytes_accessed=nbytes, transcendentals=0)


def per_device(n_rows, n_cols, grad_output, inputs, weight, block_mask):
    row, col = lax.axis_index("row"), lax.axis_index("col")
    hidden, width = weight.shape
    blocks = hidden // BLOCK
    n_pieces = 2 if blocks > 7 else 1
    piece = blocks * 5 // 14 * BLOCK if n_pieces > 1 else hidden
    sizes = [piece, hidden - piece][:n_pieces]
    n_parts = n_rows - 1
    tokens = inputs.shape[0]
    shard_rows = grad_output.shape[0]
    all_tokens = tokens * n_rows
    chunk = min(512, width)
    bf16 = jnp.bfloat16

    ring = chip_ring(n_cols)
    n_chips = len(ring)

    def send_ring(x, by):
        perm = []
        for p in range(n_chips):
            for core in range(2):
                q = (p + (by if core == 0 else -by)) % n_chips
                perm.append((ring[p] * 2 + core, ring[q] * 2 + core))
        return lax.ppermute(x, "col", perm)

    def send_core(x):
        return lax.ppermute(x, "col", [(c, c ^ 1) for c in range(n_cols)])

    def send_row(x, by):
        return lax.ppermute(x, "row", [(r, (r + by) % n_rows) for r in range(n_rows)])

    reach = [0]
    for j in range(1, n_chips // 2 + 1):
        reach += [j] if 2 * j == n_chips else [j, -j]
    near = [j for j in reach if abs(j) < 3]
    last = [j for j in reach if abs(j) > 2]
    steps = [(j, other) for other in range(2) for j in near]
    steps += [(j, other) for j in last for other in range(2)]
    table = []
    for c in range(n_cols):
        p, core = ring.index(c // 2), c % 2
        line = []
        for j, other in steps:
            of_core = core ^ other
            q = (p - j if of_core == 0 else p + j) % n_chips
            line.append(ring[q] * 2 + of_core)
        table.append(line)
    place = jnp.stack([row, col]).astype(jnp.int32)

    weight = pltpu.with_memory_space_constraint(weight, pltpu.HBM)
    block_mask = pltpu.with_memory_space_constraint(block_mask, pltpu.HBM)
    piece_blocks = piece // BLOCK
    spread = pl.pallas_call(
        spread_kernel,
        in_specs=[in_smem(), in_hbm()],
        out_specs=in_vmem(),
        out_shape=pltpu.VMEM((blocks, width), jnp.float32),
        scratch_shapes=[pltpu.VMEM(block_mask.shape, jnp.int32), pltpu.SemaphoreType.DMA],
        compiler_params=params(),
        cost_estimate=cost(1 << 34, BLOCK),
        name="spread",
    )(place, block_mask)

    def fetch_rows(first, count, flops):
        return pl.pallas_call(
            functools.partial(fetch_kernel, first),
            in_specs=[in_hbm()],
            out_specs=in_vmem(),
            out_shape=pltpu.VMEM((count * BLOCK, width), bf16),
            scratch_shapes=[pltpu.SemaphoreType.DMA((count,))],
            compiler_params=params(),
            cost_estimate=cost(flops, BLOCK),
            name="fetch",
        )(weight)

    held = {0: grad_output}
    for j in (2, -2):
        if abs(j) < n_chips // 2 or j == n_chips // 2:
            held[j] = send_ring(grad_output, j)
    far = [j for j in held if j]
    spread, again = lax.optimization_barrier((spread, grad_output))
    held[1], held[-1] = send_ring(again, 1), send_ring(again, -1)
    n_soon = max(1, blocks * 2 // 7)
    weight, spread = lax.optimization_barrier((weight, spread))
    soon = fetch_rows(0, n_soon, BLOCK)
    soon, *ready = lax.optimization_barrier((soon, *(held[j] for j in far)))
    held.update(zip(far, ready, strict=True))
    acts = [inputs] + [send_row(inputs, k) for k in range(1, n_rows)]
    for j in range(3, n_chips // 2 + 1):
        by = 1 if j % 2 else 2
        held[j] = send_ring(held[j - by], by)
        if 2 * j < n_chips:
            held[-j] = send_ring(held[by - j], -by)

    weight, held[1], held[-1], *acts = lax.optimization_barrier(
        (weight, held[1], held[-1], *acts)
    )
    rest = fetch_rows(n_soon, blocks - n_soon, 1 << 34)
    across, late = {}, [j for j in last if j != 3]
    rest, *ready = lax.optimization_barrier((rest, *(held[j] for j in late)))
    held.update(zip(late, ready, strict=True))
    for j in late:
        across[j] = send_core(held[j])
    if 3 in last:
        held[3], *ready = lax.optimization_barrier((held[3], *(across[j] for j in late)))
        across = dict(zip(late, ready, strict=True))
    packed = pl.pallas_call(
        pack_kernel,
        in_specs=[in_vmem()] * len(near),
        out_specs=in_vmem(),
        out_shape=jax.ShapeDtypeStruct((len(near) * shard_rows, width), bf16),
        compiler_params=params(),
        name="pack",
    )(*(held[j] for j in near))
    shards = [held[j] for j in near] + [send_core(packed)]
    for j in last:
        shards += [held[j], across[j] if j in across else send_core(held[j])]
    n_shards = len(shards)
    def out_shapes(rows):
        code_rows = -(-(rows // BLOCK) // 16) * 16
        sent_shape = jax.ShapeDtypeStruct((rows + code_rows, tokens), jnp.int16)
        return [jax.ShapeDtypeStruct((rows, tokens), jnp.float32)] + [sent_shape] * n_parts

    small_cost = cost(piece * width, piece * width // 8)
    full, turned, own, *coded = pl.pallas_call(
        functools.partial(
            first_terms_kernel, n_shards, n_parts, tokens // shard_rows, chunk, piece_blocks
        ),
        in_specs=[in_smem()] * 2 + [in_vmem()] * (n_shards + 3),
        out_specs=[in_vmem()] * (3 + n_parts),
        out_shape=[
            jax.ShapeDtypeStruct((all_tokens, width), bf16),
            jax.ShapeDtypeStruct((width, all_tokens), bf16),
        ]
        + out_shapes(piece),
        scratch_shapes=[pltpu.VMEM((piece, all_tokens), jnp.float32)],
        compiler_params=params(),
        cost_estimate=small_cost,
        name="first_terms",
    )(place, jnp.array(table, jnp.int32), *shards, soon, rest, spread)
    owns = [own]
    parts = [send_row(coded[k], k + 1) for k in range(n_parts)]

    acts_shape = jax.ShapeDtypeStruct((hidden, all_tokens), bf16)
    if n_pieces > 1:
        own, *coded, acts_turned = pl.pallas_call(
            functools.partial(more_terms_kernel, n_parts, piece_blocks, chunk),
            in_specs=[in_vmem()] * (3 + n_rows),
            out_specs=[in_vmem()] * (2 + n_parts),
            out_shape=out_shapes(sizes[1]) + [acts_shape],
            scratch_shapes=[pltpu.VMEM((sizes[1], all_tokens), jnp.float32)],
            compiler_params=params(),
            cost_estimate=small_cost,
            name="more_terms",
        )(turned, rest, spread, *acts)
        owns.append(own)
        parts += [send_row(coded[k], k + 1) for k in range(n_parts)]
    else:
        acts_turned = pl.pallas_call(
            turn_kernel,
            in_specs=[in_vmem()] * n_rows,
            out_specs=in_vmem(),
            out_shape=acts_shape,
            compiler_params=params(),
            name="turn",
        )(*acts)

    grad_weight = pl.pallas_call(
        functools.partial(weight_grad_kernel, chunk),
        in_specs=[in_vmem()] * 3,
        out_specs=in_hbm(),
        out_shape=jax.ShapeDtypeStruct((hidden, width), bf16),
        scratch_shapes=[
            pltpu.VMEM((hidden, width), bf16),
            pltpu.SemaphoreType.DMA((blocks,)),
        ],
        compiler_params=params(),
        cost_estimate=small_cost,
        name="weight_grad",
    )(acts_turned, full, spread)

    grad_input = None
    for p, rows in enumerate(sizes):
        operands = [owns[p], *parts[p * n_parts : (p + 1) * n_parts]]
        specs = [in_vmem()] * len(operands)
        if p:
            operands.append(grad_input)
            specs.append(in_hbm())
        grad_input = pl.pallas_call(
            functools.partial(finish_kernel, sum(sizes[:p]), n_parts),
            in_specs=specs,
            out_specs=in_hbm(),
            out_shape=jax.ShapeDtypeStruct((tokens, hidden), bf16),
            scratch_shapes=[pltpu.VMEM((tokens, rows), bf16), pltpu.SemaphoreType.DMA],
            input_output_aliases={len(operands) - 1: 0} if p else {},
            compiler_params=params(),
            cost_estimate=cost(BLOCK if p else 1 << 34, BLOCK),
            name="add_terms",
        )(*operands)
    return (grad_input, grad_weight)


def solution(mesh):
    return jax.shard_map(
        functools.partial(per_device, mesh.shape["row"], mesh.shape["col"]),
        mesh=mesh,
        in_specs=(P("col", "row"), P("row", "col"), P("col", "row"), P("col", None)),
        out_specs=(P("row", "col"), P("col", "row")),
        check_vma=False,
    )
```
